32 devices in a mesh: groups: 2 (over y), ops: 16 (over z, x, core).
Axes of the slice: x: 2, y: 2, z: 4, core: 2. Of those that a mesh axis runs over, the one named last changes fastest.
Arguments:
- psi: bfloat16 [32, 128, 128], P(('groups', 'ops')), parts along dimension 0, may hold values from -6 to 6
- left_ops: bfloat16 [512, 128, 128], P(('groups', 'ops')), parts along dimension 0, may hold values from -0.5 to 0.5
- right_ops: bfloat16 [512, 128, 128], P(('groups', 'ops')), parts along dimension 0, may hold values from -0.125 to 0.125
- couplings: int32 [3, 12288], P(None, ('groups', 'ops')), parts along dimension 1, may hold values from 0 to 15, as said below
- live: int32 [32], P(('groups', 'ops')), parts along dimension 0, may hold values from 48 to 384, as said below
Outputs:
- sigma: float32 [32, 128, 128], P(('groups', 'ops')), parts along dimension 0
The draws below stay inside these ranges and needn't reach their ends.
There are 2 independent parts, one for each index of `groups`. The reference program is written for one: setup_inputs(seed, part) draws one part's arguments, and reference() takes and returns one part's arrays. A program takes and returns all parts, laid end to end along the dimension named above; each array names one. Nothing has to cross between parts.
Inputs may be any that keep to these rules, and one draw needn't show every extreme that they name: `couplings`: row 0 lies in 0 to 15, rows 1 and 2 in 0 to 15. Some list has all 384 slots live, and some list only 48.
All inputs are finite; a program needn't handle non-finite values.
Results may differ from the reference program's by a relative error of at most 0.0029.
Values may be sent and summed in bfloat16 or wider, within the bound.
No kernel may reach another device: no remote copies, remote signals or barrier semaphores. Data moves between devices by JAX's collectives and lax.ppermute only.
A program may use at most 128 MiB of HBM per device.

```python
import jax
import jax.numpy as jnp
from jax import lax

M = 128
OPS_DEV = 16
C_DEV = 384
NSEC = 16
NOPS = 256
NLIST = 16
NCOUP = 6144


def draw_couplings(key, part):
    key = jax.random.fold_in(key, 11)
    key_block, key_source, key_target = jax.random.split(key, 3)
    block_row = jax.random.randint(key_block, (1, NCOUP), 0, OPS_DEV)
    source_row = jax.random.randint(key_source, (1, NCOUP), 0, NSEC)
    target_row = jax.random.randint(key_target, (1, NCOUP), 0, NSEC)
    return jnp.concatenate([block_row, source_row, target_row], axis=0).astype(jnp.int32)


def draw_live(key, part):
    key = jax.random.fold_in(key, 23)
    key_count, key_place, key_step = jax.random.split(key, 3)
    counts = jax.random.randint(key_count, (NLIST,), max(1, C_DEV // 8), C_DEV + 1)
    place = jax.random.randint(key_place, (), 0, NLIST)
    step_size = jax.random.randint(key_step, (), 1, NLIST)
    counts = counts.at[place].set(C_DEV)
    counts = counts.at[(place + step_size) % NLIST].set(max(1, C_DEV // 8))
    return counts.astype(jnp.int32)


def steps_of(key, shape, cuts, smallest, top_value):
    level, own = 1.0, jax.random.fold_in(key, 6)
    for axis_at, shards_of in cuts:
        heights = jnp.exp(jax.random.uniform(jax.random.fold_in(own, axis_at), (shards_of,), jnp.float32, smallest / len(cuts), top_value / len(cuts)))
        level = level * jnp.repeat(heights, shape[axis_at] // shards_of).reshape([-1 if axis == axis_at else 1 for axis in range(len(shape))])
    return level


def noise(rng, shape, width, limit, shards=(), kind=jnp.bfloat16):
    loudness = steps_of(rng, shape, shards, -0.22, 0.18) if shards else 1.0
    drawn = jax.random.normal(rng, shape, jnp.float32) * width * loudness
    return jnp.minimum(jnp.maximum(drawn, -limit), limit).astype(kind)


def setup_inputs(seed: int = 0, part: int = 0) -> dict:
    streams_of = jax.random.split(jax.random.key(seed), 6)
    own_keys = jax.random.split(jax.random.fold_in(streams_of[5], part), 6)
    psi = noise(own_keys[0], (NSEC, M, M), 1.0, 6.0, ((0, 16),))
    left_ops = noise(own_keys[1], (NOPS, M, M), M ** -0.5, 0.5, ((0, 16),))
    right_ops = noise(own_keys[2], (NOPS, M, M), (M * 16) ** -0.5, 0.125, ((0, 16),))
    couplings = draw_couplings(jax.random.fold_in(jax.random.fold_in(streams_of[5], part), 71), part)
    live = draw_live(jax.random.fold_in(jax.random.fold_in(streams_of[5], part), 71), part)
    return {"psi": psi, "left_ops": left_ops, "right_ops": right_ops, "couplings": couplings, "live": live}


def reference(psi, left_ops, right_ops, couplings, live):
    slot = jnp.arange(NCOUP, dtype=jnp.int32)
    owner = slot // C_DEV
    valid = ((slot % C_DEV) < live[owner]).astype(jnp.float32)
    block_ids = owner * OPS_DEV + couplings[0]
    sources = couplings[1]
    targets = couplings[2]

    def step(total, items):
        block_id, source, target, weight = items
        left = left_ops[block_id].astype(jnp.float32)
        right = right_ops[block_id].astype(jnp.float32)
        state = psi[source].astype(jnp.float32)
        half = jnp.einsum("bij,bjk->bik", left, state).astype(jnp.bfloat16)
        term = jnp.einsum("bij,bkj->bik", half.astype(jnp.float32), right)
        term = term * weight[:, None, None]
        return total.at[target].add(term), None

    items = (block_ids.reshape(NLIST, C_DEV), sources.reshape(NLIST, C_DEV),
             targets.reshape(NLIST, C_DEV), valid.reshape(NLIST, C_DEV))
    start = jnp.zeros((NSEC, M, M), jnp.float32)
    total, unused = lax.scan(step, start, items)
    return total
```

```python
import jax
import jax.numpy as jnp
from jax import lax
from jax.experimental import pallas as pl
from jax.experimental.pallas import tpu as pltpu
from jax.sharding import PartitionSpec as P

VMEM_LIMIT = 60 * 1024 * 1024


def transposed_dot(a, b):
    return lax.dot_general(
        a, b, (((1,), (1,)), ((), ())), preferred_element_type=jnp.float32
    )


def table_kernel(nsec, nops, me_ref, live_ref, coup_ref, *refs):
    psi = refs[:nsec]
    left_ref, right_ref = refs[nsec : nsec + 2]
    odd_ref, even_ref = refs[nsec + 2 : nsec + 4]
    half_ref, sum_ref = refs[nsec + 4 :]
    m = left_ref.shape[1]
    me = me_ref[0]

    step = 4
    for s in range(0, nsec, 2):
        pair = jnp.concatenate([psi[s][0], psi[s + 1][0]], axis=1)
        for g in range(0, nops, step):
            rows = left_ref[g : g + step].reshape(step * m, m)
            both = jnp.dot(rows, pair, preferred_element_type=jnp.float32).astype(jnp.bfloat16)
            half_ref[s, g : g + step] = both[:, :m].reshape(step, m, m)
            half_ref[s + 1, g : g + step] = both[:, m:].reshape(step, m, m)

    @pl.loop(0, nsec)
    def _(t):
        sum_ref[t] = jnp.zeros(sum_ref.shape[1:], jnp.float32)

    @pl.loop(0, live_ref[0])
    def _(c):
        g = coup_ref[0, c]
        s = coup_ref[1, c] ^ me
        t = coup_ref[2, c] ^ me
        sum_ref[t, g] += half_ref[s, g].astype(jnp.float32)

    rights = jnp.concatenate([right_ref[g] for g in range(nops)], axis=1)
    for t in range(nsec):
        sums = jnp.concatenate([sum_ref[t, g].astype(jnp.bfloat16) for g in range(nops)], axis=1)
        out = transposed_dot(sums, rights)
        if t % 2:
            odd_ref[t // 2] = out
        else:
            even_ref[t // 2] = out


def by_table(psi_blocks, left_ops, right_ops, couplings, live, me):
    nsec = len(psi_blocks)
    nops, m, _ = left_ops.shape
    vmem = pl.BlockSpec(memory_space=pltpu.VMEM)
    smem = pl.BlockSpec(memory_space=pltpu.SMEM)
    return pl.pallas_call(
        lambda *refs: table_kernel(nsec, nops, *refs),
        out_shape=[jax.ShapeDtypeStruct((nsec // 2, m, m), jnp.float32)] * 2,
        in_specs=[smem] * 3 + [vmem] * (nsec + 2),
        out_specs=[vmem] * 2,
        scratch_shapes=[
            pltpu.VMEM((nsec, nops, m, m), jnp.bfloat16),
            pltpu.VMEM((nsec, nops, m, m), jnp.float32),
        ],
        compiler_params=pltpu.CompilerParams(vmem_limit_bytes=VMEM_LIMIT),
        name="table",
    )(me, live, couplings, *psi_blocks, left_ops, right_ops)


def slot_kernel(live_ref, coup_ref, psi_ref, left_ref, right_ref, out_ref):
    out_ref[...] = jnp.zeros_like(out_ref)

    @pl.loop(0, live_ref[0])
    def _(c):
        g = coup_ref[0, c]
        half = jnp.dot(left_ref[g], psi_ref[coup_ref[1, c]], preferred_element_type=jnp.float32)
        out_ref[coup_ref[2, c]] += transposed_dot(half.astype(jnp.bfloat16), right_ref[g])


def by_slot(whole, left_ops, right_ops, couplings, live):
    vmem = pl.BlockSpec(memory_space=pltpu.VMEM)
    smem = pl.BlockSpec(memory_space=pltpu.SMEM)
    return pl.pallas_call(
        slot_kernel,
        out_shape=jax.ShapeDtypeStruct(whole.shape, jnp.float32),
        in_specs=[smem] * 2 + [vmem] * 3,
        out_specs=vmem,
        compiler_params=pltpu.CompilerParams(vmem_limit_bytes=VMEM_LIMIT),
        name="slots",
    )(live, couplings, whole, left_ops, right_ops)


def swap(x, ops, d):
    return lax.ppermute(x, "ops", [(i, i ^ d) for i in range(ops)])


def shards_small(ops, psi, left_ops, right_ops, couplings, live):
    me = lax.axis_index("ops").astype(jnp.int32)
    blocks = [None] * ops
    blocks[0] = psi
    for d in range(2, ops, 2):
        blocks[d] = swap(psi, ops, d)
    for d in range(0, ops, 2):
        blocks[d + 1] = swap(blocks[d], ops, 1)
    odd, even = by_table(blocks, left_ops, right_ops, couplings, live, me[None])
    chip = even + swap(odd, ops, 1)
    total = chip[0]
    for d in range(2, ops, 2):
        total = total + swap(chip[d // 2].astype(jnp.bfloat16), ops, d).astype(jnp.float32)
    return total[None]


def shards_large(psi, left_ops, right_ops, couplings, live):
    whole = lax.all_gather(psi, "ops", axis=0, tiled=True)
    total = by_slot(whole, left_ops, right_ops, couplings, live)
    return lax.psum_scatter(total, "ops", scatter_dimension=0, tiled=True)


def solution(mesh):
    ops = mesh.shape["ops"]
    placed = (
        P(("groups", "ops"), None, None),
        P(("groups", "ops"), None, None),
        P(("groups", "ops"), None, None),
        P(None, ("groups", "ops")),
        P(("groups", "ops")),
    )

    def shards(psi, *rest):
        small = psi.shape[0] == 1 and ops <= 16 and ops & (ops - 1) == 0
        if small:
            return shards_small(ops, psi, *rest)
        return shards_large(psi, *rest)

    return jax.shard_map(
        shards,
        mesh=mesh,
        in_specs=placed,
        out_specs=P(("groups", "ops"), None, None),
        check_vma=False,
    )
```

```python
import jax
import jax.numpy as jnp
from jax import lax
from jax.experimental import pallas as pl
from jax.experimental.pallas import tpu as pltpu
from jax.sharding import PartitionSpec as P

VMEM_LIMIT = 60 * 1024 * 1024


def transposed_dot(a, b):
    return lax.dot_general(
        a, b, (((1,), (1,)), ((), ())), preferred_element_type=jnp.float32
    )


def table_kernel(
    me_ref, live_ref, coup_ref, mine_ref, other_ref, left_ref, right_ref,
    sums_ref, sums_other_ref, half_ref, sum_ref,
):
    nops, m, _ = left_ref.shape
    chips = mine_ref.shape[0]
    me = me_ref[0]

    def place(sector):
        return ((sector ^ me) & 1) * chips + (sector >> 1)

    step = 4
    for s in range(0, 2 * chips, 2):
        psi_ref = mine_ref if s < chips else other_ref
        pair = jnp.concatenate([psi_ref[s % chips], psi_ref[s % chips + 1]], axis=1)
        for g in range(0, nops, step):
            rows = left_ref[g : g + step].reshape(step * m, m)
            both = jnp.dot(rows, pair, preferred_element_type=jnp.float32).astype(jnp.bfloat16)
            half_ref[s, g : g + step] = both[:, :m].reshape(step, m, m)
            half_ref[s + 1, g : g + step] = both[:, m:].reshape(step, m, m)

    @pl.loop(0, 2 * chips)
    def _(t):
        sum_ref[t] = jnp.zeros(sum_ref.shape[1:], jnp.float32)

    @pl.loop(0, live_ref[0])
    def _(c):
        g = coup_ref[0, c]
        sum_ref[place(coup_ref[2, c]), g] += half_ref[place(coup_ref[1, c]), g].astype(jnp.float32)

    rights = jnp.concatenate([right_ref[g] for g in range(nops)], axis=1)
    for t in range(2 * chips):
        sums = jnp.concatenate([sum_ref[t, g].astype(jnp.bfloat16) for g in range(nops)], axis=1)
        out_ref = sums_ref if t < chips else sums_other_ref
        out_ref[t % chips] = transposed_dot(sums, rights)


def by_table(mine, other, left_ops, right_ops, couplings, live, me):
    chips = mine.shape[0]
    nops, m, _ = left_ops.shape
    vmem = pl.BlockSpec(memory_space=pltpu.VMEM)
    smem = pl.BlockSpec(memory_space=pltpu.SMEM)
    return pl.pallas_call(
        table_kernel,
        out_shape=[jax.ShapeDtypeStruct((chips, m, m), jnp.float32)] * 2,
        in_specs=[smem] * 3 + [vmem] * 4,
        out_specs=[vmem] * 2,
        scratch_shapes=[
            pltpu.VMEM((2 * chips, nops, m, m), jnp.bfloat16),
            pltpu.VMEM((2 * chips, nops, m, m), jnp.float32),
        ],
        compiler_params=pltpu.CompilerParams(vmem_limit_bytes=VMEM_LIMIT),
        name="table",
    )(me, live, couplings, mine, other, left_ops, right_ops)


def slot_kernel(live_ref, coup_ref, psi_ref, left_ref, right_ref, out_ref):
    out_ref[...] = jnp.zeros_like(out_ref)

    @pl.loop(0, live_ref[0])
    def _(c):
        g = coup_ref[0, c]
        half = jnp.dot(left_ref[g], psi_ref[coup_ref[1, c]], preferred_element_type=jnp.float32)
        out_ref[coup_ref[2, c]] += transposed_dot(half.astype(jnp.bfloat16), right_ref[g])


def by_slot(whole, left_ops, right_ops, couplings, live):
    vmem = pl.BlockSpec(memory_space=pltpu.VMEM)
    smem = pl.BlockSpec(memory_space=pltpu.SMEM)
    return pl.pallas_call(
        slot_kernel,
        out_shape=jax.ShapeDtypeStruct(whole.shape, jnp.float32),
        in_specs=[smem] * 2 + [vmem] * 3,
        out_specs=vmem,
        compiler_params=pltpu.CompilerParams(vmem_limit_bytes=VMEM_LIMIT),
        name="slots",
    )(live, couplings, whole, left_ops, right_ops)


def swap(x, ops, d):
    return lax.ppermute(x, "ops", [(i, i ^ d) for i in range(ops)])


def shards_small(ops, psi, left_ops, right_ops, couplings, live):
    me = lax.axis_index("ops").astype(jnp.int32)
    same_core = [list(range(core, ops, 2)) for core in range(2)]
    copies = jnp.broadcast_to(psi, (ops // 2, *psi.shape[1:]))
    mine = lax.all_to_all(copies, "ops", 0, 0, axis_index_groups=same_core, tiled=True)
    other = swap(mine, ops, 1)
    sums, sums_other = by_table(mine, other, left_ops, right_ops, couplings, live, me[None])
    chip = sums + swap(sums_other, ops, 1)
    parts = lax.all_to_all(
        chip.astype(jnp.bfloat16), "ops", 0, 0, axis_index_groups=same_core, tiled=True
    )
    own = (jnp.arange(ops // 2, dtype=jnp.int32) == me >> 1)[:, None, None]
    return jnp.sum(jnp.where(own, chip, parts.astype(jnp.float32)), axis=0, keepdims=True)


def shards_large(psi, left_ops, right_ops, couplings, live):
    whole = lax.all_gather(psi, "ops", axis=0, tiled=True)
    total = by_slot(whole, left_ops, right_ops, couplings, live)
    return lax.psum_scatter(total, "ops", scatter_dimension=0, tiled=True)


def solution(mesh):
    ops = mesh.shape["ops"]
    placed = (
        P(("groups", "ops"), None, None),
        P(("groups", "ops"), None, None),
        P(("groups", "ops"), None, None),
        P(None, ("groups", "ops")),
        P(("groups", "ops")),
    )

    def shards(psi, *rest):
        small = psi.shape[0] == 1 and ops <= 16 and ops & (ops - 1) == 0
        if small:
            return shards_small(ops, psi, *rest)
        return shards_large(psi, *rest)

    return jax.shard_map(
        shards,
        mesh=mesh,
        in_specs=placed,
        out_specs=P(("groups", "ops"), None, None),
        check_vma=False,
    )
```

```python
import jax
import jax.numpy as jnp
from jax import lax
from jax.experimental import pallas as pl
from jax.experimental.pallas import tpu as pltpu
from jax.sharding import PartitionSpec as P

VMEM = pl.BlockSpec(memory_space=pltpu.VMEM)
SMEM = pl.BlockSpec(memory_space=pltpu.SMEM)

BLOCKS, CELL_BLOCK, SUM_FIRST, SUM_COUNT, TOTALS = range(5)


def transposed_dot(a, b):
    return lax.dot_general(
        a, b, (((1,), (1,)), ((), ())), preferred_element_type=jnp.float32
    )


def iota(shape, axis):
    return lax.broadcasted_iota(jnp.int32, shape, axis)


def count(mask, axis):
    return jnp.sum(mask.astype(jnp.float32), axis=axis, keepdims=True).astype(jnp.int32)


def picked(mask, values, axis):
    kept = jnp.where(mask, values, 0).astype(jnp.float32)
    return jnp.sum(kept, axis=axis, keepdims=True).astype(jnp.int32)


def as_column(row):
    n = row.shape[1]
    return picked(iota((n, n), 0) == iota((n, n), 1), row, 1)


def order_kernel(bits, nops, me_ref, live_ref, coup_ref, out_ref):
    slots = coup_ref.shape[1]
    cells = (1 << bits) * nops
    me = me_ref[0]

    def place(sector):
        near = sector ^ me
        spot = near & 0
        for b in range(bits):
            spot = spot | (((near >> b) & 1) << (bits - 1 - b))
        return spot

    g = coup_ref[0:1, :]
    alive = iota((1, slots), 1) < live_ref[0]
    cell = jnp.where(alive, place(coup_ref[2:3, :]) * nops + g, cells)
    block = place(coup_ref[1:2, :]) * nops + g
    cell_col = as_column(cell)
    block_col = as_column(block)
    square = (slots, slots)
    ahead = (cell < cell_col) | ((cell == cell_col) & (iota(square, 1) < iota(square, 0)))
    spot_col = count(ahead, 1)
    out_ref[BLOCKS : BLOCKS + 1, :] = picked(spot_col == iota(square, 1), block_col, 0)

    lane = iota((1, cells), 1)
    first = count(cell_col < lane, 0)
    here = cell_col == lane
    number = count(here, 0)
    only = picked(here, block_col, 0)
    kind = (number > 1).astype(jnp.int32) + (number > 2) + (number > 4)
    square = (cells, cells)
    kind_col = as_column(kind)
    ahead = (kind_col > kind) | ((kind_col == kind) & (iota(square, 0) < iota(square, 1)))
    spot = count(ahead, 0)
    cell_block = jnp.where(number == 0, cells, jnp.where(number == 1, only, cells + 1 + spot))
    chosen = as_column(spot) == iota(square, 1)
    out_ref[CELL_BLOCK : CELL_BLOCK + 1, :cells] = cell_block
    out_ref[SUM_FIRST : SUM_FIRST + 1, :cells] = picked(chosen, as_column(first), 0)
    out_ref[SUM_COUNT : SUM_COUNT + 1, :cells] = picked(chosen, as_column(number), 0)
    small = iota((1, 128), 1)
    ends = [count(kind > k, 1) for k in (2, 1, 0)]
    out_ref[TOTALS : TOTALS + 1, :128] = jnp.where(
        small == 0, ends[0], jnp.where(small == 1, ends[1], ends[2])
    )


def order_slots(bits, nops, couplings, live, me):
    slots = couplings.shape[1]
    cells = (1 << bits) * nops
    return pl.pallas_call(
        lambda *refs: order_kernel(bits, nops, *refs),
        out_shape=jax.ShapeDtypeStruct((8, max(slots, cells)), jnp.int32),
        in_specs=[SMEM, SMEM, VMEM],
        out_specs=VMEM,
        compiler_params=pltpu.CompilerParams(vmem_limit_bytes=16 * 1024 * 1024),
        cost_estimate=pl.CostEstimate(
            flops=20 * slots * slots, bytes_accessed=4 * 11 * slots, transcendentals=0
        ),
        name="order",
    )(me, live, couplings)


def table_kernel(order_ref, near_ref, far_ref, left_ref, right_ref, keep_ref, send_ref, block_ref):
    nops, m, _ = left_ref.shape
    half = near_ref.shape[0]
    cells = 2 * half * nops

    step = 4
    for s in range(0, 2 * half, 2):
        psi_ref = near_ref if s < half else far_ref
        pair = jnp.concatenate([psi_ref[s % half], psi_ref[s % half + 1]], axis=1)
        for g in range(0, nops, step):
            rows = left_ref[g : g + step].reshape(step * m, m)
            both = jnp.dot(rows, pair, preferred_element_type=jnp.float32).astype(jnp.bfloat16)
            at = s * nops + g
            block_ref[at : at + step] = both[:, :m].reshape(step, m, m)
            block_ref[at + nops : at + nops + step] = both[:, m:].reshape(step, m, m)
    block_ref[cells] = jnp.zeros((m, m), jnp.bfloat16)

    many, some, two = (order_ref[TOTALS, k] for k in range(3))

    @pl.loop(0, many)
    def _(k):
        first = order_ref[SUM_FIRST, k]

        def add(j, total):
            return total + block_ref[order_ref[BLOCKS, first + j]].astype(jnp.float32)

        total = lax.fori_loop(0, order_ref[SUM_COUNT, k], add, jnp.zeros((m, m), jnp.float32))
        block_ref[cells + 1 + k] = total.astype(jnp.bfloat16)

    @pl.loop(many, some)
    def _(k):
        first = order_ref[SUM_FIRST, k]
        fourth = jnp.where(order_ref[SUM_COUNT, k] == 4, order_ref[BLOCKS, first + 3], cells)
        total = block_ref[order_ref[BLOCKS, first]].astype(jnp.float32)
        total += block_ref[order_ref[BLOCKS, first + 1]].astype(jnp.float32)
        total += block_ref[order_ref[BLOCKS, first + 2]].astype(jnp.float32)
        total += block_ref[fourth].astype(jnp.float32)
        block_ref[cells + 1 + k] = total.astype(jnp.bfloat16)

    @pl.loop(some, two, step=2)
    def _(k):
        ks = (k, jnp.minimum(k + 1, two - 1))
        firsts = [order_ref[SUM_FIRST, k] for k in ks]
        totals = [
            block_ref[order_ref[BLOCKS, first]] + block_ref[order_ref[BLOCKS, first + 1]]
            for first in firsts
        ]
        for k, total in zip(ks, totals):
            block_ref[cells + 1 + k] = total

    rights = jnp.concatenate([right_ref[g] for g in range(nops)], axis=1)
    for t in range(0, 2 * half, 2):
        rows = [
            jnp.concatenate(
                [block_ref[order_ref[CELL_BLOCK, (t + i) * nops + g]] for g in range(nops)], axis=1
            )
            for i in range(2)
        ]
        out = transposed_dot(jnp.concatenate(rows, axis=0), rights)
        out_ref = keep_ref if t < half else send_ref
        out_ref[t % half : t % half + 2] = out.reshape(2, m, m)


def by_table(near, far, left_ops, right_ops, order):
    half = near.shape[0]
    nops, m, _ = left_ops.shape
    cells = 2 * half * nops
    slots = order.shape[1]
    return pl.pallas_call(
        table_kernel,
        out_shape=[jax.ShapeDtypeStruct((half, m, m), jnp.float32)] * 2,
        in_specs=[SMEM] + [VMEM] * 4,
        out_specs=[VMEM] * 2,
        scratch_shapes=[pltpu.VMEM((cells + 1 + slots // 2, m, m), jnp.bfloat16)],
        compiler_params=pltpu.CompilerParams(vmem_limit_bytes=24 * 1024 * 1024),
        cost_estimate=pl.CostEstimate(
            flops=4 * cells * m**3, bytes_accessed=4 * nops * m * m, transcendentals=0
        ),
        name="table",
    )(order, near, far, left_ops, right_ops)


def slot_kernel(live_ref, coup_ref, psi_ref, left_ref, right_ref, out_ref):
    out_ref[...] = jnp.zeros_like(out_ref)

    @pl.loop(0, live_ref[0])
    def _(c):
        g = coup_ref[0, c]
        half = jnp.dot(left_ref[g], psi_ref[coup_ref[1, c]], preferred_element_type=jnp.float32)
        out_ref[coup_ref[2, c]] += transposed_dot(half.astype(jnp.bfloat16), right_ref[g])


def by_slot(whole, left_ops, right_ops, couplings, live):
    return pl.pallas_call(
        slot_kernel,
        out_shape=jax.ShapeDtypeStruct(whole.shape, jnp.float32),
        in_specs=[SMEM] * 2 + [VMEM] * 3,
        out_specs=VMEM,
        compiler_params=pltpu.CompilerParams(vmem_limit_bytes=60 * 1024 * 1024),
        name="slots",
    )(live, couplings, whole, left_ops, right_ops)


def swap(x, ops, d):
    return lax.ppermute(x, "ops", [(i, i ^ d) for i in range(ops)])


def shards_small(ops, psi, left_ops, right_ops, couplings, live):
    bits = ops.bit_length() - 1
    me = lax.axis_index("ops").astype(jnp.int32)
    order = order_slots(bits, left_ops.shape[0], couplings, live, me[None])
    near = psi
    for b in reversed(range(1, bits)):
        near = jnp.concatenate([near, swap(near, ops, 1 << b)], axis=0)
    far = swap(near, ops, 1)
    keep, send = by_table(near, far, left_ops, right_ops, order)
    for b in range(bits):
        came = swap(send, ops, 1 << b).astype(jnp.float32)
        half = keep.shape[0] // 2
        if half:
            send = (keep[half:] + came[half:]).astype(jnp.bfloat16)
            keep = keep[:half] + came[:half]
    return keep + came


def shards_large(psi, left_ops, right_ops, couplings, live):
    whole = lax.all_gather(psi, "ops", axis=0, tiled=True)
    total = by_slot(whole, left_ops, right_ops, couplings, live)
    return lax.psum_scatter(total, "ops", scatter_dimension=0, tiled=True)


def solution(mesh):
    ops = mesh.shape["ops"]
    placed = (
        P(("groups", "ops"), None, None),
        P(("groups", "ops"), None, None),
        P(("groups", "ops"), None, None),
        P(None, ("groups", "ops")),
        P(("groups", "ops")),
    )

    def shards(psi, *rest):
        small = psi.shape[0] == 1 and 4 <= ops <= 16 and ops & (ops - 1) == 0
        if small:
            return shards_small(ops, psi, *rest)
        return shards_large(psi, *rest)

    return jax.shard_map(
        shards,
        mesh=mesh,
        in_specs=placed,
        out_specs=P(("groups", "ops"), None, None),
        check_vma=False,
    )
```

```python
import jax
import jax.numpy as jnp
from jax import lax
from jax.experimental import pallas as pl
from jax.experimental.pallas import tpu as pltpu
from jax.sharding import PartitionSpec as P

VMEM = pl.BlockSpec(memory_space=pltpu.VMEM)
SMEM = pl.BlockSpec(memory_space=pltpu.SMEM)

BLOCKS, CELL_BLOCK, SUM_FIRST, SUM_COUNT, ENDS = range(5)


def transposed_dot(a, b):
    return lax.dot_general(
        a, b, (((1,), (1,)), ((), ())), preferred_element_type=jnp.float32
    )


def iota(shape, axis):
    return lax.broadcasted_iota(jnp.int32, shape, axis)


def count(mask, axis):
    return jnp.sum(mask.astype(jnp.float32), axis=axis, keepdims=True).astype(jnp.int32)


def picked(mask, values, axis):
    kept = jnp.where(mask, values, 0).astype(jnp.float32)
    return jnp.sum(kept, axis=axis, keepdims=True).astype(jnp.int32)


def as_column(row):
    n = row.shape[1]
    return picked(iota((n, n), 0) == iota((n, n), 1), row, 1)


def order_kernel(chips, nops, me_ref, live_ref, coup_ref, right_ref, out_ref, turned_ref):
    slots = coup_ref.shape[1]
    m = right_ref.shape[1]
    cells = 2 * chips * nops
    me = me_ref[0]

    def place(sector):
        return ((sector ^ me) & 1) * chips + (sector >> 1)

    g = coup_ref[0:1, :]
    alive = iota((1, slots), 1) < live_ref[0]
    cell = jnp.where(alive, place(coup_ref[2:3, :]) * nops + g, cells)
    block = place(coup_ref[1:2, :]) * nops + g
    cell_col = as_column(cell)
    block_col = as_column(block)
    square = (slots, slots)
    ahead = (cell < cell_col) | ((cell == cell_col) & (iota(square, 1) < iota(square, 0)))
    spot_col = count(ahead, 1)
    out_ref[BLOCKS : BLOCKS + 1, :] = picked(spot_col == iota(square, 1), block_col, 0)

    lane = iota((1, cells), 1)
    first = count(cell_col < lane, 0)
    here = cell_col == lane
    number = count(here, 0)
    only = picked(here, block_col, 0)
    few = (number <= 4).astype(jnp.int32) + (number <= 2).astype(jnp.int32)
    kind = jnp.where(number < 2, 6, few + jnp.where(lane < cells // 2, 3, 0))
    square = (cells, cells)
    kind_col = as_column(kind)
    ahead = (kind_col < kind) | ((kind_col == kind) & (iota(square, 0) < iota(square, 1)))
    spot = count(ahead, 0)
    cell_block = jnp.where(number == 0, cells, jnp.where(number == 1, only, cells + 1 + spot))
    chosen = as_column(spot) == iota(square, 1)
    out_ref[CELL_BLOCK : CELL_BLOCK + 1, :cells] = cell_block
    out_ref[SUM_FIRST : SUM_FIRST + 1, :cells] = picked(chosen, as_column(first), 0)
    out_ref[SUM_COUNT : SUM_COUNT + 1, :cells] = picked(chosen, as_column(number), 0)
    small = iota((1, 128), 1)
    ends = jnp.zeros((1, 128), jnp.int32)
    for k in range(6):
        ends = jnp.where(small == k, count(kind <= k, 1), ends)
    out_ref[ENDS : ENDS + 1, :128] = ends

    for g in range(nops):
        turned_ref[g * m : (g + 1) * m] = right_ref[g].T


def order_slots(chips, right_ops, couplings, live, me):
    slots = couplings.shape[1]
    nops, m, _ = right_ops.shape
    cells = 2 * chips * nops
    return pl.pallas_call(
        lambda *refs: order_kernel(chips, nops, *refs),
        out_shape=[
            jax.ShapeDtypeStruct((8, max(slots, cells)), jnp.int32),
            jax.ShapeDtypeStruct((nops * m, m), jnp.bfloat16),
        ],
        in_specs=[SMEM, SMEM, VMEM, VMEM],
        out_specs=[VMEM, VMEM],
        compiler_params=pltpu.CompilerParams(vmem_limit_bytes=16 * 1024 * 1024),
        cost_estimate=pl.CostEstimate(
            flops=20 * slots * slots, bytes_accessed=4 * nops * m * m, transcendentals=0
        ),
        name="order",
    )(me, live, couplings, right_ops)


def add_up(order_ref, block_ref, cells, begin, ends):
    many, some, two = ends
    m = block_ref.shape[1]

    @pl.loop(begin, many)
    def _(k):
        first = order_ref[SUM_FIRST, k]

        def add(j, total):
            return total + block_ref[order_ref[BLOCKS, first + j]].astype(jnp.float32)

        total = lax.fori_loop(0, order_ref[SUM_COUNT, k], add, jnp.zeros((m, m), jnp.float32))
        block_ref[cells + 1 + k] = total.astype(jnp.bfloat16)

    @pl.loop(many, some)
    def _(k):
        first = order_ref[SUM_FIRST, k]
        fourth = jnp.where(order_ref[SUM_COUNT, k] == 4, order_ref[BLOCKS, first + 3], cells)
        total = block_ref[order_ref[BLOCKS, first]].astype(jnp.float32)
        total += block_ref[order_ref[BLOCKS, first + 1]].astype(jnp.float32)
        total += block_ref[order_ref[BLOCKS, first + 2]].astype(jnp.float32)
        total += block_ref[fourth].astype(jnp.float32)
        block_ref[cells + 1 + k] = total.astype(jnp.bfloat16)

    @pl.loop(some, two, step=2)
    def _(k):
        ks = (k, jnp.minimum(k + 1, two - 1))
        firsts = [order_ref[SUM_FIRST, k] for k in ks]
        totals = [
            block_ref[order_ref[BLOCKS, first]] + block_ref[order_ref[BLOCKS, first + 1]]
            for first in firsts
        ]
        for k, total in zip(ks, totals):
            block_ref[cells + 1 + k] = total


def multiply(order_ref, block_ref, turned_ref, out_ref, offset, nops):
    half, m, _ = out_ref.shape
    for t in range(0, half, 2):
        rows = [
            jnp.concatenate(
                [
                    block_ref[order_ref[CELL_BLOCK, (offset + t + i) * nops + g]]
                    for g in range(nops)
                ],
                axis=1,
            )
            for i in range(2)
        ]
        out = jnp.dot(
            jnp.concatenate(rows, axis=0), turned_ref[...], preferred_element_type=jnp.float32
        )
        out_ref[t : t + 2] = out.reshape(2, m, m)


def first_kernel(order_ref, near_ref, far_ref, left_ref, turned_ref, block_ref, send_ref):
    nops, m, _ = left_ref.shape
    half = near_ref.shape[0]
    cells = 2 * half * nops

    step = 4
    for s in range(0, 2 * half, 2):
        psi_ref = near_ref if s < half else far_ref
        pair = jnp.concatenate([psi_ref[s % half], psi_ref[s % half + 1]], axis=1)
        for g in range(0, nops, step):
            rows = left_ref[g : g + step].reshape(step * m, m)
            both = jnp.dot(rows, pair, preferred_element_type=jnp.float32).astype(jnp.bfloat16)
            at = s * nops + g
            block_ref[at : at + step] = both[:, :m].reshape(step, m, m)
            block_ref[at + nops : at + nops + step] = both[:, m:].reshape(step, m, m)
    block_ref[cells] = jnp.zeros((m, m), jnp.bfloat16)

    add_up(order_ref, block_ref, cells, 0, [order_ref[ENDS, k] for k in range(3)])
    multiply(order_ref, block_ref, turned_ref, send_ref, half, nops)


def second_kernel(nops, order_ref, _, turned_ref, block_ref, keep_ref):
    half = keep_ref.shape[0]
    ends = [order_ref[ENDS, k] for k in range(2, 6)]
    add_up(order_ref, block_ref, 2 * half * nops, ends[0], ends[1:])
    multiply(order_ref, block_ref, turned_ref, keep_ref, 0, nops)


def first_part(near, far, left_ops, turned, order):
    half = near.shape[0]
    nops, m, _ = left_ops.shape
    cells = 2 * half * nops
    slots = order.shape[1]
    return pl.pallas_call(
        first_kernel,
        out_shape=[
            jax.ShapeDtypeStruct((cells + 1 + slots // 2, m, m), jnp.bfloat16),
            jax.ShapeDtypeStruct((half, m, m), jnp.float32),
        ],
        in_specs=[SMEM] + [VMEM] * 4,
        out_specs=[VMEM, VMEM],
        compiler_params=pltpu.CompilerParams(vmem_limit_bytes=24 * 1024 * 1024),
        cost_estimate=pl.CostEstimate(
            flops=4 * cells * m**3, bytes_accessed=4 * nops * m * m, transcendentals=0
        ),
        name="first",
    )(order, near, far, left_ops, turned)


def second_part(half, blocks, turned, order):
    m = blocks.shape[1]
    nops = turned.shape[0] // m
    return pl.pallas_call(
        lambda *refs: second_kernel(nops, *refs),
        out_shape=[
            jax.ShapeDtypeStruct(blocks.shape, blocks.dtype),
            jax.ShapeDtypeStruct((half, m, m), jnp.float32),
        ],
        in_specs=[SMEM, VMEM, VMEM],
        out_specs=[VMEM, VMEM],
        input_output_aliases={1: 0},
        compiler_params=pltpu.CompilerParams(vmem_limit_bytes=24 * 1024 * 1024),
        cost_estimate=pl.CostEstimate(
            flops=4 * half * nops * m**3, bytes_accessed=4 * nops * m * m, transcendentals=0
        ),
        name="second",
    )(order, blocks, turned)[1]


def slot_kernel(live_ref, coup_ref, psi_ref, left_ref, right_ref, out_ref):
    out_ref[...] = jnp.zeros_like(out_ref)

    @pl.loop(0, live_ref[0])
    def _(c):
        g = coup_ref[0, c]
        half = jnp.dot(left_ref[g], psi_ref[coup_ref[1, c]], preferred_element_type=jnp.float32)
        out_ref[coup_ref[2, c]] += transposed_dot(half.astype(jnp.bfloat16), right_ref[g])


def by_slot(whole, left_ops, right_ops, couplings, live):
    return pl.pallas_call(
        slot_kernel,
        out_shape=jax.ShapeDtypeStruct(whole.shape, jnp.float32),
        in_specs=[SMEM] * 2 + [VMEM] * 3,
        out_specs=VMEM,
        compiler_params=pltpu.CompilerParams(vmem_limit_bytes=60 * 1024 * 1024),
        name="slots",
    )(live, couplings, whole, left_ops, right_ops)


def swap(x, ops, d):
    return lax.ppermute(x, "ops", [(i, i ^ d) for i in range(ops)])


def shards_small(ops, psi, left_ops, right_ops, couplings, live):
    chips = ops // 2
    me = lax.axis_index("ops").astype(jnp.int32)
    same_core = [list(range(core, ops, 2)) for core in range(2)]
    order, turned = order_slots(chips, right_ops, couplings, live, me[None])
    copies = jnp.broadcast_to(psi, (chips, *psi.shape[1:]))
    near = lax.all_to_all(copies, "ops", 0, 0, axis_index_groups=same_core, tiled=True)
    far = swap(near, ops, 1)
    blocks, send = first_part(near, far, left_ops, turned, order)
    came = swap(send, ops, 1)
    keep = second_part(chips, blocks, turned, order)
    chip = keep + came
    parts = lax.all_to_all(
        chip.astype(jnp.bfloat16), "ops", 0, 0, axis_index_groups=same_core, tiled=True
    )
    own = (jnp.arange(chips, dtype=jnp.int32) == me >> 1)[:, None, None]
    return jnp.sum(jnp.where(own, chip, parts.astype(jnp.float32)), axis=0, keepdims=True)


def shards_large(psi, left_ops, right_ops, couplings, live):
    whole = lax.all_gather(psi, "ops", axis=0, tiled=True)
    total = by_slot(whole, left_ops, right_ops, couplings, live)
    return lax.psum_scatter(total, "ops", scatter_dimension=0, tiled=True)


def solution(mesh):
    ops = mesh.shape["ops"]
    placed = (
        P(("groups", "ops"), None, None),
        P(("groups", "ops"), None, None),
        P(("groups", "ops"), None, None),
        P(None, ("groups", "ops")),
        P(("groups", "ops")),
    )

    def shards(psi, *rest):
        small = psi.shape[0] == 1 and 4 <= ops <= 16 and ops & (ops - 1) == 0
        if small:
            return shards_small(ops, psi, *rest)
        return shards_large(psi, *rest)

    return jax.shard_map(
        shards,
        mesh=mesh,
        in_specs=placed,
        out_specs=P(("groups", "ops"), None, None),
        check_vma=False,
    )
```

```python
import jax
import jax.numpy as jnp
from jax import lax
from jax.experimental import pallas as pl
from jax.experimental.pallas import tpu as pltpu
from jax.sharding import PartitionSpec as P

VMEM = pl.BlockSpec(memory_space=pltpu.VMEM)
SMEM = pl.BlockSpec(memory_space=pltpu.SMEM)

BLOCKS, CELL_BLOCK, SUM_FIRST, SUM_COUNT, ENDS = range(5)


def transposed_dot(a, b):
    return lax.dot_general(
        a, b, (((1,), (1,)), ((), ())), preferred_element_type=jnp.float32
    )


def iota(shape, axis):
    return lax.broadcasted_iota(jnp.int32, shape, axis)


def count(mask, axis):
    return jnp.sum(mask.astype(jnp.float32), axis=axis, keepdims=True).astype(jnp.int32)


def picked(mask, values, axis):
    kept = jnp.where(mask, values, 0).astype(jnp.float32)
    return jnp.sum(kept, axis=axis, keepdims=True).astype(jnp.int32)


def as_column(row):
    n = row.shape[1]
    return picked(iota((n, n), 0) == iota((n, n), 1), row, 1)


CHAINS = ((1, 3, 2), (3, 2, 1))
OPS = 16


def partners(step):
    return [(i, i ^ (1 << CHAINS[i & 1][step])) for i in range(OPS)]


def other_core(x):
    return lax.ppermute(x, "ops", [(i, i ^ 1) for i in range(OPS)])


def place(sector, me):
    near = sector ^ me
    spots = [
        sum(((near >> bit) & 1) << step for step, bit in enumerate(chain)) for chain in CHAINS
    ]
    return (near & 1) * (OPS // 2) + jnp.where(sector & 1 == 0, spots[0], spots[1])


def order_kernel(nops, coup_ref, out_ref):
    slots = coup_ref.shape[1]
    cells = OPS * nops
    me = lax.axis_index("ops").astype(jnp.int32)

    g = coup_ref[0:1, :]
    alive = iota((1, slots), 1) < coup_ref[3:4, :]
    cell = jnp.where(alive, place(coup_ref[2:3, :], me) * nops + g, cells)
    block = place(coup_ref[1:2, :], me) * nops + g
    cell_col = as_column(cell)
    block_col = as_column(block)
    square = (slots, slots)
    ahead = (cell < cell_col) | ((cell == cell_col) & (iota(square, 1) < iota(square, 0)))
    spot_col = count(ahead, 1)
    out_ref[BLOCKS : BLOCKS + 1, :] = picked(spot_col == iota(square, 1), block_col, 0)

    lane = iota((1, cells), 1)
    first = count(cell_col < lane, 0)
    here = cell_col == lane
    number = count(here, 0)
    only = picked(here, block_col, 0)
    few = (number <= 4).astype(jnp.int32) + (number <= 2).astype(jnp.int32)
    group = (lane < cells // 2).astype(jnp.int32) + (lane < cells // 4).astype(jnp.int32)
    kind = jnp.where(number < 2, 9, few + 3 * group)
    square = (cells, cells)
    kind_col = as_column(kind)
    ahead = (kind_col < kind) | ((kind_col == kind) & (iota(square, 0) < iota(square, 1)))
    spot = count(ahead, 0)
    cell_block = jnp.where(number == 0, cells, jnp.where(number == 1, only, cells + 1 + spot))
    chosen = as_column(spot) == iota(square, 1)
    out_ref[CELL_BLOCK : CELL_BLOCK + 1, :cells] = cell_block
    out_ref[SUM_FIRST : SUM_FIRST + 1, :cells] = picked(chosen, as_column(first), 0)
    out_ref[SUM_COUNT : SUM_COUNT + 1, :cells] = picked(chosen, as_column(number), 0)
    small = iota((1, 128), 1)
    ends = jnp.zeros((1, 128), jnp.int32)
    for k in range(9):
        ends = jnp.where(small == k, count(kind <= k, 1), ends)
    out_ref[ENDS : ENDS + 1, :128] = ends


def params(limit):
    return pltpu.CompilerParams(vmem_limit_bytes=limit * 1024 * 1024)


def cost(flops):
    return pl.CostEstimate(flops=flops, bytes_accessed=1 << 20, transcendentals=0)


def order_slots(nops, couplings, live):
    slots = couplings.shape[1]
    rows = jnp.concatenate([couplings, jnp.broadcast_to(live[None], (1, slots))], axis=0)
    return pl.pallas_call(
        lambda *refs: order_kernel(nops, *refs),
        out_shape=jax.ShapeDtypeStruct((8, max(slots, OPS * nops)), jnp.int32),
        in_specs=[VMEM],
        out_specs=VMEM,
        compiler_params=params(16),
        cost_estimate=cost(20 * slots * slots),
        name="order",
    )(rows)


def hold_kernel(psi_ref, left_ref, psi_out, left_out):
    psi_out[...] = psi_ref[...]
    left_out[...] = left_ref[...]


def hold(psi, left_ops):
    return pl.pallas_call(
        hold_kernel,
        out_shape=[jax.ShapeDtypeStruct(x.shape, x.dtype) for x in (psi, left_ops)],
        in_specs=[VMEM] * 2,
        out_specs=[VMEM] * 2,
        compiler_params=params(4),
        cost_estimate=cost(0),
        name="hold",
    )(psi, left_ops)


def turn_kernel(right_ref, turned_ref):
    nops, m, _ = right_ref.shape
    for g in range(nops):
        turned_ref[g * m : (g + 1) * m] = right_ref[g].T


def turn(right_ops):
    nops, m, _ = right_ops.shape
    return pl.pallas_call(
        turn_kernel,
        out_shape=jax.ShapeDtypeStruct((nops * m, m), jnp.bfloat16),
        in_specs=[VMEM],
        out_specs=VMEM,
        compiler_params=params(4),
        cost_estimate=cost(0),
        name="turn",
    )(right_ops)


def add_up(order_ref, block_ref, cells, begin, ends):
    many, some, two = ends
    m = block_ref.shape[1]

    @pl.loop(begin, many)
    def _(k):
        first = order_ref[SUM_FIRST, k]

        def add(j, total):
            return total + block_ref[order_ref[BLOCKS, first + j]].astype(jnp.float32)

        total = lax.fori_loop(0, order_ref[SUM_COUNT, k], add, jnp.zeros((m, m), jnp.float32))
        block_ref[cells + 1 + k] = total.astype(jnp.bfloat16)

    @pl.loop(many, some)
    def _(k):
        first = order_ref[SUM_FIRST, k]
        fourth = jnp.where(order_ref[SUM_COUNT, k] == 4, order_ref[BLOCKS, first + 3], cells)
        total = block_ref[order_ref[BLOCKS, first]].astype(jnp.float32)
        total += block_ref[order_ref[BLOCKS, first + 1]].astype(jnp.float32)
        total += block_ref[order_ref[BLOCKS, first + 2]].astype(jnp.float32)
        total += block_ref[fourth].astype(jnp.float32)
        block_ref[cells + 1 + k] = total.astype(jnp.bfloat16)

    @pl.loop(some, two, step=2)
    def _(k):
        ks = (k, jnp.minimum(k + 1, two - 1))
        firsts = [order_ref[SUM_FIRST, k] for k in ks]
        totals = [
            block_ref[order_ref[BLOCKS, first]] + block_ref[order_ref[BLOCKS, first + 1]]
            for first in firsts
        ]
        for k, total in zip(ks, totals):
            block_ref[cells + 1 + k] = total


def multiply(order_ref, block_ref, turned_ref, out_ref, offset, nops):
    half, m, _ = out_ref.shape
    for t in range(0, half, 2):
        rows = [
            jnp.concatenate(
                [
                    block_ref[order_ref[CELL_BLOCK, (offset + t + i) * nops + g]]
                    for g in range(nops)
                ],
                axis=1,
            )
            for i in range(2)
        ]
        out = jnp.dot(
            jnp.concatenate(rows, axis=0), turned_ref[...], preferred_element_type=jnp.float32
        )
        out_ref[t : t + 2] = out.reshape(2, m, m)


def fill(psi_ref, left_ref, block_ref, offset):
    nops, m, _ = left_ref.shape
    step = 4
    for s in range(0, psi_ref.shape[0], 2):
        pair = jnp.concatenate([psi_ref[s], psi_ref[s + 1]], axis=1)
        for g in range(0, nops, step):
            rows = left_ref[g : g + step].reshape(step * m, m)
            both = jnp.dot(rows, pair, preferred_element_type=jnp.float32).astype(jnp.bfloat16)
            at = (offset + s) * nops + g
            block_ref[at : at + step] = both[:, :m].reshape(step, m, m)
            block_ref[at + nops : at + nops + step] = both[:, m:].reshape(step, m, m)


def early_kernel(psi_ref, left_ref, block_ref):
    nops, m, _ = left_ref.shape
    fill(psi_ref, left_ref, block_ref, 0)
    block_ref[OPS * nops] = jnp.zeros((m, m), jnp.bfloat16)


def early(psi, left, slots):
    nops, m, _ = left.shape
    cells = OPS * nops
    return pl.pallas_call(
        early_kernel,
        out_shape=jax.ShapeDtypeStruct((cells + 1 + slots // 2, m, m), jnp.bfloat16),
        in_specs=[VMEM] * 2,
        out_specs=VMEM,
        compiler_params=params(24),
        cost_estimate=cost(2 * psi.shape[0] * nops * m**3),
        name="early",
    )(psi, left)


def more(psi, left, blocks, offset):
    nops, m, _ = left.shape

    def kernel(psi_ref, left_ref, _, block_ref):
        fill(psi_ref, left_ref, block_ref, offset)

    return pl.pallas_call(
        kernel,
        out_shape=jax.ShapeDtypeStruct(blocks.shape, blocks.dtype),
        in_specs=[VMEM] * 3,
        out_specs=VMEM,
        input_output_aliases={2: 0},
        compiler_params=params(24),
        cost_estimate=cost(2 * psi.shape[0] * nops * m**3),
        name="more",
    )(psi, left, blocks)


def terms(order, turned, blocks, group, offset, number, psi=None, left=None):
    m = blocks.shape[1]
    nops = turned.shape[0] // m
    cells = OPS * nops
    extra = [] if psi is None else [psi, left]

    def kernel(order_ref, turned_ref, *refs):
        block_ref, out_ref = refs[-2:]
        if extra:
            fill(refs[0], refs[1], block_ref, OPS // 2)
        begin = order_ref[ENDS, 3 * group - 1] if group else 0
        add_up(
            order_ref, block_ref, cells, begin, [order_ref[ENDS, 3 * group + k] for k in range(3)]
        )
        multiply(order_ref, block_ref, turned_ref, out_ref, offset, nops)

    return pl.pallas_call(
        kernel,
        out_shape=[
            jax.ShapeDtypeStruct(blocks.shape, blocks.dtype),
            jax.ShapeDtypeStruct((number, m, m), jnp.float32),
        ],
        in_specs=[SMEM] + [VMEM] * (2 + len(extra)),
        out_specs=[VMEM] * 2,
        input_output_aliases={2 + len(extra): 0},
        compiler_params=params(24),
        cost_estimate=cost(2 * (number + len(extra) * 4) * nops * m**3),
        name=f"terms_{group}",
    )(order, turned, *extra, blocks)


def slot_kernel(live_ref, coup_ref, psi_ref, left_ref, right_ref, out_ref):
    out_ref[...] = jnp.zeros_like(out_ref)

    @pl.loop(0, live_ref[0])
    def _(c):
        g = coup_ref[0, c]
        half = jnp.dot(left_ref[g], psi_ref[coup_ref[1, c]], preferred_element_type=jnp.float32)
        out_ref[coup_ref[2, c]] += transposed_dot(half.astype(jnp.bfloat16), right_ref[g])


def by_slot(whole, left_ops, right_ops, couplings, live):
    return pl.pallas_call(
        slot_kernel,
        out_shape=jax.ShapeDtypeStruct(whole.shape, jnp.float32),
        in_specs=[SMEM] * 2 + [VMEM] * 3,
        out_specs=VMEM,
        compiler_params=pltpu.CompilerParams(vmem_limit_bytes=60 * 1024 * 1024),
        name="slots",
    )(live, couplings, whole, left_ops, right_ops)


def shards_small(psi, left_ops, right_ops, couplings, live):
    slots = couplings.shape[1]
    came = lax.ppermute(psi, "ops", partners(0))
    psi, left = hold(psi, left_ops)
    two, left = lax.optimization_barrier((jnp.concatenate([psi, came], axis=0), left))
    came = lax.ppermute(two, "ops", partners(1))
    order = order_slots(left_ops.shape[0], couplings, live)
    four, order = lax.optimization_barrier((jnp.concatenate([two, came], axis=0), order))
    came = lax.ppermute(four, "ops", partners(2))
    blocks = early(four, left, slots)
    turned = turn(right_ops)
    eight, turned, blocks = lax.optimization_barrier(
        (jnp.concatenate([four, came], axis=0), turned, blocks)
    )
    far = other_core(eight)
    blocks = more(came, left, blocks, 4)
    blocks, send = terms(order, turned, blocks, 0, 8, 8, far, left)
    came = other_core(send)
    blocks, next_four = terms(order, turned, blocks, 1, 4, 4)
    leaving = (next_four + came[4:]).astype(jnp.bfloat16)
    arrived = lax.ppermute(leaving, "ops", partners(2))
    _, last_four = terms(order, turned, blocks, 2, 0, 4)
    keep = last_four + came[:4]
    for step in (1, 0):
        half = keep.shape[0] // 2
        both = keep + arrived.astype(jnp.float32)
        keep, leaving = both[:half], both[half:].astype(jnp.bfloat16)
        arrived = lax.ppermute(leaving, "ops", partners(step))
    return keep + arrived.astype(jnp.float32)


def shards_large(psi, left_ops, right_ops, couplings, live):
    whole = lax.all_gather(psi, "ops", axis=0, tiled=True)
    total = by_slot(whole, left_ops, right_ops, couplings, live)
    return lax.psum_scatter(total, "ops", scatter_dimension=0, tiled=True)


def solution(mesh):
    ops = mesh.shape["ops"]
    placed = (
        P(("groups", "ops"), None, None),
        P(("groups", "ops"), None, None),
        P(("groups", "ops"), None, None),
        P(None, ("groups", "ops")),
        P(("groups", "ops")),
    )

    def shards(psi, *rest):
        if ops == OPS and psi.shape[0] == 1:
            return shards_small(psi, *rest)
        return shards_large(psi, *rest)

    return jax.shard_map(
        shards,
        mesh=mesh,
        in_specs=placed,
        out_specs=P(("groups", "ops"), None, None),
        check_vma=False,
    )
```

```python
import jax
import jax.numpy as jnp
from jax import lax
from jax.experimental import pallas as pl
from jax.experimental.pallas import tpu as pltpu
from jax.sharding import PartitionSpec as P

VMEM = pl.BlockSpec(memory_space=pltpu.VMEM)
SMEM = pl.BlockSpec(memory_space=pltpu.SMEM)

BLOCKS, CELL_BLOCK, SUM, ENDS, ORDER_SIZE = 0, 384, 640, 896, 1024
COUNT_BITS = 10


def transposed_dot(a, b):
    return lax.dot_general(
        a, b, (((1,), (1,)), ((), ())), preferred_element_type=jnp.float32
    )


def iota(shape, axis):
    return lax.broadcasted_iota(jnp.int32, shape, axis)


def count(mask, axis):
    return jnp.sum(mask.astype(jnp.float32), axis=axis, keepdims=True).astype(jnp.int32)


def picked(mask, values, axis):
    kept = jnp.where(mask, values, 0).astype(jnp.float32)
    return jnp.sum(kept, axis=axis, keepdims=True).astype(jnp.int32)


def as_column(row):
    n = row.shape[1]
    return picked(iota((n, n), 0) == iota((n, n), 1), row, 1)


OPS = 16


def other_core(x):
    return lax.ppermute(x, "ops", [(i, i ^ 1) for i in range(OPS)])


def between_chips(x):
    same_core = [list(range(core, OPS, 2)) for core in range(2)]
    return lax.all_to_all(x, "ops", 0, 0, axis_index_groups=same_core, tiled=True)


def place(sector, me):
    return ((sector ^ me) & 1) * (OPS // 2) + (sector >> 1)


def order_kernel(nops, coup_ref, out_ref):
    slots = coup_ref.shape[1]
    cells = OPS * nops
    me = lax.axis_index("ops").astype(jnp.int32)

    g = coup_ref[0:1, :]
    alive = iota((1, slots), 1) < coup_ref[3:4, :]
    cell = jnp.where(alive, place(coup_ref[2:3, :], me) * nops + g, cells)
    block = place(coup_ref[1:2, :], me) * nops + g
    cell_col = as_column(cell)
    block_col = as_column(block)
    square = (slots, slots)
    ahead = (cell < cell_col) | ((cell == cell_col) & (iota(square, 1) < iota(square, 0)))
    spot_col = count(ahead, 1)
    out_ref[:, BLOCKS : BLOCKS + slots] = picked(spot_col == iota(square, 1), block_col, 0)

    lane = iota((1, cells), 1)
    first = count(cell_col < lane, 0)
    here = cell_col == lane
    number = count(here, 0)
    only = picked(here, block_col, 0)
    few = (number <= 4).astype(jnp.int32) + (number <= 2).astype(jnp.int32)
    kind = jnp.where(number < 2, 6, few + jnp.where(lane < cells // 2, 3, 0))
    square = (cells, cells)
    kind_col = as_column(kind)
    ahead = (kind_col < kind) | ((kind_col == kind) & (iota(square, 0) < iota(square, 1)))
    spot = count(ahead, 0)
    cell_block = jnp.where(number == 0, cells, jnp.where(number == 1, only, cells + 1 + spot))
    chosen = as_column(spot) == iota(square, 1)
    out_ref[:, CELL_BLOCK : CELL_BLOCK + cells] = cell_block
    firsts = picked(chosen, as_column(first), 0)
    out_ref[:, SUM : SUM + cells] = (firsts << COUNT_BITS) + picked(chosen, as_column(number), 0)
    small = iota((1, 128), 1)
    ends = jnp.zeros((1, 128), jnp.int32)
    for k in range(6):
        ends = jnp.where(small == k, count(kind <= k, 1), ends)
    out_ref[:, ENDS : ENDS + 128] = ends


def params(limit):
    return pltpu.CompilerParams(vmem_limit_bytes=limit * 1024 * 1024)


def cost(flops):
    return pl.CostEstimate(flops=flops, bytes_accessed=1 << 20, transcendentals=0)


def order_slots(nops, couplings, live):
    slots = couplings.shape[1]
    rows = jnp.concatenate([couplings, jnp.broadcast_to(live[None], (1, slots))], axis=0)
    return pl.pallas_call(
        lambda *refs: order_kernel(nops, *refs),
        out_shape=jax.ShapeDtypeStruct((1, ORDER_SIZE), jnp.int32),
        in_specs=[VMEM],
        out_specs=VMEM,
        compiler_params=params(16),
        cost_estimate=cost(20 * slots * slots),
        name="order",
    )(rows)


def hold_kernel(left_ref, right_ref, left_out, turned_ref):
    nops, m, _ = right_ref.shape
    left_out[...] = left_ref[...]
    for g in range(nops):
        turned_ref[g * m : (g + 1) * m] = right_ref[g].T


def hold(left_ops, right_ops):
    nops, m, _ = right_ops.shape
    return pl.pallas_call(
        hold_kernel,
        out_shape=[
            jax.ShapeDtypeStruct(left_ops.shape, left_ops.dtype),
            jax.ShapeDtypeStruct((nops * m, m), right_ops.dtype),
        ],
        in_specs=[VMEM] * 2,
        out_specs=[VMEM] * 2,
        compiler_params=params(4),
        cost_estimate=cost(0),
        name="hold",
    )(left_ops, right_ops)


def add_up(order, block_ref, cells, begin, ends):
    many, some, two = ends
    m = block_ref.shape[1]

    def cell(k):
        packed = order(SUM + k)
        return packed >> COUNT_BITS, packed & ((1 << COUNT_BITS) - 1)

    @pl.loop(begin, many)
    def _(k):
        first, number = cell(k)

        def add(j, total):
            return total + block_ref[order(BLOCKS + first + j)].astype(jnp.float32)

        total = lax.fori_loop(0, number, add, jnp.zeros((m, m), jnp.float32))
        block_ref[cells + 1 + k] = total.astype(jnp.bfloat16)

    @pl.loop(many, some)
    def _(k):
        first, number = cell(k)
        fourth = jnp.where(number == 4, order(BLOCKS + first + 3), cells)
        total = block_ref[order(BLOCKS + first)].astype(jnp.float32)
        total += block_ref[order(BLOCKS + first + 1)].astype(jnp.float32)
        total += block_ref[order(BLOCKS + first + 2)].astype(jnp.float32)
        total += block_ref[fourth].astype(jnp.float32)
        block_ref[cells + 1 + k] = total.astype(jnp.bfloat16)

    @pl.loop(some, two, step=2)
    def _(k):
        ks = (k, jnp.minimum(k + 1, two - 1))
        firsts = [cell(k)[0] for k in ks]
        totals = [
            block_ref[order(BLOCKS + first)] + block_ref[order(BLOCKS + first + 1)]
            for first in firsts
        ]
        for k, total in zip(ks, totals):
            block_ref[cells + 1 + k] = total


def multiply(order, block_ref, turned_ref, out_ref, offset, nops):
    half, m, _ = out_ref.shape
    for t in range(0, half, 2):
        rows = [
            jnp.concatenate(
                [
                    block_ref[order(CELL_BLOCK + (offset + t + i) * nops + g)]
                    for g in range(nops)
                ],
                axis=1,
            )
            for i in range(2)
        ]
        out = jnp.dot(
            jnp.concatenate(rows, axis=0), turned_ref[...], preferred_element_type=jnp.float32
        )
        out_ref[t : t + 2] = out.reshape(2, m, m)


def fill(psi_ref, left_ref, block_ref, offset):
    nops, m, _ = left_ref.shape
    step = 4
    for s in range(0, psi_ref.shape[0], 2):
        pair = jnp.concatenate([psi_ref[s], psi_ref[s + 1]], axis=1)
        for g in range(0, nops, step):
            rows = left_ref[g : g + step].reshape(step * m, m)
            both = jnp.dot(rows, pair, preferred_element_type=jnp.float32).astype(jnp.bfloat16)
            at = (offset + s) * nops + g
            block_ref[at : at + step] = both[:, :m].reshape(step, m, m)
            block_ref[at + nops : at + nops + step] = both[:, m:].reshape(step, m, m)


def early_kernel(psi_ref, left_ref, block_ref):
    nops, m, _ = left_ref.shape
    fill(psi_ref, left_ref, block_ref, 0)
    block_ref[OPS * nops] = jnp.zeros((m, m), jnp.bfloat16)


def early(psi, left, slots):
    nops, m, _ = left.shape
    cells = OPS * nops
    return pl.pallas_call(
        early_kernel,
        out_shape=jax.ShapeDtypeStruct((cells + 1 + slots // 2, m, m), jnp.bfloat16),
        in_specs=[VMEM] * 2,
        out_specs=VMEM,
        compiler_params=params(24),
        cost_estimate=cost(2 * psi.shape[0] * nops * m**3),
        name="early",
    )(psi, left)


def terms(order, turned, blocks, group, offset, number, psi=None, left=None):
    m = blocks.shape[1]
    nops = turned.shape[0] // m
    cells = OPS * nops
    extra = [] if psi is None else [psi, left]

    def kernel(order_in, turned_ref, *refs):
        block_ref, out_ref, order_ref, sem = refs[-4:]
        copy = pltpu.make_async_copy(order_in, order_ref, sem)
        copy.start()
        if extra:
            fill(refs[0], refs[1], block_ref, OPS // 2)
        copy.wait()

        def order(i):
            return order_ref[0, i]

        begin = order(ENDS + 3 * group - 1) if group else 0
        ends = [order(ENDS + 3 * group + k) for k in range(3)]
        add_up(order, block_ref, cells, begin, ends)
        multiply(order, block_ref, turned_ref, out_ref, offset, nops)

    return pl.pallas_call(
        kernel,
        out_shape=[
            jax.ShapeDtypeStruct(blocks.shape, blocks.dtype),
            jax.ShapeDtypeStruct((number, m, m), jnp.float32),
        ],
        in_specs=[VMEM] * (3 + len(extra)),
        out_specs=[VMEM] * 2,
        scratch_shapes=[pltpu.SMEM(order.shape, jnp.int32), pltpu.SemaphoreType.DMA],
        input_output_aliases={2 + len(extra): 0},
        compiler_params=params(24),
        cost_estimate=cost(2 * (number + len(extra) * 4) * nops * m**3),
        name=f"terms_{group}",
    )(order, turned, *extra, blocks)


def slot_kernel(live_ref, coup_ref, psi_ref, left_ref, right_ref, out_ref):
    out_ref[...] = jnp.zeros_like(out_ref)

    @pl.loop(0, live_ref[0])
    def _(c):
        g = coup_ref[0, c]
        half = jnp.dot(left_ref[g], psi_ref[coup_ref[1, c]], preferred_element_type=jnp.float32)
        out_ref[coup_ref[2, c]] += transposed_dot(half.astype(jnp.bfloat16), right_ref[g])


def by_slot(whole, left_ops, right_ops, couplings, live):
    return pl.pallas_call(
        slot_kernel,
        out_shape=jax.ShapeDtypeStruct(whole.shape, jnp.float32),
        in_specs=[SMEM] * 2 + [VMEM] * 3,
        out_specs=VMEM,
        compiler_params=pltpu.CompilerParams(vmem_limit_bytes=60 * 1024 * 1024),
        name="slots",
    )(live, couplings, whole, left_ops, right_ops)


def shards_small(psi, left_ops, right_ops, couplings, live):
    nops, m, _ = left_ops.shape
    order = order_slots(nops, couplings, live)
    left, turned = hold(left_ops, right_ops)
    near = between_chips(jnp.broadcast_to(psi, (OPS // 2, m, m)))
    near, order, left, turned = lax.optimization_barrier((near, order, left, turned))
    far = other_core(near)
    blocks = early(near, left, couplings.shape[1])
    blocks, send = terms(order, turned, blocks, 0, OPS // 2, OPS // 2, far, left)
    came = other_core(send)
    _, keep = terms(order, turned, blocks, 1, 0, OPS // 2)
    parts = between_chips((keep + came).astype(jnp.bfloat16))
    return jnp.sum(parts.astype(jnp.float32), axis=0, keepdims=True)


def shards_large(psi, left_ops, right_ops, couplings, live):
    whole = lax.all_gather(psi, "ops", axis=0, tiled=True)
    total = by_slot(whole, left_ops, right_ops, couplings, live)
    return lax.psum_scatter(total, "ops", scatter_dimension=0, tiled=True)


def solution(mesh):
    ops = mesh.shape["ops"]
    placed = (
        P(("groups", "ops"), None, None),
        P(("groups", "ops"), None, None),
        P(("groups", "ops"), None, None),
        P(None, ("groups", "ops")),
        P(("groups", "ops")),
    )

    def shards(psi, *rest):
        if ops == OPS and psi.shape[0] == 1 and rest[0].shape[0] == 16 and rest[2].shape[1] == 384:
            return shards_small(psi, *rest)
        return shards_large(psi, *rest)

    return jax.shard_map(
        shards,
        mesh=mesh,
        in_specs=placed,
        out_specs=P(("groups", "ops"), None, None),
        check_vma=False,
    )
```

```python
import jax
import jax.numpy as jnp
from jax import lax
from jax.experimental import pallas as pl
from jax.experimental.pallas import tpu as pltpu
from jax.sharding import PartitionSpec as P

VMEM = pl.BlockSpec(memory_space=pltpu.VMEM)
SMEM = pl.BlockSpec(memory_space=pltpu.SMEM)

BLOCKS, CELL_BLOCK, SUM, ENDS, ORDER_SIZE = 0, 384, 640, 896, 1024
COUNT_BITS = 10


def transposed_dot(a, b):
    return lax.dot_general(
        a, b, (((1,), (1,)), ((), ())), preferred_element_type=jnp.float32
    )


def iota(shape, axis):
    return lax.broadcasted_iota(jnp.int32, shape, axis)


def count(mask, axis):
    return jnp.sum(mask.astype(jnp.float32), axis=axis, keepdims=True).astype(jnp.int32)


def picked(mask, values, axis):
    kept = jnp.where(mask, values, 0).astype(jnp.float32)
    return jnp.sum(kept, axis=axis, keepdims=True).astype(jnp.int32)


def as_column(row):
    n = row.shape[1]
    return picked(iota((n, n), 0) == iota((n, n), 1), row, 1)


CHAINS = ((3, 2, 1), (1, 3, 2))
OPS = 16


def partners(step):
    return [(i, i ^ (1 << CHAINS[i & 1][step])) for i in range(OPS)]


def other_core(x):
    return lax.ppermute(x, "ops", [(i, i ^ 1) for i in range(OPS)])


def place(sector, me):
    near = sector ^ me
    spots = [
        sum(((near >> bit) & 1) << step for step, bit in enumerate(chain)) for chain in CHAINS
    ]
    return (near & 1) * (OPS // 2) + jnp.where(sector & 1 == 0, spots[0], spots[1])


def order_kernel(nops, coup_ref, out_ref):
    slots = coup_ref.shape[1]
    cells = OPS * nops
    me = lax.axis_index("ops").astype(jnp.int32)

    g = coup_ref[0:1, :]
    alive = iota((1, slots), 1) < coup_ref[3:4, :]
    cell = jnp.where(alive, place(coup_ref[2:3, :], me) * nops + g, cells)
    block = place(coup_ref[1:2, :], me) * nops + g
    cell_col = as_column(cell)
    block_col = as_column(block)
    square = (slots, slots)
    ahead = (cell < cell_col) | ((cell == cell_col) & (iota(square, 1) < iota(square, 0)))
    spot_col = count(ahead, 1)
    out_ref[:, BLOCKS : BLOCKS + slots] = picked(spot_col == iota(square, 1), block_col, 0)

    lane = iota((1, cells), 1)
    first = count(cell_col < lane, 0)
    here = cell_col == lane
    number = count(here, 0)
    only = picked(here, block_col, 0)
    few = (number <= 4).astype(jnp.int32) + (number <= 2).astype(jnp.int32)
    group = (lane < cells // 2).astype(jnp.int32) + (lane < cells // 4).astype(jnp.int32)
    kind = jnp.where(number < 2, 9, few + 3 * group)
    square = (cells, cells)
    kind_col = as_column(kind)
    ahead = (kind_col < kind) | ((kind_col == kind) & (iota(square, 0) < iota(square, 1)))
    spot = count(ahead, 0)
    cell_block = jnp.where(number == 0, cells, jnp.where(number == 1, only, cells + 1 + spot))
    chosen = as_column(spot) == iota(square, 1)
    out_ref[:, CELL_BLOCK : CELL_BLOCK + cells] = cell_block
    firsts = picked(chosen, as_column(first), 0)
    out_ref[:, SUM : SUM + cells] = (firsts << COUNT_BITS) + picked(chosen, as_column(number), 0)
    small = iota((1, 128), 1)
    ends = jnp.zeros((1, 128), jnp.int32)
    for k in range(9):
        ends = jnp.where(small == k, count(kind <= k, 1), ends)
    out_ref[:, ENDS : ENDS + 128] = ends


def params(limit):
    return pltpu.CompilerParams(vmem_limit_bytes=limit * 1024 * 1024)


def cost(flops):
    return pl.CostEstimate(flops=flops, bytes_accessed=1 << 20, transcendentals=0)


def order_slots(nops, couplings, live):
    slots = couplings.shape[1]
    rows = jnp.concatenate([couplings, jnp.broadcast_to(live[None], (1, slots))], axis=0)
    return pl.pallas_call(
        lambda *refs: order_kernel(nops, *refs),
        out_shape=jax.ShapeDtypeStruct((1, ORDER_SIZE), jnp.int32),
        in_specs=[VMEM],
        out_specs=VMEM,
        compiler_params=params(16),
        cost_estimate=cost(20 * slots * slots),
        name="order",
    )(rows)


def hold_kernel(psi_ref, left_ref, psi_out, left_out):
    psi_out[...] = psi_ref[...]
    left_out[...] = left_ref[...]


def hold(psi, left_ops):
    return pl.pallas_call(
        hold_kernel,
        out_shape=[jax.ShapeDtypeStruct(x.shape, x.dtype) for x in (psi, left_ops)],
        in_specs=[VMEM] * 2,
        out_specs=[VMEM] * 2,
        compiler_params=params(4),
        cost_estimate=cost(0),
        name="hold",
    )(psi, left_ops)


def turn_kernel(right_ref, turned_ref):
    nops, m, _ = right_ref.shape
    for g in range(nops):
        turned_ref[g * m : (g + 1) * m] = right_ref[g].T


def turn(right_ops):
    nops, m, _ = right_ops.shape
    return pl.pallas_call(
        turn_kernel,
        out_shape=jax.ShapeDtypeStruct((nops * m, m), jnp.bfloat16),
        in_specs=[VMEM],
        out_specs=VMEM,
        compiler_params=params(4),
        cost_estimate=cost(0),
        name="turn",
    )(right_ops)


def add_up(order, block_ref, cells, begin, ends):
    many, some, two = ends
    m = block_ref.shape[1]

    def cell(k):
        packed = order(SUM + k)
        return packed >> COUNT_BITS, packed & ((1 << COUNT_BITS) - 1)

    @pl.loop(begin, many)
    def _(k):
        first, number = cell(k)

        def add(j, total):
            return total + block_ref[order(BLOCKS + first + j)].astype(jnp.float32)

        total = lax.fori_loop(0, number, add, jnp.zeros((m, m), jnp.float32))
        block_ref[cells + 1 + k] = total.astype(jnp.bfloat16)

    @pl.loop(many, some)
    def _(k):
        first, number = cell(k)
        fourth = jnp.where(number == 4, order(BLOCKS + first + 3), cells)
        total = block_ref[order(BLOCKS + first)].astype(jnp.float32)
        total += block_ref[order(BLOCKS + first + 1)].astype(jnp.float32)
        total += block_ref[order(BLOCKS + first + 2)].astype(jnp.float32)
        total += block_ref[fourth].astype(jnp.float32)
        block_ref[cells + 1 + k] = total.astype(jnp.bfloat16)

    @pl.loop(some, two, step=2)
    def _(k):
        ks = (k, jnp.minimum(k + 1, two - 1))
        firsts = [cell(k)[0] for k in ks]
        totals = [
            block_ref[order(BLOCKS + first)] + block_ref[order(BLOCKS + first + 1)]
            for first in firsts
        ]
        for k, total in zip(ks, totals):
            block_ref[cells + 1 + k] = total


def multiply(order, block_ref, turned_ref, out_ref, offset, nops):
    half, m, _ = out_ref.shape
    for t in range(0, half, 2):
        rows = [
            jnp.concatenate(
                [
                    block_ref[order(CELL_BLOCK + (offset + t + i) * nops + g)]
                    for g in range(nops)
                ],
                axis=1,
            )
            for i in range(2)
        ]
        out = jnp.dot(
            jnp.concatenate(rows, axis=0), turned_ref[...], preferred_element_type=jnp.float32
        )
        out_ref[t : t + 2] = out.reshape(2, m, m)


def fill(psi_ref, left_ref, block_ref, offset):
    nops, m, _ = left_ref.shape
    step = 4
    for s in range(0, psi_ref.shape[0], 2):
        pair = jnp.concatenate([psi_ref[s], psi_ref[s + 1]], axis=1)
        for g in range(0, nops, step):
            rows = left_ref[g : g + step].reshape(step * m, m)
            both = jnp.dot(rows, pair, preferred_element_type=jnp.float32).astype(jnp.bfloat16)
            at = (offset + s) * nops + g
            block_ref[at : at + step] = both[:, :m].reshape(step, m, m)
            block_ref[at + nops : at + nops + step] = both[:, m:].reshape(step, m, m)


def early_kernel(psi_ref, left_ref, block_ref):
    nops, m, _ = left_ref.shape
    fill(psi_ref, left_ref, block_ref, 0)
    block_ref[OPS * nops] = jnp.zeros((m, m), jnp.bfloat16)


def early(psi, left, slots):
    nops, m, _ = left.shape
    cells = OPS * nops
    return pl.pallas_call(
        early_kernel,
        out_shape=jax.ShapeDtypeStruct((cells + 1 + slots // 2, m, m), jnp.bfloat16),
        in_specs=[VMEM] * 2,
        out_specs=VMEM,
        compiler_params=params(24),
        cost_estimate=cost(2 * psi.shape[0] * nops * m**3),
        name="early",
    )(psi, left)


def more(psi, left, blocks, offset):
    nops, m, _ = left.shape

    def kernel(psi_ref, left_ref, _, block_ref):
        fill(psi_ref, left_ref, block_ref, offset)

    return pl.pallas_call(
        kernel,
        out_shape=jax.ShapeDtypeStruct(blocks.shape, blocks.dtype),
        in_specs=[VMEM] * 3,
        out_specs=VMEM,
        input_output_aliases={2: 0},
        compiler_params=params(24),
        cost_estimate=cost(2 * psi.shape[0] * nops * m**3),
        name="more",
    )(psi, left, blocks)


def terms(order, turned, blocks, group, offset, number, psi=None, left=None):
    m = blocks.shape[1]
    nops = turned.shape[0] // m
    cells = OPS * nops
    extra = [] if psi is None else [psi, left]

    def kernel(order_in, turned_ref, *refs):
        block_ref, out_ref, order_ref, sem = refs[-4:]
        copy = pltpu.make_async_copy(order_in, order_ref, sem)
        copy.start()
        if extra:
            fill(refs[0], refs[1], block_ref, OPS // 2)
        copy.wait()

        def order(i):
            return order_ref[0, i]

        begin = order(ENDS + 3 * group - 1) if group else 0
        ends = [order(ENDS + 3 * group + k) for k in range(3)]
        add_up(order, block_ref, cells, begin, ends)
        multiply(order, block_ref, turned_ref, out_ref, offset, nops)

    return pl.pallas_call(
        kernel,
        out_shape=[
            jax.ShapeDtypeStruct(blocks.shape, blocks.dtype),
            jax.ShapeDtypeStruct((number, m, m), jnp.float32),
        ],
        in_specs=[VMEM] * (3 + len(extra)),
        out_specs=[VMEM] * 2,
        scratch_shapes=[pltpu.SMEM(order.shape, jnp.int32), pltpu.SemaphoreType.DMA],
        input_output_aliases={2 + len(extra): 0},
        compiler_params=params(24),
        cost_estimate=cost(2 * (number + len(extra) * 4) * nops * m**3),
        name=f"terms_{group}",
    )(order, turned, *extra, blocks)


def slot_kernel(live_ref, coup_ref, psi_ref, left_ref, right_ref, out_ref):
    out_ref[...] = jnp.zeros_like(out_ref)

    @pl.loop(0, live_ref[0])
    def _(c):
        g = coup_ref[0, c]
        half = jnp.dot(left_ref[g], psi_ref[coup_ref[1, c]], preferred_element_type=jnp.float32)
        out_ref[coup_ref[2, c]] += transposed_dot(half.astype(jnp.bfloat16), right_ref[g])


def by_slot(whole, left_ops, right_ops, couplings, live):
    return pl.pallas_call(
        slot_kernel,
        out_shape=jax.ShapeDtypeStruct(whole.shape, jnp.float32),
        in_specs=[SMEM] * 2 + [VMEM] * 3,
        out_specs=VMEM,
        compiler_params=pltpu.CompilerParams(vmem_limit_bytes=60 * 1024 * 1024),
        name="slots",
    )(live, couplings, whole, left_ops, right_ops)


def shards_small(psi, left_ops, right_ops, couplings, live):
    slots = couplings.shape[1]
    came = lax.ppermute(psi, "ops", partners(0))
    psi, left = hold(psi, left_ops)
    two, left = lax.optimization_barrier((jnp.concatenate([psi, came], axis=0), left))
    came = lax.ppermute(two, "ops", partners(1))
    order = order_slots(left_ops.shape[0], couplings, live)
    four, order = lax.optimization_barrier((jnp.concatenate([two, came], axis=0), order))
    came = lax.ppermute(four, "ops", partners(2))
    blocks = early(four, left, slots)
    turned = turn(right_ops)
    eight, turned, blocks = lax.optimization_barrier(
        (jnp.concatenate([four, came], axis=0), turned, blocks)
    )
    far = other_core(eight)
    blocks = more(came, left, blocks, 4)
    blocks, send = terms(order, turned, blocks, 0, 8, 8, far, left)
    came = other_core(send)
    blocks, next_four = terms(order, turned, blocks, 1, 4, 4)
    leaving = (next_four + came[4:]).astype(jnp.bfloat16)
    arrived = lax.ppermute(leaving, "ops", partners(2))
    _, last_four = terms(order, turned, blocks, 2, 0, 4)
    keep = last_four + came[:4]
    for step in (1, 0):
        half = keep.shape[0] // 2
        both = keep + arrived.astype(jnp.float32)
        keep, leaving = both[:half], both[half:].astype(jnp.bfloat16)
        arrived = lax.ppermute(leaving, "ops", partners(step))
    return keep + arrived.astype(jnp.float32)


def shards_large(psi, left_ops, right_ops, couplings, live):
    whole = lax.all_gather(psi, "ops", axis=0, tiled=True)
    total = by_slot(whole, left_ops, right_ops, couplings, live)
    return lax.psum_scatter(total, "ops", scatter_dimension=0, tiled=True)


def solution(mesh):
    ops = mesh.shape["ops"]
    placed = (
        P(("groups", "ops"), None, None),
        P(("groups", "ops"), None, None),
        P(("groups", "ops"), None, None),
        P(None, ("groups", "ops")),
        P(("groups", "ops")),
    )

    def shards(psi, *rest):
        if ops == OPS and psi.shape[0] == 1 and rest[0].shape[0] == 16 and rest[2].shape[1] == 384:
            return shards_small(psi, *rest)
        return shards_large(psi, *rest)

    return jax.shard_map(
        shards,
        mesh=mesh,
        in_specs=placed,
        out_specs=P(("groups", "ops"), None, None),
        check_vma=False,
    )
```

```python
import jax
import jax.numpy as jnp
from jax import lax
from jax.experimental import pallas as pl
from jax.experimental.pallas import tpu as pltpu
from jax.sharding import PartitionSpec as P

VMEM = pl.BlockSpec(memory_space=pltpu.VMEM)
SMEM = pl.BlockSpec(memory_space=pltpu.SMEM)

BLOCKS, CELL_BLOCK, SUM, ENDS, ORDER_SIZE = 0, 384, 640, 896, 1024
COUNT_BITS = 10


def transposed_dot(a, b):
    return lax.dot_general(
        a, b, (((1,), (1,)), ((), ())), preferred_element_type=jnp.float32
    )


def iota(shape, axis):
    return lax.broadcasted_iota(jnp.int32, shape, axis)


def count(mask, axis):
    return jnp.sum(mask.astype(jnp.float32), axis=axis, keepdims=True).astype(jnp.int32)


def picked(mask, values, axis):
    kept = jnp.where(mask, values, 0).astype(jnp.float32)
    return jnp.sum(kept, axis=axis, keepdims=True).astype(jnp.int32)


def as_column(row):
    n = row.shape[1]
    return picked(iota((n, n), 0) == iota((n, n), 1), row, 1)


CHAIN = (3, 2, 1)
OPS = 16


def between_chips(x, step):
    return lax.ppermute(x, "ops", [(i, i ^ (1 << CHAIN[step])) for i in range(1, OPS, 2)])


def to_core(core, x):
    return lax.ppermute(x, "ops", [(i ^ 1, i) for i in range(core, OPS, 2)])


def place(sector, me):
    near = sector ^ me
    spot = sum(((near >> bit) & 1) << step for step, bit in enumerate(CHAIN))
    return spot * 2 + (sector & 1)


def order_kernel(nops, coup_ref, out_ref):
    slots = coup_ref.shape[1]
    cells = OPS * nops
    me = lax.axis_index("ops").astype(jnp.int32)

    g = coup_ref[0:1, :]
    alive = iota((1, slots), 1) < coup_ref[3:4, :]
    cell = jnp.where(alive, place(coup_ref[2:3, :], me) * nops + g, cells)
    block = place(coup_ref[1:2, :], me) * nops + g
    cell_col = as_column(cell)
    block_col = as_column(block)
    square = (slots, slots)
    ahead = (cell < cell_col) | ((cell == cell_col) & (iota(square, 1) < iota(square, 0)))
    spot_col = count(ahead, 1)
    out_ref[:, BLOCKS : BLOCKS + slots] = picked(spot_col == iota(square, 1), block_col, 0)

    lane = iota((1, cells), 1)
    first = count(cell_col < lane, 0)
    here = cell_col == lane
    number = count(here, 0)
    only = picked(here, block_col, 0)
    few = (number <= 4).astype(jnp.int32) + (number <= 2).astype(jnp.int32)
    group = (lane < cells // 2).astype(jnp.int32) + (lane < cells // 4).astype(jnp.int32)
    kind = jnp.where(number < 2, 9, few + 3 * group)
    square = (cells, cells)
    kind_col = as_column(kind)
    ahead = (kind_col < kind) | ((kind_col == kind) & (iota(square, 0) < iota(square, 1)))
    spot = count(ahead, 0)
    cell_block = jnp.where(number == 0, cells, jnp.where(number == 1, only, cells + 1 + spot))
    chosen = as_column(spot) == iota(square, 1)
    out_ref[:, CELL_BLOCK : CELL_BLOCK + cells] = cell_block
    firsts = picked(chosen, as_column(first), 0)
    out_ref[:, SUM : SUM + cells] = (firsts << COUNT_BITS) + picked(chosen, as_column(number), 0)
    small = iota((1, 128), 1)
    ends = jnp.zeros((1, 128), jnp.int32)
    for k in range(9):
        ends = jnp.where(small == k, count(kind <= k, 1), ends)
    out_ref[:, ENDS : ENDS + 128] = ends


def params(limit):
    return pltpu.CompilerParams(vmem_limit_bytes=limit * 1024 * 1024)


def cost(flops):
    return pl.CostEstimate(flops=flops, bytes_accessed=1 << 20, transcendentals=0)


def order_slots(nops, couplings, live):
    slots = couplings.shape[1]
    rows = jnp.concatenate([couplings, jnp.broadcast_to(live[None], (1, slots))], axis=0)
    return pl.pallas_call(
        lambda *refs: order_kernel(nops, *refs),
        out_shape=jax.ShapeDtypeStruct((1, ORDER_SIZE), jnp.int32),
        in_specs=[VMEM],
        out_specs=VMEM,
        compiler_params=params(16),
        cost_estimate=cost(20 * slots * slots),
        name="order",
    )(rows)


def hold_kernel(in_ref, out_ref):
    out_ref[...] = in_ref[...]


def hold(x):
    return pl.pallas_call(
        hold_kernel,
        out_shape=jax.ShapeDtypeStruct(x.shape, x.dtype),
        in_specs=[VMEM],
        out_specs=VMEM,
        compiler_params=params(4),
        cost_estimate=cost(0),
        name="hold",
    )(x)


def turn_kernel(right_ref, turned_ref):
    nops, m, _ = right_ref.shape
    for g in range(nops):
        turned_ref[g * m : (g + 1) * m] = right_ref[g].T


def turn(right_ops):
    nops, m, _ = right_ops.shape
    return pl.pallas_call(
        turn_kernel,
        out_shape=jax.ShapeDtypeStruct((nops * m, m), jnp.bfloat16),
        in_specs=[VMEM],
        out_specs=VMEM,
        compiler_params=params(4),
        cost_estimate=cost(0),
        name="turn",
    )(right_ops)


def add_up(order, block_ref, cells, begin, ends):
    many, some, two = ends
    m = block_ref.shape[1]

    def cell(k):
        packed = order(SUM + k)
        return packed >> COUNT_BITS, packed & ((1 << COUNT_BITS) - 1)

    @pl.loop(begin, many)
    def _(k):
        first, number = cell(k)

        def add(j, total):
            return total + block_ref[order(BLOCKS + first + j)].astype(jnp.float32)

        total = lax.fori_loop(0, number, add, jnp.zeros((m, m), jnp.float32))
        block_ref[cells + 1 + k] = total.astype(jnp.bfloat16)

    @pl.loop(many, some)
    def _(k):
        first, number = cell(k)
        fourth = jnp.where(number == 4, order(BLOCKS + first + 3), cells)
        total = block_ref[order(BLOCKS + first)].astype(jnp.float32)
        total += block_ref[order(BLOCKS + first + 1)].astype(jnp.float32)
        total += block_ref[order(BLOCKS + first + 2)].astype(jnp.float32)
        total += block_ref[fourth].astype(jnp.float32)
        block_ref[cells + 1 + k] = total.astype(jnp.bfloat16)

    @pl.loop(some, two, step=2)
    def _(k):
        ks = (k, jnp.minimum(k + 1, two - 1))
        firsts = [cell(k)[0] for k in ks]
        totals = [
            block_ref[order(BLOCKS + first)] + block_ref[order(BLOCKS + first + 1)]
            for first in firsts
        ]
        for k, total in zip(ks, totals):
            block_ref[cells + 1 + k] = total


def multiply(order, block_ref, turned_ref, out_ref, offset, nops):
    half, m, _ = out_ref.shape
    for t in range(0, half, 2):
        rows = [
            jnp.concatenate(
                [
                    block_ref[order(CELL_BLOCK + (offset + t + i) * nops + g)]
                    for g in range(nops)
                ],
                axis=1,
            )
            for i in range(2)
        ]
        out = jnp.dot(
            jnp.concatenate(rows, axis=0), turned_ref[...], preferred_element_type=jnp.float32
        )
        out_ref[t : t + 2] = out.reshape(2, m, m)


def fill(psi_ref, left_ref, block_ref, offset):
    nops, m, _ = left_ref.shape
    step = 4
    for s in range(0, psi_ref.shape[0], 2):
        pair = jnp.concatenate([psi_ref[s], psi_ref[s + 1]], axis=1)
        for g in range(0, nops, step):
            rows = left_ref[g : g + step].reshape(step * m, m)
            both = jnp.dot(rows, pair, preferred_element_type=jnp.float32).astype(jnp.bfloat16)
            at = (offset + s) * nops + g
            block_ref[at : at + step] = both[:, :m].reshape(step, m, m)
            block_ref[at + nops : at + nops + step] = both[:, m:].reshape(step, m, m)


def early_kernel(psi_ref, left_ref, block_ref):
    nops, m, _ = left_ref.shape
    fill(psi_ref, left_ref, block_ref, 0)
    block_ref[OPS * nops] = jnp.zeros((m, m), jnp.bfloat16)


def early(psi, left, slots):
    nops, m, _ = left.shape
    cells = OPS * nops
    return pl.pallas_call(
        early_kernel,
        out_shape=jax.ShapeDtypeStruct((cells + 1 + slots // 2, m, m), jnp.bfloat16),
        in_specs=[VMEM] * 2,
        out_specs=VMEM,
        compiler_params=params(24),
        cost_estimate=cost(2 * psi.shape[0] * nops * m**3),
        name="early",
    )(psi, left)


def more(psi, left, blocks, offset):
    nops, m, _ = left.shape

    def kernel(psi_ref, left_ref, _, block_ref):
        fill(psi_ref, left_ref, block_ref, offset)

    return pl.pallas_call(
        kernel,
        out_shape=jax.ShapeDtypeStruct(blocks.shape, blocks.dtype),
        in_specs=[VMEM] * 3,
        out_specs=VMEM,
        input_output_aliases={2: 0},
        compiler_params=params(24),
        cost_estimate=cost(2 * psi.shape[0] * nops * m**3),
        name="more",
    )(psi, left, blocks)


def terms(order, turned, blocks, group, offset, number, psi=None, left=None):
    m = blocks.shape[1]
    nops = turned.shape[0] // m
    cells = OPS * nops
    extra = [] if psi is None else [psi, left]

    def kernel(order_in, turned_ref, *refs):
        block_ref, out_ref, order_ref, sem = refs[-4:]
        copy = pltpu.make_async_copy(order_in, order_ref, sem)
        copy.start()
        if extra:
            fill(refs[0], refs[1], block_ref, OPS // 2)
        copy.wait()

        def order(i):
            return order_ref[0, i]

        begin = order(ENDS + 3 * group - 1) if group else 0
        ends = [order(ENDS + 3 * group + k) for k in range(3)]
        add_up(order, block_ref, cells, begin, ends)
        multiply(order, block_ref, turned_ref, out_ref, offset, nops)

    return pl.pallas_call(
        kernel,
        out_shape=[
            jax.ShapeDtypeStruct(blocks.shape, blocks.dtype),
            jax.ShapeDtypeStruct((number, m, m), jnp.float32),
        ],
        in_specs=[VMEM] * (3 + len(extra)),
        out_specs=[VMEM] * 2,
        scratch_shapes=[pltpu.SMEM(order.shape, jnp.int32), pltpu.SemaphoreType.DMA],
        input_output_aliases={2 + len(extra): 0},
        compiler_params=params(24),
        cost_estimate=cost(2 * (number + len(extra) * 4) * nops * m**3),
        name=f"terms_{group}",
    )(order, turned, *extra, blocks)


def slot_kernel(live_ref, coup_ref, psi_ref, left_ref, right_ref, out_ref):
    out_ref[...] = jnp.zeros_like(out_ref)

    @pl.loop(0, live_ref[0])
    def _(c):
        g = coup_ref[0, c]
        half = jnp.dot(left_ref[g], psi_ref[coup_ref[1, c]], preferred_element_type=jnp.float32)
        out_ref[coup_ref[2, c]] += transposed_dot(half.astype(jnp.bfloat16), right_ref[g])


def by_slot(whole, left_ops, right_ops, couplings, live):
    return pl.pallas_call(
        slot_kernel,
        out_shape=jax.ShapeDtypeStruct(whole.shape, jnp.float32),
        in_specs=[SMEM] * 2 + [VMEM] * 3,
        out_specs=VMEM,
        compiler_params=pltpu.CompilerParams(vmem_limit_bytes=60 * 1024 * 1024),
        name="slots",
    )(live, couplings, whole, left_ops, right_ops)


def shards_small(psi, left_ops, right_ops, couplings, live):
    slots = couplings.shape[1]
    first_core = lax.axis_index("ops") & 1 == 0

    def shared(x):
        return jnp.where(first_core, to_core(0, x), x)

    came = lax.ppermute(psi, "ops", [(i, i ^ 1) for i in range(OPS)])
    psi = hold(psi)
    two = jnp.concatenate(
        [jnp.where(first_core, psi, came), jnp.where(first_core, came, psi)], axis=0
    )
    came_two = between_chips(two, 0)
    left = hold(left_ops)
    four, left = lax.optimization_barrier((jnp.concatenate([two, came_two], axis=0), left))
    came_four = between_chips(four, 1)
    order = order_slots(left_ops.shape[0], couplings, live)
    eight, order = lax.optimization_barrier((jnp.concatenate([four, came_four], axis=0), order))
    came_eight = between_chips(eight, 2)
    blocks = early(jnp.concatenate([two, shared(came_two)], axis=0), left, slots)
    blocks = more(shared(came_four), left, blocks, 4)
    turned = turn(right_ops)
    came_eight, turned, blocks = lax.optimization_barrier((came_eight, turned, blocks))
    blocks, leaving = terms(order, turned, blocks, 0, 8, 8, shared(came_eight), left)
    others = to_core(1, leaving)
    blocks, next_four = terms(order, turned, blocks, 1, 4, 4)
    arrived = between_chips((leaving + others).astype(jnp.bfloat16), 2)
    _, last_four = terms(order, turned, blocks, 2, 0, 4)
    keep = jnp.concatenate([last_four, next_four], axis=0)
    keep = keep + to_core(1, keep)
    for step in (1, 0):
        half = keep.shape[0] // 2
        both = keep + arrived.astype(jnp.float32)
        keep = both[:half]
        arrived = between_chips(both[half:].astype(jnp.bfloat16), step)
    both = keep + arrived.astype(jnp.float32)
    return jnp.where(first_core, to_core(0, both[:1]), both[1:])


def shards_large(psi, left_ops, right_ops, couplings, live):
    whole = lax.all_gather(psi, "ops", axis=0, tiled=True)
    total = by_slot(whole, left_ops, right_ops, couplings, live)
    return lax.psum_scatter(total, "ops", scatter_dimension=0, tiled=True)


def solution(mesh):
    ops = mesh.shape["ops"]
    placed = (
        P(("groups", "ops"), None, None),
        P(("groups", "ops"), None, None),
        P(("groups", "ops"), None, None),
        P(None, ("groups", "ops")),
        P(("groups", "ops")),
    )

    def shards(psi, *rest):
        if ops == OPS and psi.shape[0] == 1 and rest[0].shape[0] == 16 and rest[2].shape[1] == 384:
            return shards_small(psi, *rest)
        return shards_large(psi, *rest)

    return jax.shard_map(
        shards,
        mesh=mesh,
        in_specs=placed,
        out_specs=P(("groups", "ops"), None, None),
        check_vma=False,
    )
```

```python
import jax
import jax.numpy as jnp
from jax import lax
from jax.experimental import pallas as pl
from jax.experimental.pallas import tpu as pltpu
from jax.sharding import PartitionSpec as P

VMEM = pl.BlockSpec(memory_space=pltpu.VMEM)
SMEM = pl.BlockSpec(memory_space=pltpu.SMEM)

BLOCKS, CELL_BLOCK, SUM, ENDS, ORDER_SIZE = 0, 384, 640, 896, 1024
COUNT_BITS = 10


def transposed_dot(a, b):
    return lax.dot_general(
        a, b, (((1,), (1,)), ((), ())), preferred_element_type=jnp.float32
    )


def iota(shape, axis):
    return lax.broadcasted_iota(jnp.int32, shape, axis)


def count(mask, axis):
    return jnp.sum(mask.astype(jnp.float32), axis=axis, keepdims=True).astype(jnp.int32)


def picked(mask, values, axis):
    kept = jnp.where(mask, values, 0).astype(jnp.float32)
    return jnp.sum(kept, axis=axis, keepdims=True).astype(jnp.int32)


def as_column(row):
    n = row.shape[1]
    return picked(iota((n, n), 0) == iota((n, n), 1), row, 1)


CHAIN = (3, 2, 1)
OPS = 16


def between_chips(x, step):
    return lax.ppermute(x, "ops", [(i, i ^ ((i & 1) << CHAIN[step])) for i in range(OPS)])


def other_core(x):
    return lax.ppermute(x, "ops", [(i, i ^ 1) for i in range(OPS)])


def place(sector, me):
    near = sector ^ me
    spot = sum(((near >> bit) & 1) << step for step, bit in enumerate(CHAIN))
    return spot * 2 + (sector & 1)


def order_kernel(nops, coup_ref, out_ref):
    slots = coup_ref.shape[1]
    cells = OPS * nops
    me = lax.axis_index("ops").astype(jnp.int32)

    g = coup_ref[0:1, :]
    alive = iota((1, slots), 1) < coup_ref[3:4, :]
    cell = jnp.where(alive, place(coup_ref[2:3, :], me) * nops + g, cells)
    block = place(coup_ref[1:2, :], me) * nops + g
    cell_col = as_column(cell)
    block_col = as_column(block)
    square = (slots, slots)
    ahead = (cell < cell_col) | ((cell == cell_col) & (iota(square, 1) < iota(square, 0)))
    spot_col = count(ahead, 1)
    out_ref[:, BLOCKS : BLOCKS + slots] = picked(spot_col == iota(square, 1), block_col, 0)

    lane = iota((1, cells), 1)
    first = count(cell_col < lane, 0)
    here = cell_col == lane
    number = count(here, 0)
    only = picked(here, block_col, 0)
    few = (number <= 4).astype(jnp.int32) + (number <= 2).astype(jnp.int32)
    group = (lane < cells // 2).astype(jnp.int32) + (lane < cells // 4).astype(jnp.int32)
    kind = jnp.where(number < 2, 9, few + 3 * group)
    square = (cells, cells)
    kind_col = as_column(kind)
    ahead = (kind_col < kind) | ((kind_col == kind) & (iota(square, 0) < iota(square, 1)))
    spot = count(ahead, 0)
    cell_block = jnp.where(number == 0, cells, jnp.where(number == 1, only, cells + 1 + spot))
    chosen = as_column(spot) == iota(square, 1)
    out_ref[:, CELL_BLOCK : CELL_BLOCK + cells] = cell_block
    firsts = picked(chosen, as_column(first), 0)
    out_ref[:, SUM : SUM + cells] = (firsts << COUNT_BITS) + picked(chosen, as_column(number), 0)
    small = iota((1, 128), 1)
    ends = jnp.zeros((1, 128), jnp.int32)
    for k in range(9):
        ends = jnp.where(small == k, count(kind <= k, 1), ends)
    out_ref[:, ENDS : ENDS + 128] = ends


def params(limit):
    return pltpu.CompilerParams(vmem_limit_bytes=limit * 1024 * 1024)


def cost(flops):
    return pl.CostEstimate(flops=flops, bytes_accessed=1 << 20, transcendentals=0)


def order_slots(nops, couplings, live):
    slots = couplings.shape[1]
    rows = jnp.concatenate([couplings, jnp.broadcast_to(live[None], (1, slots))], axis=0)
    return pl.pallas_call(
        lambda *refs: order_kernel(nops, *refs),
        out_shape=jax.ShapeDtypeStruct((1, ORDER_SIZE), jnp.int32),
        in_specs=[VMEM],
        out_specs=VMEM,
        compiler_params=params(16),
        cost_estimate=cost(20 * slots * slots),
        name="order",
    )(rows)


def hold_kernel(in_ref, out_ref):
    out_ref[...] = in_ref[...]


def hold(x):
    return pl.pallas_call(
        hold_kernel,
        out_shape=jax.ShapeDtypeStruct(x.shape, x.dtype),
        in_specs=[VMEM],
        out_specs=VMEM,
        compiler_params=params(4),
        cost_estimate=cost(0),
        name="hold",
    )(x)


def turn_kernel(right_ref, turned_ref):
    nops, m, _ = right_ref.shape
    for g in range(nops):
        turned_ref[g * m : (g + 1) * m] = right_ref[g].T


def turn(right_ops):
    nops, m, _ = right_ops.shape
    return pl.pallas_call(
        turn_kernel,
        out_shape=jax.ShapeDtypeStruct((nops * m, m), jnp.bfloat16),
        in_specs=[VMEM],
        out_specs=VMEM,
        compiler_params=params(4),
        cost_estimate=cost(0),
        name="turn",
    )(right_ops)


def add_up(order, block_ref, cells, begin, ends):
    many, some, two = ends
    m = block_ref.shape[1]

    def cell(k):
        packed = order(SUM + k)
        return packed >> COUNT_BITS, packed & ((1 << COUNT_BITS) - 1)

    @pl.loop(begin, many)
    def _(k):
        first, number = cell(k)

        def add(j, total):
            return total + block_ref[order(BLOCKS + first + j)].astype(jnp.float32)

        total = lax.fori_loop(0, number, add, jnp.zeros((m, m), jnp.float32))
        block_ref[cells + 1 + k] = total.astype(jnp.bfloat16)

    @pl.loop(many, some)
    def _(k):
        first, number = cell(k)
        fourth = jnp.where(number == 4, order(BLOCKS + first + 3), cells)
        total = block_ref[order(BLOCKS + first)].astype(jnp.float32)
        total += block_ref[order(BLOCKS + first + 1)].astype(jnp.float32)
        total += block_ref[order(BLOCKS + first + 2)].astype(jnp.float32)
        total += block_ref[fourth].astype(jnp.float32)
        block_ref[cells + 1 + k] = total.astype(jnp.bfloat16)

    @pl.loop(some, two, step=2)
    def _(k):
        ks = (k, jnp.minimum(k + 1, two - 1))
        firsts = [cell(k)[0] for k in ks]
        totals = [
            block_ref[order(BLOCKS + first)] + block_ref[order(BLOCKS + first + 1)]
            for first in firsts
        ]
        for k, total in zip(ks, totals):
            block_ref[cells + 1 + k] = total


def multiply(order, block_ref, turned_ref, out_ref, offset, nops):
    half, m, _ = out_ref.shape
    for t in range(0, half, 2):
        rows = [
            jnp.concatenate(
                [
                    block_ref[order(CELL_BLOCK + (offset + t + i) * nops + g)]
                    for g in range(nops)
                ],
                axis=1,
            )
            for i in range(2)
        ]
        out = jnp.dot(
            jnp.concatenate(rows, axis=0), turned_ref[...], preferred_element_type=jnp.float32
        )
        out_ref[t : t + 2] = out.reshape(2, m, m)


def fill(psi_ref, left_ref, block_ref, offset):
    nops, m, _ = left_ref.shape
    step = 4
    for s in range(0, psi_ref.shape[0], 2):
        pair = jnp.concatenate([psi_ref[s], psi_ref[s + 1]], axis=1)
        for g in range(0, nops, step):
            rows = left_ref[g : g + step].reshape(step * m, m)
            both = jnp.dot(rows, pair, preferred_element_type=jnp.float32).astype(jnp.bfloat16)
            at = (offset + s) * nops + g
            block_ref[at : at + step] = both[:, :m].reshape(step, m, m)
            block_ref[at + nops : at + nops + step] = both[:, m:].reshape(step, m, m)


def early_kernel(psi_ref, left_ref, block_ref):
    nops, m, _ = left_ref.shape
    fill(psi_ref, left_ref, block_ref, 0)
    block_ref[OPS * nops] = jnp.zeros((m, m), jnp.bfloat16)


def early(psi, left, slots):
    nops, m, _ = left.shape
    cells = OPS * nops
    return pl.pallas_call(
        early_kernel,
        out_shape=jax.ShapeDtypeStruct((cells + 1 + slots // 2, m, m), jnp.bfloat16),
        in_specs=[VMEM] * 2,
        out_specs=VMEM,
        compiler_params=params(24),
        cost_estimate=cost(2 * psi.shape[0] * nops * m**3),
        name="early",
    )(psi, left)


def more(psi, left, blocks, offset):
    nops, m, _ = left.shape

    def kernel(psi_ref, left_ref, _, block_ref):
        fill(psi_ref, left_ref, block_ref, offset)

    return pl.pallas_call(
        kernel,
        out_shape=jax.ShapeDtypeStruct(blocks.shape, blocks.dtype),
        in_specs=[VMEM] * 3,
        out_specs=VMEM,
        input_output_aliases={2: 0},
        compiler_params=params(24),
        cost_estimate=cost(2 * psi.shape[0] * nops * m**3),
        name="more",
    )(psi, left, blocks)


def terms(order, turned, blocks, group, offset, number, psi=None, left=None):
    m = blocks.shape[1]
    nops = turned.shape[0] // m
    cells = OPS * nops
    extra = [] if psi is None else [psi, left]

    def kernel(order_in, turned_ref, *refs):
        block_ref, out_ref, order_ref, sem = refs[-4:]
        copy = pltpu.make_async_copy(order_in, order_ref, sem)
        copy.start()
        if extra:
            fill(refs[0], refs[1], block_ref, OPS // 2)
        copy.wait()

        def order(i):
            return order_ref[0, i]

        begin = order(ENDS + 3 * group - 1) if group else 0
        ends = [order(ENDS + 3 * group + k) for k in range(3)]
        add_up(order, block_ref, cells, begin, ends)
        multiply(order, block_ref, turned_ref, out_ref, offset, nops)

    return pl.pallas_call(
        kernel,
        out_shape=[
            jax.ShapeDtypeStruct(blocks.shape, blocks.dtype),
            jax.ShapeDtypeStruct((number, m, m), jnp.float32),
        ],
        in_specs=[VMEM] * (3 + len(extra)),
        out_specs=[VMEM] * 2,
        scratch_shapes=[pltpu.SMEM(order.shape, jnp.int32), pltpu.SemaphoreType.DMA],
        input_output_aliases={2 + len(extra): 0},
        compiler_params=params(24),
        cost_estimate=cost(2 * (number + len(extra) * 4) * nops * m**3),
        name=f"terms_{group}",
    )(order, turned, *extra, blocks)


def slot_kernel(live_ref, coup_ref, psi_ref, left_ref, right_ref, out_ref):
    out_ref[...] = jnp.zeros_like(out_ref)

    @pl.loop(0, live_ref[0])
    def _(c):
        g = coup_ref[0, c]
        half = jnp.dot(left_ref[g], psi_ref[coup_ref[1, c]], preferred_element_type=jnp.float32)
        out_ref[coup_ref[2, c]] += transposed_dot(half.astype(jnp.bfloat16), right_ref[g])


def by_slot(whole, left_ops, right_ops, couplings, live):
    return pl.pallas_call(
        slot_kernel,
        out_shape=jax.ShapeDtypeStruct(whole.shape, jnp.float32),
        in_specs=[SMEM] * 2 + [VMEM] * 3,
        out_specs=VMEM,
        compiler_params=pltpu.CompilerParams(vmem_limit_bytes=60 * 1024 * 1024),
        name="slots",
    )(live, couplings, whole, left_ops, right_ops)


def shards_small(psi, left_ops, right_ops, couplings, live):
    slots = couplings.shape[1]
    first_core = lax.axis_index("ops") & 1 == 0

    def shared(x):
        return jnp.where(first_core, other_core(x), x)

    came = other_core(psi)
    psi = hold(psi)
    two = jnp.concatenate(
        [jnp.where(first_core, psi, came), jnp.where(first_core, came, psi)], axis=0
    )
    came_two = between_chips(two, 0)
    left = hold(left_ops)
    four, left = lax.optimization_barrier((jnp.concatenate([two, came_two], axis=0), left))
    came_four = between_chips(four, 1)
    order = order_slots(left_ops.shape[0], couplings, live)
    eight, order = lax.optimization_barrier((jnp.concatenate([four, came_four], axis=0), order))
    came_eight = between_chips(eight, 2)
    blocks = early(jnp.concatenate([two, shared(came_two)], axis=0), left, slots)
    blocks = more(shared(came_four), left, blocks, 4)
    turned = turn(right_ops)
    came_eight, turned, blocks = lax.optimization_barrier((came_eight, turned, blocks))
    blocks, leaving = terms(order, turned, blocks, 0, 8, 8, shared(came_eight), left)
    others = other_core(leaving)
    blocks, next_four = terms(order, turned, blocks, 1, 4, 4)
    arrived = between_chips((leaving + others).astype(jnp.bfloat16), 2)
    _, last_four = terms(order, turned, blocks, 2, 0, 4)
    keep = jnp.concatenate([last_four, next_four], axis=0)
    keep = keep + other_core(keep)
    for step in (1, 0):
        half = keep.shape[0] // 2
        both = keep + arrived.astype(jnp.float32)
        keep = both[:half]
        arrived = between_chips(both[half:].astype(jnp.bfloat16), step)
    both = keep + arrived.astype(jnp.float32)
    return jnp.where(first_core, other_core(both[:1]), both[1:])


def shards_large(psi, left_ops, right_ops, couplings, live):
    whole = lax.all_gather(psi, "ops", axis=0, tiled=True)
    total = by_slot(whole, left_ops, right_ops, couplings, live)
    return lax.psum_scatter(total, "ops", scatter_dimension=0, tiled=True)


def solution(mesh):
    ops = mesh.shape["ops"]
    placed = (
        P(("groups", "ops"), None, None),
        P(("groups", "ops"), None, None),
        P(("groups", "ops"), None, None),
        P(None, ("groups", "ops")),
        P(("groups", "ops")),
    )

    def shards(psi, *rest):
        if ops == OPS and psi.shape[0] == 1 and rest[0].shape[0] == 16 and rest[2].shape[1] == 384:
            return shards_small(psi, *rest)
        return shards_large(psi, *rest)

    return jax.shard_map(
        shards,
        mesh=mesh,
        in_specs=placed,
        out_specs=P(("groups", "ops"), None, None),
        check_vma=False,
    )
```

```python
import jax
import jax.numpy as jnp
from jax import lax
from jax.experimental import pallas as pl
from jax.experimental.pallas import tpu as pltpu
from jax.sharding import PartitionSpec as P

VMEM = pl.BlockSpec(memory_space=pltpu.VMEM)
SMEM = pl.BlockSpec(memory_space=pltpu.SMEM)

BLOCKS, CELL_BLOCK, SUM, ENDS, ORDER_SIZE = 0, 384, 640, 896, 1024
COUNT_BITS = 10


def transposed_dot(a, b):
    return lax.dot_general(
        a, b, (((1,), (1,)), ((), ())), preferred_element_type=jnp.float32
    )


def iota(shape, axis):
    return lax.broadcasted_iota(jnp.int32, shape, axis)


def count(mask, axis):
    return jnp.sum(mask.astype(jnp.float32), axis=axis, keepdims=True).astype(jnp.int32)


def picked(mask, values, axis):
    kept = jnp.where(mask, values, 0).astype(jnp.float32)
    return jnp.sum(kept, axis=axis, keepdims=True).astype(jnp.int32)


def as_column(row):
    n = row.shape[1]
    return picked(iota((n, n), 0) == iota((n, n), 1), row, 1)


CHAINS = ((3, 2, 1), (1, 3, 2))
OPS = 16


def partners(step):
    return [(i, i ^ (1 << CHAINS[i & 1][step])) for i in range(OPS)]


def other_core(x):
    return lax.ppermute(x, "ops", [(i, i ^ 1) for i in range(OPS)])


def between_chips(x):
    same_core = [list(range(core, OPS, 2)) for core in range(2)]
    return lax.all_to_all(x, "ops", 0, 0, axis_index_groups=same_core, tiled=True)


def source_place(sector, me):
    near = sector ^ me
    spots = [
        sum(((near >> bit) & 1) << step for step, bit in enumerate(chain)) for chain in CHAINS
    ]
    return (near & 1) * (OPS // 2) + jnp.where(sector & 1 == 0, spots[0], spots[1])


def target_place(sector, me):
    return ((sector ^ me) & 1) * (OPS // 2) + (sector >> 1)


def order_kernel(nops, coup_ref, out_ref):
    slots = coup_ref.shape[1]
    cells = OPS * nops
    me = lax.axis_index("ops").astype(jnp.int32)

    g = coup_ref[0:1, :]
    alive = iota((1, slots), 1) < coup_ref[3:4, :]
    cell = jnp.where(alive, target_place(coup_ref[2:3, :], me) * nops + g, cells)
    block = source_place(coup_ref[1:2, :], me) * nops + g
    cell_col = as_column(cell)
    block_col = as_column(block)
    square = (slots, slots)
    ahead = (cell < cell_col) | ((cell == cell_col) & (iota(square, 1) < iota(square, 0)))
    spot_col = count(ahead, 1)
    out_ref[:, BLOCKS : BLOCKS + slots] = picked(spot_col == iota(square, 1), block_col, 0)

    lane = iota((1, cells), 1)
    first = count(cell_col < lane, 0)
    here = cell_col == lane
    number = count(here, 0)
    only = picked(here, block_col, 0)
    few = (number <= 4).astype(jnp.int32) + (number <= 2).astype(jnp.int32)
    kind = jnp.where(number < 2, 6, few + jnp.where(lane < cells // 2, 3, 0))
    square = (cells, cells)
    kind_col = as_column(kind)
    ahead = (kind_col < kind) | ((kind_col == kind) & (iota(square, 0) < iota(square, 1)))
    spot = count(ahead, 0)
    cell_block = jnp.where(number == 0, cells, jnp.where(number == 1, only, cells + 1 + spot))
    chosen = as_column(spot) == iota(square, 1)
    out_ref[:, CELL_BLOCK : CELL_BLOCK + cells] = cell_block
    firsts = picked(chosen, as_column(first), 0)
    out_ref[:, SUM : SUM + cells] = (firsts << COUNT_BITS) + picked(chosen, as_column(number), 0)
    small = iota((1, 128), 1)
    ends = jnp.zeros((1, 128), jnp.int32)
    for k in range(6):
        ends = jnp.where(small == k, count(kind <= k, 1), ends)
    out_ref[:, ENDS : ENDS + 128] = ends


def params(limit):
    return pltpu.CompilerParams(vmem_limit_bytes=limit * 1024 * 1024)


def cost(flops):
    return pl.CostEstimate(flops=flops, bytes_accessed=1 << 20, transcendentals=0)


def order_slots(nops, couplings, live):
    slots = couplings.shape[1]
    rows = jnp.concatenate([couplings, jnp.broadcast_to(live[None], (1, slots))], axis=0)
    return pl.pallas_call(
        lambda *refs: order_kernel(nops, *refs),
        out_shape=jax.ShapeDtypeStruct((1, ORDER_SIZE), jnp.int32),
        in_specs=[VMEM],
        out_specs=VMEM,
        compiler_params=params(16),
        cost_estimate=cost(20 * slots * slots),
        name="order",
    )(rows)


def hold_kernel(psi_ref, left_ref, psi_out, left_out):
    psi_out[...] = psi_ref[...]
    left_out[...] = left_ref[...]


def hold(psi, left_ops):
    return pl.pallas_call(
        hold_kernel,
        out_shape=[jax.ShapeDtypeStruct(x.shape, x.dtype) for x in (psi, left_ops)],
        in_specs=[VMEM] * 2,
        out_specs=[VMEM] * 2,
        compiler_params=params(4),
        cost_estimate=cost(0),
        name="hold",
    )(psi, left_ops)


def turn_kernel(right_ref, turned_ref):
    nops, m, _ = right_ref.shape
    for g in range(nops):
        turned_ref[g * m : (g + 1) * m] = right_ref[g].T


def turn(right_ops):
    nops, m, _ = right_ops.shape
    return pl.pallas_call(
        turn_kernel,
        out_shape=jax.ShapeDtypeStruct((nops * m, m), jnp.bfloat16),
        in_specs=[VMEM],
        out_specs=VMEM,
        compiler_params=params(4),
        cost_estimate=cost(0),
        name="turn",
    )(right_ops)


def add_up(order, block_ref, cells, begin, ends):
    many, some, two = ends
    m = block_ref.shape[1]

    def cell(k):
        packed = order(SUM + k)
        return packed >> COUNT_BITS, packed & ((1 << COUNT_BITS) - 1)

    @pl.loop(begin, many)
    def _(k):
        first, number = cell(k)

        def add(j, total):
            return total + block_ref[order(BLOCKS + first + j)].astype(jnp.float32)

        total = lax.fori_loop(0, number, add, jnp.zeros((m, m), jnp.float32))
        block_ref[cells + 1 + k] = total.astype(jnp.bfloat16)

    @pl.loop(many, some)
    def _(k):
        first, number = cell(k)
        fourth = jnp.where(number == 4, order(BLOCKS + first + 3), cells)
        total = block_ref[order(BLOCKS + first)].astype(jnp.float32)
        total += block_ref[order(BLOCKS + first + 1)].astype(jnp.float32)
        total += block_ref[order(BLOCKS + first + 2)].astype(jnp.float32)
        total += block_ref[fourth].astype(jnp.float32)
        block_ref[cells + 1 + k] = total.astype(jnp.bfloat16)

    @pl.loop(some, two, step=2)
    def _(k):
        ks = (k, jnp.minimum(k + 1, two - 1))
        firsts = [cell(k)[0] for k in ks]
        totals = [
            block_ref[order(BLOCKS + first)] + block_ref[order(BLOCKS + first + 1)]
            for first in firsts
        ]
        for k, total in zip(ks, totals):
            block_ref[cells + 1 + k] = total


def multiply(order, block_ref, turned_ref, out_ref, offset, nops):
    half, m, _ = out_ref.shape
    for t in range(0, half, 2):
        rows = [
            jnp.concatenate(
                [
                    block_ref[order(CELL_BLOCK + (offset + t + i) * nops + g)]
                    for g in range(nops)
                ],
                axis=1,
            )
            for i in range(2)
        ]
        out = jnp.dot(
            jnp.concatenate(rows, axis=0), turned_ref[...], preferred_element_type=jnp.float32
        )
        out_ref[t : t + 2] = out.reshape(2, m, m)


def fill(psi_ref, left_ref, block_ref, offset):
    nops, m, _ = left_ref.shape
    step = 4
    for s in range(0, psi_ref.shape[0], 2):
        pair = jnp.concatenate([psi_ref[s], psi_ref[s + 1]], axis=1)
        for g in range(0, nops, step):
            rows = left_ref[g : g + step].reshape(step * m, m)
            both = jnp.dot(rows, pair, preferred_element_type=jnp.float32).astype(jnp.bfloat16)
            at = (offset + s) * nops + g
            block_ref[at : at + step] = both[:, :m].reshape(step, m, m)
            block_ref[at + nops : at + nops + step] = both[:, m:].reshape(step, m, m)


def early_kernel(psi_ref, left_ref, block_ref):
    nops, m, _ = left_ref.shape
    fill(psi_ref, left_ref, block_ref, 0)
    block_ref[OPS * nops] = jnp.zeros((m, m), jnp.bfloat16)


def early(psi, left, slots):
    nops, m, _ = left.shape
    cells = OPS * nops
    return pl.pallas_call(
        early_kernel,
        out_shape=jax.ShapeDtypeStruct((cells + 1 + slots // 2, m, m), jnp.bfloat16),
        in_specs=[VMEM] * 2,
        out_specs=VMEM,
        compiler_params=params(24),
        cost_estimate=cost(2 * psi.shape[0] * nops * m**3),
        name="early",
    )(psi, left)


def more(psi, left, blocks, offset):
    nops, m, _ = left.shape

    def kernel(psi_ref, left_ref, _, block_ref):
        fill(psi_ref, left_ref, block_ref, offset)

    return pl.pallas_call(
        kernel,
        out_shape=jax.ShapeDtypeStruct(blocks.shape, blocks.dtype),
        in_specs=[VMEM] * 3,
        out_specs=VMEM,
        input_output_aliases={2: 0},
        compiler_params=params(24),
        cost_estimate=cost(2 * psi.shape[0] * nops * m**3),
        name="more",
    )(psi, left, blocks)


def terms(order, turned, blocks, group, offset, number, psi=None, left=None):
    m = blocks.shape[1]
    nops = turned.shape[0] // m
    cells = OPS * nops
    extra = [] if psi is None else [psi, left]

    def kernel(order_in, turned_ref, *refs):
        block_ref, out_ref, order_ref, sem = refs[-4:]
        copy = pltpu.make_async_copy(order_in, order_ref, sem)
        copy.start()
        if extra:
            fill(refs[0], refs[1], block_ref, OPS - psi.shape[0])
        copy.wait()

        def order(i):
            return order_ref[0, i]

        begin = order(ENDS + 3 * group - 1) if group else 0
        ends = [order(ENDS + 3 * group + k) for k in range(3)]
        add_up(order, block_ref, cells, begin, ends)
        multiply(order, block_ref, turned_ref, out_ref, offset, nops)

    return pl.pallas_call(
        kernel,
        out_shape=[
            jax.ShapeDtypeStruct(blocks.shape, blocks.dtype),
            jax.ShapeDtypeStruct((number, m, m), jnp.float32),
        ],
        in_specs=[VMEM] * (3 + len(extra)),
        out_specs=[VMEM] * 2,
        scratch_shapes=[pltpu.SMEM(order.shape, jnp.int32), pltpu.SemaphoreType.DMA],
        input_output_aliases={2 + len(extra): 0},
        compiler_params=params(24),
        cost_estimate=cost(2 * (number + len(extra) * 4) * nops * m**3),
        name=f"terms_{group}",
    )(order, turned, *extra, blocks)


def slot_kernel(live_ref, coup_ref, psi_ref, left_ref, right_ref, out_ref):
    out_ref[...] = jnp.zeros_like(out_ref)

    @pl.loop(0, live_ref[0])
    def _(c):
        g = coup_ref[0, c]
        half = jnp.dot(left_ref[g], psi_ref[coup_ref[1, c]], preferred_element_type=jnp.float32)
        out_ref[coup_ref[2, c]] += transposed_dot(half.astype(jnp.bfloat16), right_ref[g])


def by_slot(whole, left_ops, right_ops, couplings, live):
    return pl.pallas_call(
        slot_kernel,
        out_shape=jax.ShapeDtypeStruct(whole.shape, jnp.float32),
        in_specs=[SMEM] * 2 + [VMEM] * 3,
        out_specs=VMEM,
        compiler_params=pltpu.CompilerParams(vmem_limit_bytes=60 * 1024 * 1024),
        name="slots",
    )(live, couplings, whole, left_ops, right_ops)


def shards_small(psi, left_ops, right_ops, couplings, live):
    slots = couplings.shape[1]
    came = lax.ppermute(psi, "ops", partners(0))
    psi, left = hold(psi, left_ops)
    two, left = lax.optimization_barrier((jnp.concatenate([psi, came], axis=0), left))
    came = lax.ppermute(two, "ops", partners(1))
    order = order_slots(left_ops.shape[0], couplings, live)
    four, order = lax.optimization_barrier((jnp.concatenate([two, came], axis=0), order))
    came = lax.ppermute(four, "ops", partners(2))
    four, blocks = lax.optimization_barrier((four, early(four, left, slots)))
    far_four = other_core(four)
    turned = turn(right_ops)
    blocks = more(far_four, left, blocks, 8)
    came, turned, blocks = lax.optimization_barrier((came, turned, blocks))
    far_four = other_core(came)
    blocks = more(came, left, blocks, 4)
    blocks, send = terms(order, turned, blocks, 0, 8, 8, far_four, left)
    came = other_core(send)
    _, keep = terms(order, turned, blocks, 1, 0, 8)
    parts = between_chips((keep + came).astype(jnp.bfloat16))
    return jnp.sum(parts.astype(jnp.float32), axis=0, keepdims=True)


def shards_large(psi, left_ops, right_ops, couplings, live):
    whole = lax.all_gather(psi, "ops", axis=0, tiled=True)
    total = by_slot(whole, left_ops, right_ops, couplings, live)
    return lax.psum_scatter(total, "ops", scatter_dimension=0, tiled=True)


def solution(mesh):
    ops = mesh.shape["ops"]
    placed = (
        P(("groups", "ops"), None, None),
        P(("groups", "ops"), None, None),
        P(("groups", "ops"), None, None),
        P(None, ("groups", "ops")),
        P(("groups", "ops")),
    )

    def shards(psi, *rest):
        if ops == OPS and psi.shape[0] == 1 and rest[0].shape[0] == 16 and rest[2].shape[1] == 384:
            return shards_small(psi, *rest)
        return shards_large(psi, *rest)

    return jax.shard_map(
        shards,
        mesh=mesh,
        in_specs=placed,
        out_specs=P(("groups", "ops"), None, None),
        check_vma=False,
    )
```

```python
import jax
import jax.numpy as jnp
from jax import lax
from jax.experimental import pallas as pl
from jax.experimental.pallas import tpu as pltpu
from jax.sharding import PartitionSpec as P

VMEM = pl.BlockSpec(memory_space=pltpu.VMEM)
SMEM = pl.BlockSpec(memory_space=pltpu.SMEM)

BLOCKS, CELL_BLOCK, SUM, ENDS, ORDER_SIZE = 0, 384, 640, 896, 1024
COUNT_BITS = 10


def transposed_dot(a, b):
    return lax.dot_general(
        a, b, (((1,), (1,)), ((), ())), preferred_element_type=jnp.float32
    )


def iota(shape, axis):
    return lax.broadcasted_iota(jnp.int32, shape, axis)


def count(mask, axis):
    return jnp.sum(mask.astype(jnp.float32), axis=axis, keepdims=True).astype(jnp.int32)


def picked(mask, values, axis):
    kept = jnp.where(mask, values, 0).astype(jnp.float32)
    return jnp.sum(kept, axis=axis, keepdims=True).astype(jnp.int32)


def as_column(row):
    n = row.shape[1]
    return picked(iota((n, n), 0) == iota((n, n), 1), row, 1)


CHAINS = ((3, 2, 1), (1, 3, 2))
OPS = 16


def partners(step):
    return [(i, i ^ (1 << CHAINS[i & 1][step])) for i in range(OPS)]


def other_core(x):
    return lax.ppermute(x, "ops", [(i, i ^ 1) for i in range(OPS)])


def between_chips(x):
    same_core = [list(range(core, OPS, 2)) for core in range(2)]
    return lax.all_to_all(x, "ops", 0, 0, axis_index_groups=same_core, tiled=True)


def source_place(sector, me):
    near = sector ^ me
    spots = [
        sum(((near >> bit) & 1) << step for step, bit in enumerate(chain)) for chain in CHAINS
    ]
    return (near & 1) * (OPS // 2) + jnp.where(sector & 1 == 0, spots[0], spots[1])


def target_place(sector, me):
    return ((sector ^ me) & 1) * (OPS // 2) + (sector >> 1)


def order_kernel(nops, coup_ref, out_ref):
    slots = coup_ref.shape[1]
    cells = OPS * nops
    me = lax.axis_index("ops").astype(jnp.int32)

    g = coup_ref[0:1, :]
    alive = iota((1, slots), 1) < coup_ref[3:4, :]
    cell = jnp.where(alive, target_place(coup_ref[2:3, :], me) * nops + g, cells)
    block = source_place(coup_ref[1:2, :], me) * nops + g
    cell_col = as_column(cell)
    block_col = as_column(block)
    square = (slots, slots)
    ahead = (cell < cell_col) | ((cell == cell_col) & (iota(square, 1) < iota(square, 0)))
    spot_col = count(ahead, 1)
    out_ref[:, BLOCKS : BLOCKS + slots] = picked(spot_col == iota(square, 1), block_col, 0)

    lane = iota((1, cells), 1)
    first = count(cell_col < lane, 0)
    here = cell_col == lane
    number = count(here, 0)
    only = picked(here, block_col, 0)
    few = (number <= 4).astype(jnp.int32) + (number <= 2).astype(jnp.int32)
    kind = jnp.where(number < 2, 6, few + jnp.where(lane < cells // 2, 3, 0))
    square = (cells, cells)
    kind_col = as_column(kind)
    ahead = (kind_col < kind) | ((kind_col == kind) & (iota(square, 0) < iota(square, 1)))
    spot = count(ahead, 0)
    cell_block = jnp.where(number == 0, cells, jnp.where(number == 1, only, cells + 1 + spot))
    chosen = as_column(spot) == iota(square, 1)
    out_ref[:, CELL_BLOCK : CELL_BLOCK + cells] = cell_block
    firsts = picked(chosen, as_column(first), 0)
    out_ref[:, SUM : SUM + cells] = (firsts << COUNT_BITS) + picked(chosen, as_column(number), 0)
    small = iota((1, 128), 1)
    ends = jnp.zeros((1, 128), jnp.int32)
    for k in range(6):
        ends = jnp.where(small == k, count(kind <= k, 1), ends)
    out_ref[:, ENDS : ENDS + 128] = ends


def params(limit):
    return pltpu.CompilerParams(vmem_limit_bytes=limit * 1024 * 1024)


def cost(flops):
    return pl.CostEstimate(flops=flops, bytes_accessed=1 << 20, transcendentals=0)


def order_slots(nops, couplings, live):
    slots = couplings.shape[1]
    rows = jnp.concatenate([couplings, jnp.broadcast_to(live[None], (1, slots))], axis=0)
    return pl.pallas_call(
        lambda *refs: order_kernel(nops, *refs),
        out_shape=jax.ShapeDtypeStruct((1, ORDER_SIZE), jnp.int32),
        in_specs=[VMEM],
        out_specs=VMEM,
        compiler_params=params(16),
        cost_estimate=cost(20 * slots * slots),
        name="order",
    )(rows)


def hold_kernel(psi_ref, left_ref, psi_out, left_out):
    psi_out[...] = psi_ref[...]
    left_out[...] = left_ref[...]


def hold(psi, left_ops):
    return pl.pallas_call(
        hold_kernel,
        out_shape=[jax.ShapeDtypeStruct(x.shape, x.dtype) for x in (psi, left_ops)],
        in_specs=[VMEM] * 2,
        out_specs=[VMEM] * 2,
        compiler_params=params(4),
        cost_estimate=cost(0),
        name="hold",
    )(psi, left_ops)


def turn_kernel(right_ref, turned_ref):
    nops, m, _ = right_ref.shape
    for g in range(nops):
        turned_ref[g * m : (g + 1) * m] = right_ref[g].T


def turn(right_ops):
    nops, m, _ = right_ops.shape
    return pl.pallas_call(
        turn_kernel,
        out_shape=jax.ShapeDtypeStruct((nops * m, m), jnp.bfloat16),
        in_specs=[VMEM],
        out_specs=VMEM,
        compiler_params=params(4),
        cost_estimate=cost(0),
        name="turn",
    )(right_ops)


def add_up(order, block_ref, cells, begin, ends):
    many, some, two = ends
    m = block_ref.shape[1]

    def cell(k):
        packed = order(SUM + k)
        return packed >> COUNT_BITS, packed & ((1 << COUNT_BITS) - 1)

    @pl.loop(begin, many)
    def _(k):
        first, number = cell(k)

        def add(j, total):
            return total + block_ref[order(BLOCKS + first + j)].astype(jnp.float32)

        total = lax.fori_loop(0, number, add, jnp.zeros((m, m), jnp.float32))
        block_ref[cells + 1 + k] = total.astype(jnp.bfloat16)

    @pl.loop(many, some)
    def _(k):
        first, number = cell(k)
        fourth = jnp.where(number == 4, order(BLOCKS + first + 3), cells)
        total = block_ref[order(BLOCKS + first)].astype(jnp.float32)
        total += block_ref[order(BLOCKS + first + 1)].astype(jnp.float32)
        total += block_ref[order(BLOCKS + first + 2)].astype(jnp.float32)
        total += block_ref[fourth].astype(jnp.float32)
        block_ref[cells + 1 + k] = total.astype(jnp.bfloat16)

    @pl.loop(some, two, step=2)
    def _(k):
        ks = (k, jnp.minimum(k + 1, two - 1))
        firsts = [cell(k)[0] for k in ks]
        totals = [
            block_ref[order(BLOCKS + first)] + block_ref[order(BLOCKS + first + 1)]
            for first in firsts
        ]
        for k, total in zip(ks, totals):
            block_ref[cells + 1 + k] = total


def multiply(order, block_ref, turned_ref, out_ref, offset, nops):
    half, m, _ = out_ref.shape
    for t in range(0, half, 2):
        rows = [
            jnp.concatenate(
                [
                    block_ref[order(CELL_BLOCK + (offset + t + i) * nops + g)]
                    for g in range(nops)
                ],
                axis=1,
            )
            for i in range(2)
        ]
        out = jnp.dot(
            jnp.concatenate(rows, axis=0), turned_ref[...], preferred_element_type=jnp.float32
        )
        out_ref[t : t + 2] = out.reshape(2, m, m)


def fill(psi_ref, left_ref, block_ref, offset):
    nops, m, _ = left_ref.shape
    step = 4
    for s in range(0, psi_ref.shape[0], 2):
        pair = jnp.concatenate([psi_ref[s], psi_ref[s + 1]], axis=1)
        for g in range(0, nops, step):
            rows = left_ref[g : g + step].reshape(step * m, m)
            both = jnp.dot(rows, pair, preferred_element_type=jnp.float32).astype(jnp.bfloat16)
            at = (offset + s) * nops + g
            block_ref[at : at + step] = both[:, :m].reshape(step, m, m)
            block_ref[at + nops : at + nops + step] = both[:, m:].reshape(step, m, m)


def early_kernel(psi_ref, left_ref, block_ref):
    nops, m, _ = left_ref.shape
    fill(psi_ref, left_ref, block_ref, 0)
    block_ref[OPS * nops] = jnp.zeros((m, m), jnp.bfloat16)


def early(psi, left, slots):
    nops, m, _ = left.shape
    cells = OPS * nops
    return pl.pallas_call(
        early_kernel,
        out_shape=jax.ShapeDtypeStruct((cells + 1 + slots // 2, m, m), jnp.bfloat16),
        in_specs=[VMEM] * 2,
        out_specs=VMEM,
        compiler_params=params(24),
        cost_estimate=cost(2 * psi.shape[0] * nops * m**3),
        name="early",
    )(psi, left)


def more(psi, left, blocks, offset):
    nops, m, _ = left.shape

    def kernel(psi_ref, left_ref, _, block_ref):
        fill(psi_ref, left_ref, block_ref, offset)

    return pl.pallas_call(
        kernel,
        out_shape=jax.ShapeDtypeStruct(blocks.shape, blocks.dtype),
        in_specs=[VMEM] * 3,
        out_specs=VMEM,
        input_output_aliases={2: 0},
        compiler_params=params(24),
        cost_estimate=cost(2 * psi.shape[0] * nops * m**3),
        name="more",
    )(psi, left, blocks)


def terms(order, turned, blocks, group, offset, number, psi=None, left=None):
    m = blocks.shape[1]
    nops = turned.shape[0] // m
    cells = OPS * nops
    extra = [] if psi is None else [psi, left]

    def kernel(order_in, turned_ref, *refs):
        block_ref, out_ref, order_ref, sem = refs[-4:]
        copy = pltpu.make_async_copy(order_in, order_ref, sem)
        copy.start()
        if extra:
            fill(refs[0], refs[1], block_ref, OPS - psi.shape[0])
        copy.wait()

        def order(i):
            return order_ref[0, i]

        begin = order(ENDS + 3 * group - 1) if group else 0
        ends = [order(ENDS + 3 * group + k) for k in range(3)]
        add_up(order, block_ref, cells, begin, ends)
        multiply(order, block_ref, turned_ref, out_ref, offset, nops)

    return pl.pallas_call(
        kernel,
        out_shape=[
            jax.ShapeDtypeStruct(blocks.shape, blocks.dtype),
            jax.ShapeDtypeStruct((number, m, m), jnp.float32),
        ],
        in_specs=[VMEM] * (3 + len(extra)),
        out_specs=[VMEM] * 2,
        scratch_shapes=[pltpu.SMEM(order.shape, jnp.int32), pltpu.SemaphoreType.DMA],
        input_output_aliases={2 + len(extra): 0},
        compiler_params=params(24),
        cost_estimate=cost(2 * (number + len(extra) * 4) * nops * m**3),
        name=f"terms_{group}",
    )(order, turned, *extra, blocks)


def slot_kernel(live_ref, coup_ref, psi_ref, left_ref, right_ref, out_ref):
    out_ref[...] = jnp.zeros_like(out_ref)

    @pl.loop(0, live_ref[0])
    def _(c):
        g = coup_ref[0, c]
        half = jnp.dot(left_ref[g], psi_ref[coup_ref[1, c]], preferred_element_type=jnp.float32)
        out_ref[coup_ref[2, c]] += transposed_dot(half.astype(jnp.bfloat16), right_ref[g])


def by_slot(whole, left_ops, right_ops, couplings, live):
    return pl.pallas_call(
        slot_kernel,
        out_shape=jax.ShapeDtypeStruct(whole.shape, jnp.float32),
        in_specs=[SMEM] * 2 + [VMEM] * 3,
        out_specs=VMEM,
        compiler_params=pltpu.CompilerParams(vmem_limit_bytes=60 * 1024 * 1024),
        name="slots",
    )(live, couplings, whole, left_ops, right_ops)


def shards_small(psi, left_ops, right_ops, couplings, live):
    slots = couplings.shape[1]
    came = lax.ppermute(psi, "ops", partners(0))
    psi, left = hold(psi, left_ops)
    two, left = lax.optimization_barrier((jnp.concatenate([psi, came], axis=0), left))
    came = lax.ppermute(two, "ops", partners(1))
    order = order_slots(left_ops.shape[0], couplings, live)
    four, order = lax.optimization_barrier((jnp.concatenate([two, came], axis=0), order))
    came = lax.ppermute(four, "ops", partners(2))
    blocks = early(four, left, slots)
    turned = turn(right_ops)
    eight, turned, blocks = lax.optimization_barrier(
        (jnp.concatenate([four, came], axis=0), turned, blocks)
    )
    far = other_core(eight)
    blocks = more(came, left, blocks, 4)
    blocks, send = terms(order, turned, blocks, 0, 8, 8, far, left)
    came = other_core(send)
    _, keep = terms(order, turned, blocks, 1, 0, 8)
    parts = between_chips((keep + came).astype(jnp.bfloat16))
    return jnp.sum(parts.astype(jnp.float32), axis=0, keepdims=True)


def shards_large(psi, left_ops, right_ops, couplings, live):
    whole = lax.all_gather(psi, "ops", axis=0, tiled=True)
    total = by_slot(whole, left_ops, right_ops, couplings, live)
    return lax.psum_scatter(total, "ops", scatter_dimension=0, tiled=True)


def solution(mesh):
    ops = mesh.shape["ops"]
    placed = (
        P(("groups", "ops"), None, None),
        P(("groups", "ops"), None, None),
        P(("groups", "ops"), None, None),
        P(None, ("groups", "ops")),
        P(("groups", "ops")),
    )

    def shards(psi, *rest):
        if ops == OPS and psi.shape[0] == 1 and rest[0].shape[0] == 16 and rest[2].shape[1] == 384:
            return shards_small(psi, *rest)
        return shards_large(psi, *rest)

    return jax.shard_map(
        shards,
        mesh=mesh,
        in_specs=placed,
        out_specs=P(("groups", "ops"), None, None),
        check_vma=False,
    )
```

```python
import jax
import jax.numpy as jnp
from jax import lax
from jax.experimental import pallas as pl
from jax.experimental.pallas import tpu as pltpu
from jax.sharding import PartitionSpec as P

VMEM = pl.BlockSpec(memory_space=pltpu.VMEM)
SMEM = pl.BlockSpec(memory_space=pltpu.SMEM)

BLOCKS, CELL_BLOCK, SUM, ENDS, ORDER_SIZE = 0, 384, 640, 896, 1024
COUNT_BITS = 10


def transposed_dot(a, b):
    return lax.dot_general(
        a, b, (((1,), (1,)), ((), ())), preferred_element_type=jnp.float32
    )


def iota(shape, axis):
    return lax.broadcasted_iota(jnp.int32, shape, axis)


def count(mask, axis):
    return jnp.sum(mask.astype(jnp.float32), axis=axis, keepdims=True).astype(jnp.int32)


def picked(mask, values, axis):
    kept = jnp.where(mask, values, 0).astype(jnp.float32)
    return jnp.sum(kept, axis=axis, keepdims=True).astype(jnp.int32)


def as_column(row):
    n = row.shape[1]
    return picked(iota((n, n), 0) == iota((n, n), 1), row, 1)


ALONG_Z = (4, 8, 12)
ALONG_X = 2
OTHER_CORE = 1
OPS = 16


def exchange(x, apart):
    return lax.ppermute(x, "ops", [(i, i ^ apart) for i in range(OPS)])


def place(sector, me):
    near = sector ^ me
    return (near >> 2) | ((near & 2) << 1) | ((near & 1) << 3)


def order_kernel(nops, coup_ref, out_ref):
    slots = coup_ref.shape[1]
    cells = OPS * nops
    me = lax.axis_index("ops").astype(jnp.int32)

    g = coup_ref[0:1, :]
    alive = iota((1, slots), 1) < coup_ref[3:4, :]
    cell = jnp.where(alive, place(coup_ref[2:3, :], me) * nops + g, cells)
    block = place(coup_ref[1:2, :], me) * nops + g
    cell_col = as_column(cell)
    block_col = as_column(block)
    square = (slots, slots)
    ahead = (cell < cell_col) | ((cell == cell_col) & (iota(square, 1) < iota(square, 0)))
    spot_col = count(ahead, 1)
    out_ref[:, BLOCKS : BLOCKS + slots] = picked(spot_col == iota(square, 1), block_col, 0)

    lane = iota((1, cells), 1)
    first = count(cell_col < lane, 0)
    here = cell_col == lane
    number = count(here, 0)
    only = picked(here, block_col, 0)
    few = (number <= 4).astype(jnp.int32) + (number <= 2).astype(jnp.int32)
    group = (lane < cells // 2).astype(jnp.int32) + (lane < cells // 4).astype(jnp.int32)
    kind = jnp.where(number < 2, 9, few + 3 * group)
    square = (cells, cells)
    kind_col = as_column(kind)
    ahead = (kind_col < kind) | ((kind_col == kind) & (iota(square, 0) < iota(square, 1)))
    spot = count(ahead, 0)
    cell_block = jnp.where(number == 0, cells, jnp.where(number == 1, only, cells + 1 + spot))
    chosen = as_column(spot) == iota(square, 1)
    out_ref[:, CELL_BLOCK : CELL_BLOCK + cells] = cell_block
    firsts = picked(chosen, as_column(first), 0)
    out_ref[:, SUM : SUM + cells] = (firsts << COUNT_BITS) + picked(chosen, as_column(number), 0)
    small = iota((1, 128), 1)
    ends = jnp.zeros((1, 128), jnp.int32)
    for k in range(9):
        ends = jnp.where(small == k, count(kind <= k, 1), ends)
    out_ref[:, ENDS : ENDS + 128] = ends


def params(limit):
    return pltpu.CompilerParams(vmem_limit_bytes=limit * 1024 * 1024)


def cost(flops):
    return pl.CostEstimate(flops=flops, bytes_accessed=1 << 20, transcendentals=0)


def order_slots(nops, couplings, live):
    slots = couplings.shape[1]
    rows = jnp.concatenate([couplings, jnp.broadcast_to(live[None], (1, slots))], axis=0)
    return pl.pallas_call(
        lambda *refs: order_kernel(nops, *refs),
        out_shape=jax.ShapeDtypeStruct((1, ORDER_SIZE), jnp.int32),
        in_specs=[VMEM],
        out_specs=VMEM,
        compiler_params=params(16),
        cost_estimate=cost(20 * slots * slots),
        name="order",
    )(rows)


def hold_kernel(psi_ref, left_ref, psi_out, left_out):
    psi_out[...] = psi_ref[...]
    left_out[...] = left_ref[...]


def hold(psi, left_ops):
    return pl.pallas_call(
        hold_kernel,
        out_shape=[jax.ShapeDtypeStruct(x.shape, x.dtype) for x in (psi, left_ops)],
        in_specs=[VMEM] * 2,
        out_specs=[VMEM] * 2,
        compiler_params=params(4),
        cost_estimate=cost(0),
        name="hold",
    )(psi, left_ops)


def turn_kernel(right_ref, turned_ref):
    nops, m, _ = right_ref.shape
    for g in range(nops):
        turned_ref[g * m : (g + 1) * m] = right_ref[g].T


def turn(right_ops):
    nops, m, _ = right_ops.shape
    return pl.pallas_call(
        turn_kernel,
        out_shape=jax.ShapeDtypeStruct((nops * m, m), jnp.bfloat16),
        in_specs=[VMEM],
        out_specs=VMEM,
        compiler_params=params(4),
        cost_estimate=cost(0),
        name="turn",
    )(right_ops)


def add_up(order, block_ref, cells, begin, ends):
    many, some, two = ends
    m = block_ref.shape[1]

    def cell(k):
        packed = order(SUM + k)
        return packed >> COUNT_BITS, packed & ((1 << COUNT_BITS) - 1)

    @pl.loop(begin, many)
    def _(k):
        first, number = cell(k)

        def add(j, total):
            return total + block_ref[order(BLOCKS + first + j)].astype(jnp.float32)

        total = lax.fori_loop(0, number, add, jnp.zeros((m, m), jnp.float32))
        block_ref[cells + 1 + k] = total.astype(jnp.bfloat16)

    @pl.loop(many, some)
    def _(k):
        first, number = cell(k)
        fourth = jnp.where(number == 4, order(BLOCKS + first + 3), cells)
        total = block_ref[order(BLOCKS + first)].astype(jnp.float32)
        total += block_ref[order(BLOCKS + first + 1)].astype(jnp.float32)
        total += block_ref[order(BLOCKS + first + 2)].astype(jnp.float32)
        total += block_ref[fourth].astype(jnp.float32)
        block_ref[cells + 1 + k] = total.astype(jnp.bfloat16)

    @pl.loop(some, two, step=2)
    def _(k):
        ks = (k, jnp.minimum(k + 1, two - 1))
        firsts = [cell(k)[0] for k in ks]
        totals = [
            block_ref[order(BLOCKS + first)] + block_ref[order(BLOCKS + first + 1)]
            for first in firsts
        ]
        for k, total in zip(ks, totals):
            block_ref[cells + 1 + k] = total


def multiply(order, block_ref, turned_ref, out_ref, offset, nops):
    half, m, _ = out_ref.shape
    for t in range(0, half, 2):
        rows = [
            jnp.concatenate(
                [
                    block_ref[order(CELL_BLOCK + (offset + t + i) * nops + g)]
                    for g in range(nops)
                ],
                axis=1,
            )
            for i in range(2)
        ]
        out = jnp.dot(
            jnp.concatenate(rows, axis=0), turned_ref[...], preferred_element_type=jnp.float32
        )
        out_ref[t : t + 2] = out.reshape(2, m, m)


def fill(psi_ref, left_ref, block_ref, offset):
    nops, m, _ = left_ref.shape
    step = 4
    for s in range(0, psi_ref.shape[0], 2):
        pair = jnp.concatenate([psi_ref[s], psi_ref[s + 1]], axis=1)
        for g in range(0, nops, step):
            rows = left_ref[g : g + step].reshape(step * m, m)
            both = jnp.dot(rows, pair, preferred_element_type=jnp.float32).astype(jnp.bfloat16)
            at = (offset + s) * nops + g
            block_ref[at : at + step] = both[:, :m].reshape(step, m, m)
            block_ref[at + nops : at + nops + step] = both[:, m:].reshape(step, m, m)


def early_kernel(psi_ref, left_ref, block_ref):
    nops, m, _ = left_ref.shape
    fill(psi_ref, left_ref, block_ref, 0)
    block_ref[OPS * nops] = jnp.zeros((m, m), jnp.bfloat16)


def early(psi, left, slots):
    nops, m, _ = left.shape
    cells = OPS * nops
    return pl.pallas_call(
        early_kernel,
        out_shape=jax.ShapeDtypeStruct((cells + 1 + slots // 2, m, m), jnp.bfloat16),
        in_specs=[VMEM] * 2,
        out_specs=VMEM,
        compiler_params=params(24),
        cost_estimate=cost(2 * psi.shape[0] * nops * m**3),
        name="early",
    )(psi, left)


def more(psi, left, blocks, offset):
    nops, m, _ = left.shape

    def kernel(psi_ref, left_ref, _, block_ref):
        fill(psi_ref, left_ref, block_ref, offset)

    return pl.pallas_call(
        kernel,
        out_shape=jax.ShapeDtypeStruct(blocks.shape, blocks.dtype),
        in_specs=[VMEM] * 3,
        out_specs=VMEM,
        input_output_aliases={2: 0},
        compiler_params=params(24),
        cost_estimate=cost(2 * psi.shape[0] * nops * m**3),
        name="more",
    )(psi, left, blocks)


def terms(order, turned, blocks, group, offset, number, psi=None, left=None):
    m = blocks.shape[1]
    nops = turned.shape[0] // m
    cells = OPS * nops
    extra = [] if psi is None else [psi, left]

    def kernel(order_in, turned_ref, *refs):
        block_ref, out_ref, order_ref, sem = refs[-4:]
        copy = pltpu.make_async_copy(order_in, order_ref, sem)
        copy.start()
        if extra:
            fill(refs[0], refs[1], block_ref, OPS // 2)
        copy.wait()

        def order(i):
            return order_ref[0, i]

        begin = order(ENDS + 3 * group - 1) if group else 0
        ends = [order(ENDS + 3 * group + k) for k in range(3)]
        add_up(order, block_ref, cells, begin, ends)
        multiply(order, block_ref, turned_ref, out_ref, offset, nops)

    return pl.pallas_call(
        kernel,
        out_shape=[
            jax.ShapeDtypeStruct(blocks.shape, blocks.dtype),
            jax.ShapeDtypeStruct((number, m, m), jnp.float32),
        ],
        in_specs=[VMEM] * (3 + len(extra)),
        out_specs=[VMEM] * 2,
        scratch_shapes=[pltpu.SMEM(order.shape, jnp.int32), pltpu.SemaphoreType.DMA],
        input_output_aliases={2 + len(extra): 0},
        compiler_params=params(24),
        cost_estimate=cost(2 * (number + len(extra) * 4) * nops * m**3),
        name=f"terms_{group}",
    )(order, turned, *extra, blocks)


def slot_kernel(live_ref, coup_ref, psi_ref, left_ref, right_ref, out_ref):
    out_ref[...] = jnp.zeros_like(out_ref)

    @pl.loop(0, live_ref[0])
    def _(c):
        g = coup_ref[0, c]
        half = jnp.dot(left_ref[g], psi_ref[coup_ref[1, c]], preferred_element_type=jnp.float32)
        out_ref[coup_ref[2, c]] += transposed_dot(half.astype(jnp.bfloat16), right_ref[g])


def by_slot(whole, left_ops, right_ops, couplings, live):
    return pl.pallas_call(
        slot_kernel,
        out_shape=jax.ShapeDtypeStruct(whole.shape, jnp.float32),
        in_specs=[SMEM] * 2 + [VMEM] * 3,
        out_specs=VMEM,
        compiler_params=pltpu.CompilerParams(vmem_limit_bytes=60 * 1024 * 1024),
        name="slots",
    )(live, couplings, whole, left_ops, right_ops)


def shards_small(psi, left_ops, right_ops, couplings, live):
    slots = couplings.shape[1]
    came = [exchange(psi, apart) for apart in ALONG_Z]
    psi, left = hold(psi, left_ops)
    order = order_slots(left_ops.shape[0], couplings, live)
    four, left, order = lax.optimization_barrier(
        (jnp.concatenate([psi, *came], axis=0), left, order)
    )
    came = exchange(four, ALONG_X)
    blocks = early(four, left, slots)
    turned = turn(right_ops)
    eight, turned, blocks = lax.optimization_barrier(
        (jnp.concatenate([four, came], axis=0), turned, blocks)
    )
    far = exchange(eight, OTHER_CORE)
    blocks = more(came, left, blocks, 4)
    blocks, send = terms(order, turned, blocks, 0, 8, 8, far, left)
    came = exchange(send, OTHER_CORE)
    blocks, next_four = terms(order, turned, blocks, 1, 4, 4)
    arrived = exchange((next_four + came[4:]).astype(jnp.bfloat16), ALONG_X)
    _, last_four = terms(order, turned, blocks, 2, 0, 4)
    total = last_four + came[:4] + arrived.astype(jnp.float32)
    parts = [
        exchange(total[k + 1].astype(jnp.bfloat16), apart) for k, apart in enumerate(ALONG_Z)
    ]
    return sum((part.astype(jnp.float32) for part in parts), total[0])[None]


def shards_large(psi, left_ops, right_ops, couplings, live):
    whole = lax.all_gather(psi, "ops", axis=0, tiled=True)
    total = by_slot(whole, left_ops, right_ops, couplings, live)
    return lax.psum_scatter(total, "ops", scatter_dimension=0, tiled=True)


def solution(mesh):
    ops = mesh.shape["ops"]
    placed = (
        P(("groups", "ops"), None, None),
        P(("groups", "ops"), None, None),
        P(("groups", "ops"), None, None),
        P(None, ("groups", "ops")),
        P(("groups", "ops")),
    )

    def shards(psi, *rest):
        if ops == OPS and psi.shape[0] == 1 and rest[0].shape[0] == 16 and rest[2].shape[1] == 384:
            return shards_small(psi, *rest)
        return shards_large(psi, *rest)

    return jax.shard_map(
        shards,
        mesh=mesh,
        in_specs=placed,
        out_specs=P(("groups", "ops"), None, None),
        check_vma=False,
    )
```

```python
import jax
import jax.numpy as jnp
from jax import lax
from jax.experimental import pallas as pl
from jax.experimental.pallas import tpu as pltpu
from jax.sharding import PartitionSpec as P

VMEM = pl.BlockSpec(memory_space=pltpu.VMEM)
SMEM = pl.BlockSpec(memory_space=pltpu.SMEM)

BLOCKS, CELL_BLOCK, SUM, ENDS, ORDER_SIZE = 0, 384, 640, 896, 1024
COUNT_BITS = 10


def transposed_dot(a, b):
    return lax.dot_general(
        a, b, (((1,), (1,)), ((), ())), preferred_element_type=jnp.float32
    )


def iota(shape, axis):
    return lax.broadcasted_iota(jnp.int32, shape, axis)


def count(mask, axis):
    return jnp.sum(mask.astype(jnp.float32), axis=axis, keepdims=True).astype(jnp.int32)


def picked(mask, values, axis):
    kept = jnp.where(mask, values, 0).astype(jnp.float32)
    return jnp.sum(kept, axis=axis, keepdims=True).astype(jnp.int32)


def as_column(row):
    n = row.shape[1]
    return picked(iota((n, n), 0) == iota((n, n), 1), row, 1)


ALONG_Z = (4, 8, 12)
ALONG_X = 2
OTHER_CORE = 1
OPS = 16


def exchange(x, apart):
    return lax.ppermute(x, "ops", [(i, i ^ apart) for i in range(OPS)])


def place(near, along_z):
    return (along_z >> 2) | ((near & 2) << 1) | ((near & 1) << 3)


def order_kernel(nops, coup_ref, out_ref):
    slots = coup_ref.shape[1]
    cells = OPS * nops
    me = lax.axis_index("ops").astype(jnp.int32)

    g = coup_ref[0:1, :]
    alive = iota((1, slots), 1) < coup_ref[3:4, :]
    cell = jnp.where(alive, place(coup_ref[2:3, :] ^ me, coup_ref[2:3, :]) * nops + g, cells)
    block = place(coup_ref[1:2, :] ^ me, coup_ref[1:2, :] ^ me) * nops + g
    cell_col = as_column(cell)
    block_col = as_column(block)
    square = (slots, slots)
    ahead = (cell < cell_col) | ((cell == cell_col) & (iota(square, 1) < iota(square, 0)))
    spot_col = count(ahead, 1)
    out_ref[:, BLOCKS : BLOCKS + slots] = picked(spot_col == iota(square, 1), block_col, 0)

    lane = iota((1, cells), 1)
    first = count(cell_col < lane, 0)
    here = cell_col == lane
    number = count(here, 0)
    only = picked(here, block_col, 0)
    few = (number <= 4).astype(jnp.int32) + (number <= 2).astype(jnp.int32)
    group = (lane < cells // 2).astype(jnp.int32) + (lane < cells // 4).astype(jnp.int32)
    kind = jnp.where(number < 2, 9, few + 3 * group)
    square = (cells, cells)
    kind_col = as_column(kind)
    ahead = (kind_col < kind) | ((kind_col == kind) & (iota(square, 0) < iota(square, 1)))
    spot = count(ahead, 0)
    cell_block = jnp.where(number == 0, cells, jnp.where(number == 1, only, cells + 1 + spot))
    chosen = as_column(spot) == iota(square, 1)
    out_ref[:, CELL_BLOCK : CELL_BLOCK + cells] = cell_block
    firsts = picked(chosen, as_column(first), 0)
    out_ref[:, SUM : SUM + cells] = (firsts << COUNT_BITS) + picked(chosen, as_column(number), 0)
    small = iota((1, 128), 1)
    ends = jnp.zeros((1, 128), jnp.int32)
    for k in range(9):
        ends = jnp.where(small == k, count(kind <= k, 1), ends)
    out_ref[:, ENDS : ENDS + 128] = ends


def params(limit):
    return pltpu.CompilerParams(vmem_limit_bytes=limit * 1024 * 1024)


def cost(flops):
    return pl.CostEstimate(flops=flops, bytes_accessed=1 << 20, transcendentals=0)


def order_slots(nops, couplings, live):
    slots = couplings.shape[1]
    rows = jnp.concatenate([couplings, jnp.broadcast_to(live[None], (1, slots))], axis=0)
    return pl.pallas_call(
        lambda *refs: order_kernel(nops, *refs),
        out_shape=jax.ShapeDtypeStruct((1, ORDER_SIZE), jnp.int32),
        in_specs=[VMEM],
        out_specs=VMEM,
        compiler_params=params(16),
        cost_estimate=cost(20 * slots * slots),
        name="order",
    )(rows)


def hold_kernel(psi_ref, left_ref, psi_out, left_out):
    psi_out[...] = psi_ref[...]
    left_out[...] = left_ref[...]


def hold(psi, left_ops):
    return pl.pallas_call(
        hold_kernel,
        out_shape=[jax.ShapeDtypeStruct(x.shape, x.dtype) for x in (psi, left_ops)],
        in_specs=[VMEM] * 2,
        out_specs=[VMEM] * 2,
        compiler_params=params(4),
        cost_estimate=cost(0),
        name="hold",
    )(psi, left_ops)


def turn_kernel(right_ref, turned_ref):
    nops, m, _ = right_ref.shape
    for g in range(nops):
        turned_ref[g * m : (g + 1) * m] = right_ref[g].T


def turn(right_ops):
    nops, m, _ = right_ops.shape
    return pl.pallas_call(
        turn_kernel,
        out_shape=jax.ShapeDtypeStruct((nops * m, m), jnp.bfloat16),
        in_specs=[VMEM],
        out_specs=VMEM,
        compiler_params=params(4),
        cost_estimate=cost(0),
        name="turn",
    )(right_ops)


def add_up(order, block_ref, cells, begin, ends):
    many, some, two = ends
    m = block_ref.shape[1]

    def cell(k):
        packed = order(SUM + k)
        return packed >> COUNT_BITS, packed & ((1 << COUNT_BITS) - 1)

    @pl.loop(begin, many)
    def _(k):
        first, number = cell(k)

        def add(j, total):
            return total + block_ref[order(BLOCKS + first + j)].astype(jnp.float32)

        total = lax.fori_loop(0, number, add, jnp.zeros((m, m), jnp.float32))
        block_ref[cells + 1 + k] = total.astype(jnp.bfloat16)

    @pl.loop(many, some)
    def _(k):
        first, number = cell(k)
        fourth = jnp.where(number == 4, order(BLOCKS + first + 3), cells)
        total = block_ref[order(BLOCKS + first)].astype(jnp.float32)
        total += block_ref[order(BLOCKS + first + 1)].astype(jnp.float32)
        total += block_ref[order(BLOCKS + first + 2)].astype(jnp.float32)
        total += block_ref[fourth].astype(jnp.float32)
        block_ref[cells + 1 + k] = total.astype(jnp.bfloat16)

    @pl.loop(some, two, step=2)
    def _(k):
        ks = (k, jnp.minimum(k + 1, two - 1))
        firsts = [cell(k)[0] for k in ks]
        totals = [
            block_ref[order(BLOCKS + first)] + block_ref[order(BLOCKS + first + 1)]
            for first in firsts
        ]
        for k, total in zip(ks, totals):
            block_ref[cells + 1 + k] = total


def multiply(order, block_ref, turned_ref, out_ref, offset, nops):
    half, m, _ = out_ref.shape
    for t in range(0, half, 2):
        rows = [
            jnp.concatenate(
                [
                    block_ref[order(CELL_BLOCK + (offset + t + i) * nops + g)]
                    for g in range(nops)
                ],
                axis=1,
            )
            for i in range(2)
        ]
        out = jnp.dot(
            jnp.concatenate(rows, axis=0), turned_ref[...], preferred_element_type=jnp.float32
        )
        out_ref[t : t + 2] = out.reshape(2, m, m)


def fill(psi_ref, left_ref, block_ref, offset):
    nops, m, _ = left_ref.shape
    step = 4
    for s in range(0, psi_ref.shape[0], 2):
        pair = jnp.concatenate([psi_ref[s], psi_ref[s + 1]], axis=1)
        for g in range(0, nops, step):
            rows = left_ref[g : g + step].reshape(step * m, m)
            both = jnp.dot(rows, pair, preferred_element_type=jnp.float32).astype(jnp.bfloat16)
            at = (offset + s) * nops + g
            block_ref[at : at + step] = both[:, :m].reshape(step, m, m)
            block_ref[at + nops : at + nops + step] = both[:, m:].reshape(step, m, m)


def early_kernel(psi_ref, left_ref, block_ref):
    nops, m, _ = left_ref.shape
    fill(psi_ref, left_ref, block_ref, 0)
    block_ref[OPS * nops] = jnp.zeros((m, m), jnp.bfloat16)


def early(psi, left, slots):
    nops, m, _ = left.shape
    cells = OPS * nops
    return pl.pallas_call(
        early_kernel,
        out_shape=jax.ShapeDtypeStruct((cells + 1 + slots // 2, m, m), jnp.bfloat16),
        in_specs=[VMEM] * 2,
        out_specs=VMEM,
        compiler_params=params(24),
        cost_estimate=cost(2 * psi.shape[0] * nops * m**3),
        name="early",
    )(psi, left)


def more(psi, left, blocks, offset):
    nops, m, _ = left.shape

    def kernel(psi_ref, left_ref, _, block_ref):
        fill(psi_ref, left_ref, block_ref, offset)

    return pl.pallas_call(
        kernel,
        out_shape=jax.ShapeDtypeStruct(blocks.shape, blocks.dtype),
        in_specs=[VMEM] * 3,
        out_specs=VMEM,
        input_output_aliases={2: 0},
        compiler_params=params(24),
        cost_estimate=cost(2 * psi.shape[0] * nops * m**3),
        name="more",
    )(psi, left, blocks)


def terms(order, turned, blocks, group, offset, number, psi=None, left=None):
    m = blocks.shape[1]
    nops = turned.shape[0] // m
    cells = OPS * nops
    extra = [] if psi is None else [psi, left]

    def kernel(order_in, turned_ref, *refs):
        block_ref, out_ref, order_ref, sem = refs[-4:]
        copy = pltpu.make_async_copy(order_in, order_ref, sem)
        copy.start()
        if extra:
            fill(refs[0], refs[1], block_ref, OPS // 2)
        copy.wait()

        def order(i):
            return order_ref[0, i]

        begin = order(ENDS + 3 * group - 1) if group else 0
        ends = [order(ENDS + 3 * group + k) for k in range(3)]
        add_up(order, block_ref, cells, begin, ends)
        multiply(order, block_ref, turned_ref, out_ref, offset, nops)

    return pl.pallas_call(
        kernel,
        out_shape=[
            jax.ShapeDtypeStruct(blocks.shape, blocks.dtype),
            jax.ShapeDtypeStruct((number, m, m), jnp.float32),
        ],
        in_specs=[VMEM] * (3 + len(extra)),
        out_specs=[VMEM] * 2,
        scratch_shapes=[pltpu.SMEM(order.shape, jnp.int32), pltpu.SemaphoreType.DMA],
        input_output_aliases={2 + len(extra): 0},
        compiler_params=params(24),
        cost_estimate=cost(2 * (number + len(extra) * 4) * nops * m**3),
        name=f"terms_{group}",
    )(order, turned, *extra, blocks)


def slot_kernel(live_ref, coup_ref, psi_ref, left_ref, right_ref, out_ref):
    out_ref[...] = jnp.zeros_like(out_ref)

    @pl.loop(0, live_ref[0])
    def _(c):
        g = coup_ref[0, c]
        half = jnp.dot(left_ref[g], psi_ref[coup_ref[1, c]], preferred_element_type=jnp.float32)
        out_ref[coup_ref[2, c]] += transposed_dot(half.astype(jnp.bfloat16), right_ref[g])


def by_slot(whole, left_ops, right_ops, couplings, live):
    return pl.pallas_call(
        slot_kernel,
        out_shape=jax.ShapeDtypeStruct(whole.shape, jnp.float32),
        in_specs=[SMEM] * 2 + [VMEM] * 3,
        out_specs=VMEM,
        compiler_params=pltpu.CompilerParams(vmem_limit_bytes=60 * 1024 * 1024),
        name="slots",
    )(live, couplings, whole, left_ops, right_ops)


def shards_small(psi, left_ops, right_ops, couplings, live):
    slots = couplings.shape[1]
    came = [exchange(psi, apart) for apart in ALONG_Z]
    psi, left = hold(psi, left_ops)
    four, left = lax.optimization_barrier((jnp.concatenate([psi, *came], axis=0), left))
    came = exchange(four, ALONG_X)
    order = order_slots(left_ops.shape[0], couplings, live)
    blocks = early(four, left, slots)
    turned = turn(right_ops)
    eight, order, turned, blocks = lax.optimization_barrier(
        (jnp.concatenate([four, came], axis=0), order, turned, blocks)
    )
    far = exchange(eight, OTHER_CORE)
    blocks = more(came, left, blocks, 4)
    blocks, send = terms(order, turned, blocks, 0, 8, 8, far, left)
    came = exchange(send, OTHER_CORE)
    blocks, next_four = terms(order, turned, blocks, 1, 4, 4)
    arrived = exchange((next_four + came[4:]).astype(jnp.bfloat16), ALONG_X)
    _, last_four = terms(order, turned, blocks, 2, 0, 4)
    total = last_four + came[:4] + arrived.astype(jnp.float32)
    same_line = [[z * 4 + i for z in range(4)] for i in range(4)]
    parts = lax.all_to_all(
        total.astype(jnp.bfloat16), "ops", 0, 0, axis_index_groups=same_line, tiled=True
    )
    return jnp.sum(parts.astype(jnp.float32), axis=0, keepdims=True)


def shards_large(psi, left_ops, right_ops, couplings, live):
    whole = lax.all_gather(psi, "ops", axis=0, tiled=True)
    total = by_slot(whole, left_ops, right_ops, couplings, live)
    return lax.psum_scatter(total, "ops", scatter_dimension=0, tiled=True)


def solution(mesh):
    ops = mesh.shape["ops"]
    placed = (
        P(("groups", "ops"), None, None),
        P(("groups", "ops"), None, None),
        P(("groups", "ops"), None, None),
        P(None, ("groups", "ops")),
        P(("groups", "ops")),
    )

    def shards(psi, *rest):
        if ops == OPS and psi.shape[0] == 1 and rest[0].shape[0] == 16 and rest[2].shape[1] == 384:
            return shards_small(psi, *rest)
        return shards_large(psi, *rest)

    return jax.shard_map(
        shards,
        mesh=mesh,
        in_specs=placed,
        out_specs=P(("groups", "ops"), None, None),
        check_vma=False,
    )
```

```python
import jax
import jax.numpy as jnp
from jax import lax
from jax.experimental import pallas as pl
from jax.experimental.pallas import tpu as pltpu
from jax.sharding import PartitionSpec as P

VMEM = pl.BlockSpec(memory_space=pltpu.VMEM)
SMEM = pl.BlockSpec(memory_space=pltpu.SMEM)

BLOCKS, CELL_BLOCK, SUM, ENDS, ORDER_SIZE = 0, 384, 640, 896, 1024
COUNT_BITS = 10


def transposed_dot(a, b):
    return lax.dot_general(
        a, b, (((1,), (1,)), ((), ())), preferred_element_type=jnp.float32
    )


def iota(shape, axis):
    return lax.broadcasted_iota(jnp.int32, shape, axis)


def count(mask, axis):
    return jnp.sum(mask.astype(jnp.float32), axis=axis, keepdims=True).astype(jnp.int32)


def picked(mask, values, axis):
    kept = jnp.where(mask, values, 0).astype(jnp.float32)
    return jnp.sum(kept, axis=axis, keepdims=True).astype(jnp.int32)


def as_column(row):
    n = row.shape[1]
    return picked(iota((n, n), 0) == iota((n, n), 1), row, 1)


ALONG_Z = (12, 4, 8)
ALONG_X = 2
OTHER_CORE = 1
OPS = 16


def exchange(x, apart):
    return lax.ppermute(x, "ops", [(i, i ^ apart) for i in range(OPS)])


def place(sector, me):
    near = sector ^ me
    return (near >> 2) | ((near & 2) << 1) | ((near & 1) << 3)


def order_kernel(nops, coup_ref, out_ref):
    slots = coup_ref.shape[1]
    cells = OPS * nops
    me = lax.axis_index("ops").astype(jnp.int32)

    g = coup_ref[0:1, :]
    alive = iota((1, slots), 1) < coup_ref[3:4, :]
    cell = jnp.where(alive, place(coup_ref[2:3, :], me) * nops + g, cells)
    block = place(coup_ref[1:2, :], me) * nops + g
    cell_col = as_column(cell)
    block_col = as_column(block)
    square = (slots, slots)
    ahead = (cell < cell_col) | ((cell == cell_col) & (iota(square, 1) < iota(square, 0)))
    spot_col = count(ahead, 1)
    out_ref[:, BLOCKS : BLOCKS + slots] = picked(spot_col == iota(square, 1), block_col, 0)

    lane = iota((1, cells), 1)
    first = count(cell_col < lane, 0)
    here = cell_col == lane
    number = count(here, 0)
    only = picked(here, block_col, 0)
    few = (number <= 4).astype(jnp.int32) + (number <= 2).astype(jnp.int32)
    group = (lane < cells // 2).astype(jnp.int32) + (lane < cells // 4).astype(jnp.int32)
    kind = jnp.where(number < 2, 9, few + 3 * group)
    square = (cells, cells)
    kind_col = as_column(kind)
    ahead = (kind_col < kind) | ((kind_col == kind) & (iota(square, 0) < iota(square, 1)))
    spot = count(ahead, 0)
    cell_block = jnp.where(number == 0, cells, jnp.where(number == 1, only, cells + 1 + spot))
    chosen = as_column(spot) == iota(square, 1)
    out_ref[:, CELL_BLOCK : CELL_BLOCK + cells] = cell_block
    firsts = picked(chosen, as_column(first), 0)
    out_ref[:, SUM : SUM + cells] = (firsts << COUNT_BITS) + picked(chosen, as_column(number), 0)
    small = iota((1, 128), 1)
    ends = jnp.zeros((1, 128), jnp.int32)
    for k in range(9):
        ends = jnp.where(small == k, count(kind <= k, 1), ends)
    out_ref[:, ENDS : ENDS + 128] = ends


def params(limit):
    return pltpu.CompilerParams(vmem_limit_bytes=limit * 1024 * 1024)


def cost(flops):
    return pl.CostEstimate(flops=flops, bytes_accessed=1 << 20, transcendentals=0)


def order_slots(nops, couplings, live):
    slots = couplings.shape[1]
    rows = jnp.concatenate([couplings, jnp.broadcast_to(live[None], (1, slots))], axis=0)
    return pl.pallas_call(
        lambda *refs: order_kernel(nops, *refs),
        out_shape=jax.ShapeDtypeStruct((1, ORDER_SIZE), jnp.int32),
        in_specs=[VMEM],
        out_specs=VMEM,
        compiler_params=params(16),
        cost_estimate=cost(20 * slots * slots),
        name="order",
    )(rows)


def hold_kernel(psi_ref, left_ref, psi_out, left_out):
    psi_out[...] = psi_ref[...]
    left_out[...] = left_ref[...]


def hold(psi, left_ops):
    return pl.pallas_call(
        hold_kernel,
        out_shape=[jax.ShapeDtypeStruct(x.shape, x.dtype) for x in (psi, left_ops)],
        in_specs=[VMEM] * 2,
        out_specs=[VMEM] * 2,
        compiler_params=params(4),
        cost_estimate=cost(0),
        name="hold",
    )(psi, left_ops)


def turn_kernel(right_ref, turned_ref):
    nops, m, _ = right_ref.shape
    for g in range(nops):
        turned_ref[g * m : (g + 1) * m] = right_ref[g].T


def turn(right_ops):
    nops, m, _ = right_ops.shape
    return pl.pallas_call(
        turn_kernel,
        out_shape=jax.ShapeDtypeStruct((nops * m, m), jnp.bfloat16),
        in_specs=[VMEM],
        out_specs=VMEM,
        compiler_params=params(4),
        cost_estimate=cost(0),
        name="turn",
    )(right_ops)


def add_up(order, block_ref, cells, begin, ends):
    many, some, two = ends
    m = block_ref.shape[1]

    def cell(k):
        packed = order(SUM + k)
        return packed >> COUNT_BITS, packed & ((1 << COUNT_BITS) - 1)

    @pl.loop(begin, many)
    def _(k):
        first, number = cell(k)

        def add(i, total):
            at = first + i * 4
            for j in range(4):
                block = jnp.where(i * 4 + j < number, order(BLOCKS + at + j), cells)
                total = total + block_ref[block].astype(jnp.float32)
            return total

        chunks = (number + 3) >> 2
        total = lax.fori_loop(0, chunks, add, jnp.zeros((m, m), jnp.float32))
        block_ref[cells + 1 + k] = total.astype(jnp.bfloat16)

    @pl.loop(many, some, step=2)
    def _(k):
        ks = (k, jnp.minimum(k + 1, some - 1))
        totals = []
        for k in ks:
            first, number = cell(k)
            fourth = jnp.where(number == 4, order(BLOCKS + first + 3), cells)
            total = block_ref[order(BLOCKS + first)].astype(jnp.float32)
            total += block_ref[order(BLOCKS + first + 1)].astype(jnp.float32)
            total += block_ref[order(BLOCKS + first + 2)].astype(jnp.float32)
            total += block_ref[fourth].astype(jnp.float32)
            totals.append(total.astype(jnp.bfloat16))
        for k, total in zip(ks, totals):
            block_ref[cells + 1 + k] = total

    @pl.loop(some, two, step=4)
    def _(k):
        ks = [jnp.minimum(k + i, two - 1) for i in range(4)]
        firsts = [cell(k)[0] for k in ks]
        totals = [
            block_ref[order(BLOCKS + first)] + block_ref[order(BLOCKS + first + 1)]
            for first in firsts
        ]
        for k, total in zip(ks, totals):
            block_ref[cells + 1 + k] = total


def multiply(order, block_ref, turned_ref, out_ref, offset, nops):
    half, m, _ = out_ref.shape
    for t in range(0, half, 2):
        rows = [
            jnp.concatenate(
                [
                    block_ref[order(CELL_BLOCK + (offset + t + i) * nops + g)]
                    for g in range(nops)
                ],
                axis=1,
            )
            for i in range(2)
        ]
        out = jnp.dot(
            jnp.concatenate(rows, axis=0), turned_ref[...], preferred_element_type=jnp.float32
        )
        out_ref[t : t + 2] = out.reshape(2, m, m)


def fill(psi_ref, left_ref, block_ref, offset):
    nops, m, _ = left_ref.shape
    step = 4
    for s in range(0, psi_ref.shape[0], 2):
        pair = jnp.concatenate([psi_ref[s], psi_ref[s + 1]], axis=1)
        for g in range(0, nops, step):
            rows = left_ref[g : g + step].reshape(step * m, m)
            both = jnp.dot(rows, pair, preferred_element_type=jnp.float32).astype(jnp.bfloat16)
            at = (offset + s) * nops + g
            block_ref[at : at + step] = both[:, :m].reshape(step, m, m)
            block_ref[at + nops : at + nops + step] = both[:, m:].reshape(step, m, m)


def early_kernel(psi_ref, left_ref, block_ref):
    nops, m, _ = left_ref.shape
    fill(psi_ref, left_ref, block_ref, 0)
    block_ref[OPS * nops] = jnp.zeros((m, m), jnp.bfloat16)


def early(psi, left, slots):
    nops, m, _ = left.shape
    cells = OPS * nops
    return pl.pallas_call(
        early_kernel,
        out_shape=jax.ShapeDtypeStruct((cells + 1 + slots // 2, m, m), jnp.bfloat16),
        in_specs=[VMEM] * 2,
        out_specs=VMEM,
        compiler_params=params(24),
        cost_estimate=cost(2 * psi.shape[0] * nops * m**3),
        name="early",
    )(psi, left)


def more(psi, left, blocks, offset):
    nops, m, _ = left.shape

    def kernel(psi_ref, left_ref, _, block_ref):
        fill(psi_ref, left_ref, block_ref, offset)

    return pl.pallas_call(
        kernel,
        out_shape=jax.ShapeDtypeStruct(blocks.shape, blocks.dtype),
        in_specs=[VMEM] * 3,
        out_specs=VMEM,
        input_output_aliases={2: 0},
        compiler_params=params(24),
        cost_estimate=cost(2 * psi.shape[0] * nops * m**3),
        name="more",
    )(psi, left, blocks)


def terms(order, turned, blocks, group, offset, number, psi=None, left=None):
    m = blocks.shape[1]
    nops = turned.shape[0] // m
    cells = OPS * nops
    extra = [] if psi is None else [psi, left]

    def kernel(order_in, turned_ref, *refs):
        block_ref, out_ref, order_ref, sem = refs[-4:]
        copy = pltpu.make_async_copy(order_in, order_ref, sem)
        copy.start()
        if extra:
            fill(refs[0], refs[1], block_ref, OPS // 2)
        copy.wait()

        def order(i):
            return order_ref[0, i]

        begin = order(ENDS + 3 * group - 1) if group else 0
        ends = [order(ENDS + 3 * group + k) for k in range(3)]
        add_up(order, block_ref, cells, begin, ends)
        multiply(order, block_ref, turned_ref, out_ref, offset, nops)

    return pl.pallas_call(
        kernel,
        out_shape=[
            jax.ShapeDtypeStruct(blocks.shape, blocks.dtype),
            jax.ShapeDtypeStruct((number, m, m), jnp.float32),
        ],
        in_specs=[VMEM] * (3 + len(extra)),
        out_specs=[VMEM] * 2,
        scratch_shapes=[pltpu.SMEM(order.shape, jnp.int32), pltpu.SemaphoreType.DMA],
        input_output_aliases={2 + len(extra): 0},
        compiler_params=params(24),
        cost_estimate=cost(2 * (number + len(extra) * 4) * nops * m**3),
        name=f"terms_{group}",
    )(order, turned, *extra, blocks)


def slot_kernel(live_ref, coup_ref, psi_ref, left_ref, right_ref, out_ref):
    out_ref[...] = jnp.zeros_like(out_ref)

    @pl.loop(0, live_ref[0])
    def _(c):
        g = coup_ref[0, c]
        half = jnp.dot(left_ref[g], psi_ref[coup_ref[1, c]], preferred_element_type=jnp.float32)
        out_ref[coup_ref[2, c]] += transposed_dot(half.astype(jnp.bfloat16), right_ref[g])


def by_slot(whole, left_ops, right_ops, couplings, live):
    return pl.pallas_call(
        slot_kernel,
        out_shape=jax.ShapeDtypeStruct(whole.shape, jnp.float32),
        in_specs=[SMEM] * 2 + [VMEM] * 3,
        out_specs=VMEM,
        compiler_params=pltpu.CompilerParams(vmem_limit_bytes=60 * 1024 * 1024),
        name="slots",
    )(live, couplings, whole, left_ops, right_ops)


def shards_small(psi, left_ops, right_ops, couplings, live):
    slots = couplings.shape[1]
    came = {apart: exchange(psi, apart) for apart in ALONG_Z}
    psi, left = hold(psi, left_ops)
    order = order_slots(left_ops.shape[0], couplings, live)
    four, left, order = lax.optimization_barrier(
        (jnp.concatenate([psi, came[4], came[8], came[12]], axis=0), left, order)
    )
    came = exchange(four, ALONG_X)
    blocks = early(four, left, slots)
    turned = turn(right_ops)
    eight, turned, blocks = lax.optimization_barrier(
        (jnp.concatenate([four, came], axis=0), turned, blocks)
    )
    far = exchange(eight, OTHER_CORE)
    blocks = more(came, left, blocks, 4)
    blocks, send = terms(order, turned, blocks, 0, 8, 8, far, left)
    came = exchange(send, OTHER_CORE)
    blocks, next_four = terms(order, turned, blocks, 1, 4, 4)
    arrived = exchange((next_four + came[4:]).astype(jnp.bfloat16), ALONG_X)
    _, last_four = terms(order, turned, blocks, 2, 0, 4)
    total = last_four + came[:4] + arrived.astype(jnp.float32)
    parts = [
        exchange(total[apart // 4].astype(jnp.bfloat16), apart) for apart in ALONG_Z
    ]
    return sum((part.astype(jnp.float32) for part in parts), total[0])[None]


def shards_large(psi, left_ops, right_ops, couplings, live):
    whole = lax.all_gather(psi, "ops", axis=0, tiled=True)
    total = by_slot(whole, left_ops, right_ops, couplings, live)
    return lax.psum_scatter(total, "ops", scatter_dimension=0, tiled=True)


def solution(mesh):
    ops = mesh.shape["ops"]
    placed = (
        P(("groups", "ops"), None, None),
        P(("groups", "ops"), None, None),
        P(("groups", "ops"), None, None),
        P(None, ("groups", "ops")),
        P(("groups", "ops")),
    )

    def shards(psi, *rest):
        if ops == OPS and psi.shape[0] == 1 and rest[0].shape[0] == 16 and rest[2].shape[1] == 384:
            return shards_small(psi, *rest)
        return shards_large(psi, *rest)

    return jax.shard_map(
        shards,
        mesh=mesh,
        in_specs=placed,
        out_specs=P(("groups", "ops"), None, None),
        check_vma=False,
    )
```

```python
import jax
import jax.numpy as jnp
from jax import lax
from jax.experimental import pallas as pl
from jax.experimental.pallas import tpu as pltpu
from jax.sharding import PartitionSpec as P

VMEM = pl.BlockSpec(memory_space=pltpu.VMEM)
SMEM = pl.BlockSpec(memory_space=pltpu.SMEM)

BLOCKS, CELL_BLOCK, SUM, ENDS, ORDER_SIZE = 0, 384, 640, 896, 1024
COUNT_BITS = 10


def transposed_dot(a, b):
    return lax.dot_general(
        a, b, (((1,), (1,)), ((), ())), preferred_element_type=jnp.float32
    )


def iota(shape, axis):
    return lax.broadcasted_iota(jnp.int32, shape, axis)


def count(mask, axis):
    return jnp.sum(mask.astype(jnp.float32), axis=axis, keepdims=True).astype(jnp.int32)


def picked(mask, values, axis):
    kept = jnp.where(mask, values, 0).astype(jnp.float32)
    return jnp.sum(kept, axis=axis, keepdims=True).astype(jnp.int32)


def as_column(row):
    n = row.shape[1]
    return picked(iota((n, n), 0) == iota((n, n), 1), row, 1)


ALONG_Z = (12, 4, 8)
ALONG_X = 2
OTHER_CORE = 1
OPS = 16


def exchange(x, apart):
    return lax.ppermute(x, "ops", [(i, i ^ apart) for i in range(OPS)])


def place(sector, me):
    near = sector ^ me
    along_z = near >> 2
    spot = jnp.where(along_z == 3, 1, jnp.where(along_z == 0, 0, along_z + 1))
    return spot | ((near & 2) << 1) | ((near & 1) << 3)


def order_kernel(nops, coup_ref, out_ref):
    slots = coup_ref.shape[1]
    cells = OPS * nops
    me = lax.axis_index("ops").astype(jnp.int32)

    g = coup_ref[0:1, :]
    alive = iota((1, slots), 1) < coup_ref[3:4, :]
    cell = jnp.where(alive, place(coup_ref[2:3, :], me) * nops + g, cells)
    block = place(coup_ref[1:2, :], me) * nops + g
    cell_col = as_column(cell)
    block_col = as_column(block)
    square = (slots, slots)
    ahead = (cell < cell_col) | ((cell == cell_col) & (iota(square, 1) < iota(square, 0)))
    spot_col = count(ahead, 1)
    out_ref[:, BLOCKS : BLOCKS + slots] = picked(spot_col == iota(square, 1), block_col, 0)

    lane = iota((1, cells), 1)
    first = count(cell_col < lane, 0)
    here = cell_col == lane
    number = count(here, 0)
    only = picked(here, block_col, 0)
    few = (number <= 4).astype(jnp.int32) + (number <= 2).astype(jnp.int32)
    stays = jnp.where(lane & (cells // 4) == 0, 2, 0)
    group = stays + jnp.where(lane < cells // 2, 1, 0)
    kind = jnp.where(number < 2, 12, few + 3 * group)
    square = (cells, cells)
    kind_col = as_column(kind)
    ahead = (kind_col < kind) | ((kind_col == kind) & (iota(square, 0) < iota(square, 1)))
    spot = count(ahead, 0)
    cell_block = jnp.where(number == 0, cells, jnp.where(number == 1, only, cells + 1 + spot))
    chosen = as_column(spot) == iota(square, 1)
    out_ref[:, CELL_BLOCK : CELL_BLOCK + cells] = cell_block
    firsts = picked(chosen, as_column(first), 0)
    out_ref[:, SUM : SUM + cells] = (firsts << COUNT_BITS) + picked(chosen, as_column(number), 0)
    small = iota((1, 128), 1)
    ends = jnp.zeros((1, 128), jnp.int32)
    for k in range(12):
        ends = jnp.where(small == k, count(kind <= k, 1), ends)
    out_ref[:, ENDS : ENDS + 128] = ends


def params(limit):
    return pltpu.CompilerParams(vmem_limit_bytes=limit * 1024 * 1024)


COST = pl.CostEstimate(flops=0, bytes_accessed=1 << 16, transcendentals=0)


def order_slots(nops, couplings, live):
    slots = couplings.shape[1]
    rows = jnp.concatenate([couplings, jnp.broadcast_to(live[None], (1, slots))], axis=0)
    return pl.pallas_call(
        lambda *refs: order_kernel(nops, *refs),
        out_shape=jax.ShapeDtypeStruct((1, ORDER_SIZE), jnp.int32),
        in_specs=[VMEM],
        out_specs=VMEM,
        compiler_params=params(16),
        cost_estimate=COST,
        name="order",
    )(rows)


def hold_kernel(psi_ref, left_ref, psi_out, left_out):
    psi_out[...] = psi_ref[...]
    left_out[...] = left_ref[...]


def hold(psi, left_ops):
    return pl.pallas_call(
        hold_kernel,
        out_shape=[jax.ShapeDtypeStruct(x.shape, x.dtype) for x in (psi, left_ops)],
        in_specs=[VMEM] * 2,
        out_specs=[VMEM] * 2,
        compiler_params=params(4),
        cost_estimate=COST,
        name="hold",
    )(psi, left_ops)


def turn_kernel(right_ref, turned_ref):
    nops, m, _ = right_ref.shape
    for g in range(nops):
        turned_ref[g * m : (g + 1) * m] = right_ref[g].T


def turn(right_ops):
    nops, m, _ = right_ops.shape
    return pl.pallas_call(
        turn_kernel,
        out_shape=jax.ShapeDtypeStruct((nops * m, m), jnp.bfloat16),
        in_specs=[VMEM],
        out_specs=VMEM,
        compiler_params=params(4),
        cost_estimate=COST,
        name="turn",
    )(right_ops)


def add_up(order, block_ref, cells, begin, ends):
    many, some, two = ends
    m = block_ref.shape[1]

    def cell(k):
        packed = order(SUM + k)
        return packed >> COUNT_BITS, packed & ((1 << COUNT_BITS) - 1)

    @pl.loop(begin, many)
    def _(k):
        first, number = cell(k)

        def add(i, total):
            at = first + i * 4
            for j in range(4):
                block = jnp.where(i * 4 + j < number, order(BLOCKS + at + j), cells)
                total = total + block_ref[block].astype(jnp.float32)
            return total

        chunks = (number + 3) >> 2
        total = lax.fori_loop(0, chunks, add, jnp.zeros((m, m), jnp.float32))
        block_ref[cells + 1 + k] = total.astype(jnp.bfloat16)

    @pl.loop(many, some, step=2)
    def _(k):
        ks = (k, jnp.minimum(k + 1, some - 1))
        totals = []
        for k in ks:
            first, number = cell(k)
            fourth = jnp.where(number == 4, order(BLOCKS + first + 3), cells)
            total = block_ref[order(BLOCKS + first)].astype(jnp.float32)
            total += block_ref[order(BLOCKS + first + 1)].astype(jnp.float32)
            total += block_ref[order(BLOCKS + first + 2)].astype(jnp.float32)
            total += block_ref[fourth].astype(jnp.float32)
            totals.append(total.astype(jnp.bfloat16))
        for k, total in zip(ks, totals):
            block_ref[cells + 1 + k] = total

    @pl.loop(some, two, step=4)
    def _(k):
        ks = [jnp.minimum(k + i, two - 1) for i in range(4)]
        firsts = [cell(k)[0] for k in ks]
        totals = [
            block_ref[order(BLOCKS + first)] + block_ref[order(BLOCKS + first + 1)]
            for first in firsts
        ]
        for k, total in zip(ks, totals):
            block_ref[cells + 1 + k] = total


def multiply(order, block_ref, turned_ref, out_ref, offset, nops):
    half, m, _ = out_ref.shape
    for t in range(0, half, 2):
        rows = [
            jnp.concatenate(
                [
                    block_ref[order(CELL_BLOCK + (offset + t + i) * nops + g)]
                    for g in range(nops)
                ],
                axis=1,
            )
            for i in range(2)
        ]
        out = jnp.dot(
            jnp.concatenate(rows, axis=0), turned_ref[...], preferred_element_type=jnp.float32
        )
        out_ref[t : t + 2] = out.reshape(2, m, m)


def fill(psi_ref, left_ref, block_ref, offset):
    nops, m, _ = left_ref.shape
    step = 4
    for s in range(0, psi_ref.shape[0], 2):
        pair = jnp.concatenate([psi_ref[s], psi_ref[s + 1]], axis=1)
        for g in range(0, nops, step):
            rows = left_ref[g : g + step].reshape(step * m, m)
            both = jnp.dot(rows, pair, preferred_element_type=jnp.float32).astype(jnp.bfloat16)
            at = (offset + s) * nops + g
            block_ref[at : at + step] = both[:, :m].reshape(step, m, m)
            block_ref[at + nops : at + nops + step] = both[:, m:].reshape(step, m, m)


def early_kernel(psi_ref, left_ref, block_ref):
    nops, m, _ = left_ref.shape
    fill(psi_ref, left_ref, block_ref, 0)
    block_ref[OPS * nops] = jnp.zeros((m, m), jnp.bfloat16)


def early(psi, left, slots):
    nops, m, _ = left.shape
    cells = OPS * nops
    return pl.pallas_call(
        early_kernel,
        out_shape=jax.ShapeDtypeStruct((cells + 1 + slots // 2, m, m), jnp.bfloat16),
        in_specs=[VMEM] * 2,
        out_specs=VMEM,
        compiler_params=params(24),
        cost_estimate=COST,
        name="early",
    )(psi, left)


def more(psi, left, blocks, offset):
    nops, m, _ = left.shape

    def kernel(psi_ref, left_ref, _, block_ref):
        fill(psi_ref, left_ref, block_ref, offset)

    return pl.pallas_call(
        kernel,
        out_shape=jax.ShapeDtypeStruct(blocks.shape, blocks.dtype),
        in_specs=[VMEM] * 3,
        out_specs=VMEM,
        input_output_aliases={2: 0},
        compiler_params=params(24),
        cost_estimate=COST,
        name="more",
    )(psi, left, blocks)


def terms(order, turned, blocks, group, offset, psi=None, left=None):
    number = 4
    m = blocks.shape[1]
    nops = turned.shape[0] // m
    cells = OPS * nops
    extra = [] if psi is None else [psi, left]

    def kernel(order_in, turned_ref, *refs):
        block_ref, out_ref, order_ref, sem = refs[-4:]
        copy = pltpu.make_async_copy(order_in, order_ref, sem)
        copy.start()
        if extra:
            fill(refs[0], refs[1], block_ref, OPS - psi.shape[0])
        copy.wait()

        def order(i):
            return order_ref[0, i]

        begin = order(ENDS + 3 * group - 1) if group else 0
        ends = [order(ENDS + 3 * group + k) for k in range(3)]
        add_up(order, block_ref, cells, begin, ends)
        multiply(order, block_ref, turned_ref, out_ref, offset, nops)

    return pl.pallas_call(
        kernel,
        out_shape=[
            jax.ShapeDtypeStruct(blocks.shape, blocks.dtype),
            jax.ShapeDtypeStruct((number, m, m), jnp.float32),
        ],
        in_specs=[VMEM] * (3 + len(extra)),
        out_specs=[VMEM] * 2,
        scratch_shapes=[pltpu.SMEM(order.shape, jnp.int32), pltpu.SemaphoreType.DMA],
        input_output_aliases={2 + len(extra): 0},
        compiler_params=params(24),
        cost_estimate=COST,
        name=f"terms_{group}",
    )(order, turned, *extra, blocks)


def slot_kernel(live_ref, coup_ref, psi_ref, left_ref, right_ref, out_ref):
    out_ref[...] = jnp.zeros_like(out_ref)

    @pl.loop(0, live_ref[0])
    def _(c):
        g = coup_ref[0, c]
        half = jnp.dot(left_ref[g], psi_ref[coup_ref[1, c]], preferred_element_type=jnp.float32)
        out_ref[coup_ref[2, c]] += transposed_dot(half.astype(jnp.bfloat16), right_ref[g])


def by_slot(whole, left_ops, right_ops, couplings, live):
    return pl.pallas_call(
        slot_kernel,
        out_shape=jax.ShapeDtypeStruct(whole.shape, jnp.float32),
        in_specs=[SMEM] * 2 + [VMEM] * 3,
        out_specs=VMEM,
        compiler_params=pltpu.CompilerParams(vmem_limit_bytes=60 * 1024 * 1024),
        name="slots",
    )(live, couplings, whole, left_ops, right_ops)


def shards_small(psi, left_ops, right_ops, couplings, live):
    slots = couplings.shape[1]
    came = {apart: exchange(psi, apart) for apart in ALONG_Z}
    psi, left = hold(psi, left_ops)
    order = order_slots(left_ops.shape[0], couplings, live)
    four, left, order = lax.optimization_barrier(
        (jnp.concatenate([psi, *came.values()], axis=0), left, order)
    )
    came = exchange(four, ALONG_X)
    four, blocks = lax.optimization_barrier((four, early(four, left, slots)))
    far_four = exchange(four, OTHER_CORE)
    turned = turn(right_ops)
    came, turned, blocks = lax.optimization_barrier((came, turned, blocks))
    far = exchange(came, OTHER_CORE)
    blocks = more(came, left, blocks, 4)
    blocks, far_four = lax.optimization_barrier((blocks, far_four))
    blocks = more(far_four, left, blocks, 8)
    blocks, send = terms(order, turned, blocks, 0, 12, far, left)
    came = exchange(send, OTHER_CORE)
    blocks, keep = terms(order, turned, blocks, 1, 4)
    leaving, blocks = lax.optimization_barrier(((keep + came).astype(jnp.bfloat16), blocks))
    arrived = exchange(leaving, ALONG_X)
    blocks, send = terms(order, turned, blocks, 2, 8)
    came = exchange(send, OTHER_CORE)
    _, keep = terms(order, turned, blocks, 3, 0)
    keep, came = lax.optimization_barrier((keep + arrived.astype(jnp.float32), came))
    total = keep + came
    parts = [
        exchange(total[k + 1].astype(jnp.bfloat16), apart) for k, apart in enumerate(ALONG_Z)
    ]
    return sum((part.astype(jnp.float32) for part in parts), total[0])[None]


def shards_large(psi, left_ops, right_ops, couplings, live):
    whole = lax.all_gather(psi, "ops", axis=0, tiled=True)
    total = by_slot(whole, left_ops, right_ops, couplings, live)
    return lax.psum_scatter(total, "ops", scatter_dimension=0, tiled=True)


def solution(mesh):
    ops = mesh.shape["ops"]
    placed = (
        P(("groups", "ops"), None, None),
        P(("groups", "ops"), None, None),
        P(("groups", "ops"), None, None),
        P(None, ("groups", "ops")),
        P(("groups", "ops")),
    )

    def shards(psi, *rest):
        if ops == OPS and psi.shape[0] == 1 and rest[0].shape[0] == 16 and rest[2].shape[1] == 384:
            return shards_small(psi, *rest)
        return shards_large(psi, *rest)

    return jax.shard_map(
        shards,
        mesh=mesh,
        in_specs=placed,
        out_specs=P(("groups", "ops"), None, None),
        check_vma=False,
    )
```

```python
import jax
import jax.numpy as jnp
from jax import lax
from jax.experimental import pallas as pl
from jax.experimental.pallas import tpu as pltpu
from jax.sharding import PartitionSpec as P

VMEM = pl.BlockSpec(memory_space=pltpu.VMEM)
SMEM = pl.BlockSpec(memory_space=pltpu.SMEM)

BLOCKS, CELL_BLOCK, SUM, ENDS, ORDER_SIZE = 0, 384, 640, 896, 1024
COUNT_BITS = 10


def transposed_dot(a, b):
    return lax.dot_general(
        a, b, (((1,), (1,)), ((), ())), preferred_element_type=jnp.float32
    )


def iota(shape, axis):
    return lax.broadcasted_iota(jnp.int32, shape, axis)


def count(mask, axis):
    return jnp.sum(mask.astype(jnp.float32), axis=axis, keepdims=True).astype(jnp.int32)


def picked(mask, values, axis):
    kept = jnp.where(mask, values, 0).astype(jnp.float32)
    return jnp.sum(kept, axis=axis, keepdims=True).astype(jnp.int32)


def as_column(row):
    n = row.shape[1]
    return picked(iota((n, n), 0) == iota((n, n), 1), row, 1)


ALONG_Z = (12, 4, 8)
ALONG_X = 2
OTHER_CORE = 1
OPS = 16


def exchange(x, apart):
    return lax.ppermute(x, "ops", [(i, i ^ apart) for i in range(OPS)])


def place(sector, me):
    near = sector ^ me
    along_z = near >> 2
    spot = jnp.where(along_z == 3, 1, jnp.where(along_z == 0, 0, along_z + 1))
    return spot | ((near & 2) << 1) | ((near & 1) << 3)


def order_kernel(nops, coup_ref, out_ref):
    slots = coup_ref.shape[1]
    cells = OPS * nops
    me = lax.axis_index("ops").astype(jnp.int32)

    g = coup_ref[0:1, :]
    alive = iota((1, slots), 1) < coup_ref[3:4, 0:1]
    cell = jnp.where(alive, place(coup_ref[2:3, :], me) * nops + g, cells)
    block = place(coup_ref[1:2, :], me) * nops + g
    cell_col = as_column(cell)
    block_col = as_column(block)
    square = (slots, slots)
    ahead = (cell < cell_col) | ((cell == cell_col) & (iota(square, 1) < iota(square, 0)))
    spot_col = count(ahead, 1)
    out_ref[:, BLOCKS : BLOCKS + slots] = picked(spot_col == iota(square, 1), block_col, 0)

    lane = iota((1, cells), 1)
    first = count(cell_col < lane, 0)
    here = cell_col == lane
    number = count(here, 0)
    only = picked(here, block_col, 0)
    few = (number <= 4).astype(jnp.int32) + (number <= 2).astype(jnp.int32)
    stays = jnp.where(lane & (cells // 4) == 0, 2, 0)
    group = stays + jnp.where(lane < cells // 2, 1, 0)
    kind = jnp.where(number < 2, 12, few + 3 * group)
    square = (cells, cells)
    kind_col = as_column(kind)
    ahead = (kind_col < kind) | ((kind_col == kind) & (iota(square, 0) < iota(square, 1)))
    spot = count(ahead, 0)
    cell_block = jnp.where(number == 0, cells, jnp.where(number == 1, only, cells + 1 + spot))
    chosen = as_column(spot) == iota(square, 1)
    out_ref[:, CELL_BLOCK : CELL_BLOCK + cells] = cell_block
    firsts = picked(chosen, as_column(first), 0)
    out_ref[:, SUM : SUM + cells] = (firsts << COUNT_BITS) + picked(chosen, as_column(number), 0)
    small = iota((1, 128), 1)
    ends = jnp.zeros((1, 128), jnp.int32)
    for k in range(12):
        ends = jnp.where(small == k, count(kind <= k, 1), ends)
    out_ref[:, ENDS : ENDS + 128] = ends


def params(limit):
    return pltpu.CompilerParams(vmem_limit_bytes=limit * 1024 * 1024)


COST = pl.CostEstimate(flops=0, bytes_accessed=1 << 16, transcendentals=0)


def order_slots(nops, couplings, live):
    slots = couplings.shape[1]
    rows = jnp.concatenate([couplings, jnp.pad(live[None], ((0, 0), (0, slots - 1)))], axis=0)
    return pl.pallas_call(
        lambda *refs: order_kernel(nops, *refs),
        out_shape=jax.ShapeDtypeStruct((1, ORDER_SIZE), jnp.int32),
        in_specs=[VMEM],
        out_specs=VMEM,
        compiler_params=params(16),
        cost_estimate=COST,
        name="order",
    )(rows)


def hold_kernel(in_ref, out_ref):
    out_ref[...] = in_ref[...]


def hold(x):
    return pl.pallas_call(
        hold_kernel,
        out_shape=jax.ShapeDtypeStruct(x.shape, x.dtype),
        in_specs=[VMEM],
        out_specs=VMEM,
        compiler_params=params(4),
        cost_estimate=COST,
        name="hold",
    )(x)


def turn_kernel(right_ref, turned_ref):
    nops, m, _ = right_ref.shape
    for g in range(nops):
        turned_ref[g * m : (g + 1) * m] = right_ref[g].T


def turn(right_ops):
    nops, m, _ = right_ops.shape
    return pl.pallas_call(
        turn_kernel,
        out_shape=jax.ShapeDtypeStruct((nops * m, m), jnp.bfloat16),
        in_specs=[VMEM],
        out_specs=VMEM,
        compiler_params=params(4),
        cost_estimate=COST,
        name="turn",
    )(right_ops)


def add_up(order, block_ref, cells, begin, ends):
    many, some, two = ends
    m = block_ref.shape[1]

    def cell(k):
        packed = order(SUM + k)
        return packed >> COUNT_BITS, packed & ((1 << COUNT_BITS) - 1)

    @pl.loop(begin, many)
    def _(k):
        first, number = cell(k)

        def add(i, total):
            at = first + i * 4
            for j in range(4):
                block = jnp.where(i * 4 + j < number, order(BLOCKS + at + j), cells)
                total = total + block_ref[block].astype(jnp.float32)
            return total

        chunks = (number + 3) >> 2
        total = lax.fori_loop(0, chunks, add, jnp.zeros((m, m), jnp.float32))
        block_ref[cells + 1 + k] = total.astype(jnp.bfloat16)

    @pl.loop(many, some, step=2)
    def _(k):
        ks = (k, jnp.minimum(k + 1, some - 1))
        totals = []
        for k in ks:
            first, number = cell(k)
            fourth = jnp.where(number == 4, order(BLOCKS + first + 3), cells)
            total = block_ref[order(BLOCKS + first)].astype(jnp.float32)
            total += block_ref[order(BLOCKS + first + 1)].astype(jnp.float32)
            total += block_ref[order(BLOCKS + first + 2)].astype(jnp.float32)
            total += block_ref[fourth].astype(jnp.float32)
            totals.append(total.astype(jnp.bfloat16))
        for k, total in zip(ks, totals):
            block_ref[cells + 1 + k] = total

    @pl.loop(some, two, step=4)
    def _(k):
        ks = [jnp.minimum(k + i, two - 1) for i in range(4)]
        firsts = [cell(k)[0] for k in ks]
        totals = [
            block_ref[order(BLOCKS + first)] + block_ref[order(BLOCKS + first + 1)]
            for first in firsts
        ]
        for k, total in zip(ks, totals):
            block_ref[cells + 1 + k] = total


def multiply(order, block_ref, turned_ref, out_ref, offset, nops):
    half, m, _ = out_ref.shape
    for t in range(0, half, 2):
        rows = [
            jnp.concatenate(
                [
                    block_ref[order(CELL_BLOCK + (offset + t + i) * nops + g)]
                    for g in range(nops)
                ],
                axis=1,
            )
            for i in range(2)
        ]
        out = jnp.dot(
            jnp.concatenate(rows, axis=0), turned_ref[...], preferred_element_type=jnp.float32
        )
        out_ref[t : t + 2] = out.reshape(2, m, m)


def fill(psi_ref, left_ref, block_ref, offset):
    nops, m, _ = left_ref.shape
    step = 4
    for s in range(0, psi_ref.shape[0], 2):
        pair = jnp.concatenate([psi_ref[s], psi_ref[s + 1]], axis=1)
        for g in range(0, nops, step):
            rows = left_ref[g : g + step].reshape(step * m, m)
            both = jnp.dot(rows, pair, preferred_element_type=jnp.float32).astype(jnp.bfloat16)
            at = (offset + s) * nops + g
            block_ref[at : at + step] = both[:, :m].reshape(step, m, m)
            block_ref[at + nops : at + nops + step] = both[:, m:].reshape(step, m, m)


def early_kernel(psi_ref, left_ref, block_ref):
    nops, m, _ = left_ref.shape
    fill(psi_ref, left_ref, block_ref, 0)
    block_ref[OPS * nops] = jnp.zeros((m, m), jnp.bfloat16)


def early(psi, left, slots):
    nops, m, _ = left.shape
    cells = OPS * nops
    return pl.pallas_call(
        early_kernel,
        out_shape=jax.ShapeDtypeStruct((cells + 1 + slots // 2, m, m), jnp.bfloat16),
        in_specs=[VMEM] * 2,
        out_specs=VMEM,
        compiler_params=params(24),
        cost_estimate=COST,
        name="early",
    )(psi, left)


def more(psi, left, blocks, offset):
    nops, m, _ = left.shape

    def kernel(psi_ref, left_ref, _, block_ref):
        fill(psi_ref, left_ref, block_ref, offset)

    return pl.pallas_call(
        kernel,
        out_shape=jax.ShapeDtypeStruct(blocks.shape, blocks.dtype),
        in_specs=[VMEM] * 3,
        out_specs=VMEM,
        input_output_aliases={2: 0},
        compiler_params=params(24),
        cost_estimate=COST,
        name="more",
    )(psi, left, blocks)


def terms(order, turned, blocks, group, offset, psi=None, left=None):
    number = 4
    m = blocks.shape[1]
    nops = turned.shape[0] // m
    cells = OPS * nops
    extra = [] if psi is None else [psi, left]

    def kernel(order_in, turned_ref, *refs):
        block_ref, out_ref, order_ref, sem = refs[-4:]
        copy = pltpu.make_async_copy(order_in, order_ref, sem)
        copy.start()
        if extra:
            fill(refs[0], refs[1], block_ref, OPS - psi.shape[0])
        copy.wait()

        def order(i):
            return order_ref[0, i]

        begin = order(ENDS + 3 * group - 1) if group else 0
        ends = [order(ENDS + 3 * group + k) for k in range(3)]
        add_up(order, block_ref, cells, begin, ends)
        multiply(order, block_ref, turned_ref, out_ref, offset, nops)

    return pl.pallas_call(
        kernel,
        out_shape=[
            jax.ShapeDtypeStruct(blocks.shape, blocks.dtype),
            jax.ShapeDtypeStruct((number, m, m), jnp.float32),
        ],
        in_specs=[VMEM] * (3 + len(extra)),
        out_specs=[VMEM] * 2,
        scratch_shapes=[pltpu.SMEM(order.shape, jnp.int32), pltpu.SemaphoreType.DMA],
        input_output_aliases={2 + len(extra): 0},
        compiler_params=params(24),
        cost_estimate=COST,
        name=f"terms_{group}",
    )(order, turned, *extra, blocks)


def slot_kernel(live_ref, coup_ref, psi_ref, left_ref, right_ref, out_ref):
    out_ref[...] = jnp.zeros_like(out_ref)

    @pl.loop(0, live_ref[0])
    def _(c):
        g = coup_ref[0, c]
        half = jnp.dot(left_ref[g], psi_ref[coup_ref[1, c]], preferred_element_type=jnp.float32)
        out_ref[coup_ref[2, c]] += transposed_dot(half.astype(jnp.bfloat16), right_ref[g])


def by_slot(whole, left_ops, right_ops, couplings, live):
    return pl.pallas_call(
        slot_kernel,
        out_shape=jax.ShapeDtypeStruct(whole.shape, jnp.float32),
        in_specs=[SMEM] * 2 + [VMEM] * 3,
        out_specs=VMEM,
        compiler_params=pltpu.CompilerParams(vmem_limit_bytes=60 * 1024 * 1024),
        name="slots",
    )(live, couplings, whole, left_ops, right_ops)


def shards_small(psi, left_ops, right_ops, couplings, live):
    slots = couplings.shape[1]
    came = {apart: exchange(psi, apart) for apart in ALONG_Z}
    order = order_slots(left_ops.shape[0], couplings, live)
    four, order = lax.optimization_barrier(
        (jnp.concatenate([hold(psi), *came.values()], axis=0), order)
    )
    came = exchange(four, ALONG_X)
    left = hold(left_ops)
    four, blocks = lax.optimization_barrier((four, early(four, left, slots)))
    far_four = exchange(four, OTHER_CORE)
    turned = turn(right_ops)
    came, turned, blocks = lax.optimization_barrier((came, turned, blocks))
    far = exchange(came, OTHER_CORE)
    blocks = more(came, left, blocks, 4)
    blocks, far_four = lax.optimization_barrier((blocks, far_four))
    blocks = more(far_four, left, blocks, 8)
    blocks, send = terms(order, turned, blocks, 0, 12, far, left)
    came = exchange(send, OTHER_CORE)
    blocks, keep = terms(order, turned, blocks, 1, 4)
    leaving, blocks = lax.optimization_barrier(((keep + came).astype(jnp.bfloat16), blocks))
    arrived = exchange(leaving, ALONG_X)
    blocks, send = terms(order, turned, blocks, 2, 8)
    came = exchange(send, OTHER_CORE)
    _, keep = terms(order, turned, blocks, 3, 0)
    keep, came = lax.optimization_barrier((keep + arrived.astype(jnp.float32), came))
    total = keep + came
    parts = [
        exchange(total[k + 1].astype(jnp.bfloat16), apart) for k, apart in enumerate(ALONG_Z)
    ]
    return sum((part.astype(jnp.float32) for part in parts), total[0])[None]


def shards_large(psi, left_ops, right_ops, couplings, live):
    whole = lax.all_gather(psi, "ops", axis=0, tiled=True)
    total = by_slot(whole, left_ops, right_ops, couplings, live)
    return lax.psum_scatter(total, "ops", scatter_dimension=0, tiled=True)


def solution(mesh):
    ops = mesh.shape["ops"]
    placed = (
        P(("groups", "ops"), None, None),
        P(("groups", "ops"), None, None),
        P(("groups", "ops"), None, None),
        P(None, ("groups", "ops")),
        P(("groups", "ops")),
    )

    def shards(psi, *rest):
        if ops == OPS and psi.shape[0] == 1 and rest[0].shape[0] == 16 and rest[2].shape[1] == 384:
            return shards_small(psi, *rest)
        return shards_large(psi, *rest)

    return jax.shard_map(
        shards,
        mesh=mesh,
        in_specs=placed,
        out_specs=P(("groups", "ops"), None, None),
        check_vma=False,
    )
```

```python
import jax
import jax.numpy as jnp
from jax import lax
from jax.experimental import pallas as pl
from jax.experimental.pallas import tpu as pltpu
from jax.sharding import PartitionSpec as P

VMEM = pl.BlockSpec(memory_space=pltpu.VMEM)
SMEM = pl.BlockSpec(memory_space=pltpu.SMEM)

BLOCKS, CELL_BLOCK, SUM, ENDS, ORDER_SIZE = 0, 384, 640, 896, 1024
COUNT_BITS = 10


def transposed_dot(a, b):
    return lax.dot_general(
        a, b, (((1,), (1,)), ((), ())), preferred_element_type=jnp.float32
    )


def iota(shape, axis):
    return lax.broadcasted_iota(jnp.int32, shape, axis)


def count(mask, axis):
    return jnp.sum(mask.astype(jnp.float32), axis=axis, keepdims=True).astype(jnp.int32)


def picked(mask, values, axis):
    kept = jnp.where(mask, values, 0).astype(jnp.float32)
    return jnp.sum(kept, axis=axis, keepdims=True).astype(jnp.int32)


def as_column(row):
    n = row.shape[1]
    return picked(iota((n, n), 0) == iota((n, n), 1), row, 1)


ALONG_Z = (12, 4, 8)
ALONG_X = 2
OTHER_CORE = 1
OPS = 16


def exchange(x, apart):
    return lax.ppermute(x, "ops", [(i, i ^ apart) for i in range(OPS)])


def place(sector, me):
    near = sector ^ me
    return (near >> 2) | ((near & 2) << 1) | ((near & 1) << 3)


def order_kernel(nops, coup_ref, out_ref):
    slots = coup_ref.shape[1]
    cells = OPS * nops
    me = lax.axis_index("ops").astype(jnp.int32)

    g = coup_ref[0:1, :]
    alive = iota((1, slots), 1) < coup_ref[3:4, 0:1]
    cell = jnp.where(alive, place(coup_ref[2:3, :], me) * nops + g, cells)
    block = place(coup_ref[1:2, :], me) * nops + g
    cell_col = as_column(cell)
    block_col = as_column(block)
    square = (slots, slots)
    ahead = (cell < cell_col) | ((cell == cell_col) & (iota(square, 1) < iota(square, 0)))
    spot_col = count(ahead, 1)
    out_ref[:, BLOCKS : BLOCKS + slots] = picked(spot_col == iota(square, 1), block_col, 0)

    lane = iota((1, cells), 1)
    first = count(cell_col < lane, 0)
    here = cell_col == lane
    number = count(here, 0)
    only = picked(here, block_col, 0)
    few = (number <= 4).astype(jnp.int32) + (number <= 2).astype(jnp.int32)
    stays = jnp.where(lane & (cells // 4) == 0, 2, 0)
    group = stays + jnp.where(lane < cells // 2, 1, 0)
    kind = jnp.where(number < 2, 12, few + 3 * group)
    square = (cells, cells)
    kind_col = as_column(kind)
    ahead = (kind_col < kind) | ((kind_col == kind) & (iota(square, 0) < iota(square, 1)))
    spot = count(ahead, 0)
    cell_block = jnp.where(number == 0, cells, jnp.where(number == 1, only, cells + 1 + spot))
    chosen = as_column(spot) == iota(square, 1)
    out_ref[:, CELL_BLOCK : CELL_BLOCK + cells] = cell_block
    firsts = picked(chosen, as_column(first), 0)
    out_ref[:, SUM : SUM + cells] = (firsts << COUNT_BITS) + picked(chosen, as_column(number), 0)
    small = iota((1, 128), 1)
    ends = jnp.zeros((1, 128), jnp.int32)
    for k in range(12):
        ends = jnp.where(small == k, count(kind <= k, 1), ends)
    out_ref[:, ENDS : ENDS + 128] = ends


def params(limit):
    return pltpu.CompilerParams(vmem_limit_bytes=limit * 1024 * 1024)


COST = pl.CostEstimate(flops=0, bytes_accessed=1 << 16, transcendentals=0)


def order_slots(nops, couplings, live):
    slots = couplings.shape[1]
    rows = jnp.concatenate([couplings, jnp.pad(live[None], ((0, 0), (0, slots - 1)))], axis=0)
    return pl.pallas_call(
        lambda *refs: order_kernel(nops, *refs),
        out_shape=jax.ShapeDtypeStruct((1, ORDER_SIZE), jnp.int32),
        in_specs=[VMEM],
        out_specs=VMEM,
        compiler_params=params(16),
        cost_estimate=COST,
        name="order",
    )(rows)


def hold_kernel(in_ref, out_ref):
    out_ref[...] = in_ref[...]


def hold(x):
    return pl.pallas_call(
        hold_kernel,
        out_shape=jax.ShapeDtypeStruct(x.shape, x.dtype),
        in_specs=[VMEM],
        out_specs=VMEM,
        compiler_params=params(4),
        cost_estimate=COST,
        name="hold",
    )(x)


def turn_kernel(right_ref, turned_ref):
    nops, m, _ = right_ref.shape
    for g in range(nops):
        turned_ref[g * m : (g + 1) * m] = right_ref[g].T


def turn(right_ops):
    nops, m, _ = right_ops.shape
    return pl.pallas_call(
        turn_kernel,
        out_shape=jax.ShapeDtypeStruct((nops * m, m), jnp.bfloat16),
        in_specs=[VMEM],
        out_specs=VMEM,
        compiler_params=params(4),
        cost_estimate=COST,
        name="turn",
    )(right_ops)


def add_up(order, block_ref, cells, begin, ends):
    many, some, two = ends
    m = block_ref.shape[1]

    def cell(k):
        packed = order(SUM + k)
        return packed >> COUNT_BITS, packed & ((1 << COUNT_BITS) - 1)

    @pl.loop(begin, many)
    def _(k):
        first, number = cell(k)

        def add(i, total):
            at = first + i * 4
            for j in range(4):
                block = jnp.where(i * 4 + j < number, order(BLOCKS + at + j), cells)
                total = total + block_ref[block].astype(jnp.float32)
            return total

        chunks = (number + 3) >> 2
        total = lax.fori_loop(0, chunks, add, jnp.zeros((m, m), jnp.float32))
        block_ref[cells + 1 + k] = total.astype(jnp.bfloat16)

    @pl.loop(many, some, step=2)
    def _(k):
        ks = (k, jnp.minimum(k + 1, some - 1))
        totals = []
        for k in ks:
            first, number = cell(k)
            fourth = jnp.where(number == 4, order(BLOCKS + first + 3), cells)
            total = block_ref[order(BLOCKS + first)].astype(jnp.float32)
            total += block_ref[order(BLOCKS + first + 1)].astype(jnp.float32)
            total += block_ref[order(BLOCKS + first + 2)].astype(jnp.float32)
            total += block_ref[fourth].astype(jnp.float32)
            totals.append(total.astype(jnp.bfloat16))
        for k, total in zip(ks, totals):
            block_ref[cells + 1 + k] = total

    @pl.loop(some, two, step=4)
    def _(k):
        ks = [jnp.minimum(k + i, two - 1) for i in range(4)]
        firsts = [cell(k)[0] for k in ks]
        totals = [
            block_ref[order(BLOCKS + first)] + block_ref[order(BLOCKS + first + 1)]
            for first in firsts
        ]
        for k, total in zip(ks, totals):
            block_ref[cells + 1 + k] = total


def multiply(order, block_ref, turned_ref, out_ref, offset, nops):
    half, m, _ = out_ref.shape
    for t in range(0, half, 2):
        rows = [
            jnp.concatenate(
                [
                    block_ref[order(CELL_BLOCK + (offset + t + i) * nops + g)]
                    for g in range(nops)
                ],
                axis=1,
            )
            for i in range(2)
        ]
        out = jnp.dot(
            jnp.concatenate(rows, axis=0), turned_ref[...], preferred_element_type=jnp.float32
        )
        out_ref[t : t + 2] = out.reshape(2, m, m)


def fill(psi_ref, left_ref, block_ref, offset):
    nops, m, _ = left_ref.shape
    step = 4
    for s in range(0, psi_ref.shape[0], 2):
        pair = jnp.concatenate([psi_ref[s], psi_ref[s + 1]], axis=1)
        for g in range(0, nops, step):
            rows = left_ref[g : g + step].reshape(step * m, m)
            both = jnp.dot(rows, pair, preferred_element_type=jnp.float32).astype(jnp.bfloat16)
            at = (offset + s) * nops + g
            block_ref[at : at + step] = both[:, :m].reshape(step, m, m)
            block_ref[at + nops : at + nops + step] = both[:, m:].reshape(step, m, m)


def early_kernel(psi_ref, left_ref, block_ref):
    nops, m, _ = left_ref.shape
    fill(psi_ref, left_ref, block_ref, 0)
    block_ref[OPS * nops] = jnp.zeros((m, m), jnp.bfloat16)


def early(psi, left, slots):
    nops, m, _ = left.shape
    cells = OPS * nops
    return pl.pallas_call(
        early_kernel,
        out_shape=jax.ShapeDtypeStruct((cells + 1 + slots // 2, m, m), jnp.bfloat16),
        in_specs=[VMEM] * 2,
        out_specs=VMEM,
        compiler_params=params(24),
        cost_estimate=COST,
        name="early",
    )(psi, left)


def more(psi, left, blocks, offset):
    nops, m, _ = left.shape

    def kernel(psi_ref, left_ref, _, block_ref):
        fill(psi_ref, left_ref, block_ref, offset)

    return pl.pallas_call(
        kernel,
        out_shape=jax.ShapeDtypeStruct(blocks.shape, blocks.dtype),
        in_specs=[VMEM] * 3,
        out_specs=VMEM,
        input_output_aliases={2: 0},
        compiler_params=params(24),
        cost_estimate=COST,
        name="more",
    )(psi, left, blocks)


def terms(order, turned, blocks, group, offset, psi=None, left=None):
    number = 4
    m = blocks.shape[1]
    nops = turned.shape[0] // m
    cells = OPS * nops
    extra = [] if psi is None else [psi, left]

    def kernel(order_in, turned_ref, *refs):
        block_ref, out_ref, order_ref, sem = refs[-4:]
        copy = pltpu.make_async_copy(order_in, order_ref, sem)
        copy.start()
        if extra:
            fill(refs[0], refs[1], block_ref, OPS - psi.shape[0])
        copy.wait()

        def order(i):
            return order_ref[0, i]

        begin = order(ENDS + 3 * group - 1) if group else 0
        ends = [order(ENDS + 3 * group + k) for k in range(3)]
        add_up(order, block_ref, cells, begin, ends)
        multiply(order, block_ref, turned_ref, out_ref, offset, nops)

    return pl.pallas_call(
        kernel,
        out_shape=[
            jax.ShapeDtypeStruct(blocks.shape, blocks.dtype),
            jax.ShapeDtypeStruct((number, m, m), jnp.float32),
        ],
        in_specs=[VMEM] * (3 + len(extra)),
        out_specs=[VMEM] * 2,
        scratch_shapes=[pltpu.SMEM(order.shape, jnp.int32), pltpu.SemaphoreType.DMA],
        input_output_aliases={2 + len(extra): 0},
        compiler_params=params(24),
        cost_estimate=COST,
        name=f"terms_{group}",
    )(order, turned, *extra, blocks)


def slot_kernel(live_ref, coup_ref, psi_ref, left_ref, right_ref, out_ref):
    out_ref[...] = jnp.zeros_like(out_ref)

    @pl.loop(0, live_ref[0])
    def _(c):
        g = coup_ref[0, c]
        half = jnp.dot(left_ref[g], psi_ref[coup_ref[1, c]], preferred_element_type=jnp.float32)
        out_ref[coup_ref[2, c]] += transposed_dot(half.astype(jnp.bfloat16), right_ref[g])


def by_slot(whole, left_ops, right_ops, couplings, live):
    return pl.pallas_call(
        slot_kernel,
        out_shape=jax.ShapeDtypeStruct(whole.shape, jnp.float32),
        in_specs=[SMEM] * 2 + [VMEM] * 3,
        out_specs=VMEM,
        compiler_params=pltpu.CompilerParams(vmem_limit_bytes=60 * 1024 * 1024),
        name="slots",
    )(live, couplings, whole, left_ops, right_ops)


def shards_small(psi, left_ops, right_ops, couplings, live):
    slots = couplings.shape[1]
    came = {apart: exchange(psi, apart) for apart in ALONG_Z}
    order = order_slots(left_ops.shape[0], couplings, live)
    four, order = lax.optimization_barrier(
        (jnp.concatenate([hold(psi), came[4], came[8], came[12]], axis=0), order)
    )
    came = exchange(four, ALONG_X)
    left = hold(left_ops)
    four, blocks = lax.optimization_barrier((four, early(four, left, slots)))
    far_four = exchange(four, OTHER_CORE)
    turned = turn(right_ops)
    came, turned, blocks = lax.optimization_barrier((came, turned, blocks))
    far = exchange(came, OTHER_CORE)
    blocks = more(came, left, blocks, 4)
    blocks, far_four = lax.optimization_barrier((blocks, far_four))
    blocks = more(far_four, left, blocks, 8)
    blocks, send = terms(order, turned, blocks, 0, 12, far, left)
    came = exchange(send, OTHER_CORE)
    blocks, keep = terms(order, turned, blocks, 1, 4)
    leaving, blocks = lax.optimization_barrier(((keep + came).astype(jnp.bfloat16), blocks))
    arrived = exchange(leaving, ALONG_X)
    blocks, send = terms(order, turned, blocks, 2, 8)
    came = exchange(send, OTHER_CORE)
    _, keep = terms(order, turned, blocks, 3, 0)
    keep, came = lax.optimization_barrier((keep + arrived.astype(jnp.float32), came))
    total = keep + came
    parts = [
        exchange(total[apart // 4].astype(jnp.bfloat16), apart) for apart in ALONG_Z
    ]
    return sum((part.astype(jnp.float32) for part in parts), total[0])[None]


def shards_large(psi, left_ops, right_ops, couplings, live):
    whole = lax.all_gather(psi, "ops", axis=0, tiled=True)
    total = by_slot(whole, left_ops, right_ops, couplings, live)
    return lax.psum_scatter(total, "ops", scatter_dimension=0, tiled=True)


def solution(mesh):
    ops = mesh.shape["ops"]
    placed = (
        P(("groups", "ops"), None, None),
        P(("groups", "ops"), None, None),
        P(("groups", "ops"), None, None),
        P(None, ("groups", "ops")),
        P(("groups", "ops")),
    )

    def shards(psi, *rest):
        if ops == OPS and psi.shape[0] == 1 and rest[0].shape[0] == 16 and rest[2].shape[1] == 384:
            return shards_small(psi, *rest)
        return shards_large(psi, *rest)

    return jax.shard_map(
        shards,
        mesh=mesh,
        in_specs=placed,
        out_specs=P(("groups", "ops"), None, None),
        check_vma=False,
    )
```

```python
import jax
import jax.numpy as jnp
from jax import lax
from jax.experimental import pallas as pl
from jax.experimental.pallas import tpu as pltpu
from jax.sharding import PartitionSpec as P

VMEM = pl.BlockSpec(memory_space=pltpu.VMEM)
SMEM = pl.BlockSpec(memory_space=pltpu.SMEM)

BLOCKS, CELL_BLOCK, SUM, ENDS, ORDER_SIZE = 0, 384, 640, 896, 1024
COUNT_BITS = 10


def transposed_dot(a, b):
    return lax.dot_general(
        a, b, (((1,), (1,)), ((), ())), preferred_element_type=jnp.float32
    )


def iota(shape, axis):
    return lax.broadcasted_iota(jnp.int32, shape, axis)


def count(mask, axis):
    return jnp.sum(mask.astype(jnp.float32), axis=axis, keepdims=True).astype(jnp.int32)


def picked(mask, values, axis):
    kept = jnp.where(mask, values, 0).astype(jnp.float32)
    return jnp.sum(kept, axis=axis, keepdims=True).astype(jnp.int32)


def as_column(row):
    n = row.shape[1]
    return picked(iota((n, n), 0) == iota((n, n), 1), row, 1)


ALONG_Z = (12, 4, 8)
ALONG_X = 2
OTHER_CORE = 1
OPS = 16


def exchange(x, apart):
    return lax.ppermute(x, "ops", [(i, i ^ apart) for i in range(OPS)])


def place(sector, me):
    near = sector ^ me
    along_z = near >> 2
    spot = jnp.where(along_z == 3, 1, jnp.where(along_z == 0, 0, along_z + 1))
    return spot | ((near & 2) << 1) | ((near & 1) << 3)


def order_kernel(nops, coup_ref, out_ref):
    slots = coup_ref.shape[1]
    cells = OPS * nops
    me = lax.axis_index("ops").astype(jnp.int32)

    g = coup_ref[0:1, :]
    alive = iota((1, slots), 1) < coup_ref[3:4, 0:1]
    cell = jnp.where(alive, place(coup_ref[2:3, :], me) * nops + g, cells)
    block = place(coup_ref[1:2, :], me) * nops + g
    cell_col = as_column(cell)
    block_col = as_column(block)
    square = (slots, slots)
    ahead = (cell < cell_col) | ((cell == cell_col) & (iota(square, 1) < iota(square, 0)))
    spot_col = count(ahead, 1)
    out_ref[:, BLOCKS : BLOCKS + slots] = picked(spot_col == iota(square, 1), block_col, 0)

    lane = iota((1, cells), 1)
    first = count(cell_col < lane, 0)
    here = cell_col == lane
    number = count(here, 0)
    only = picked(here, block_col, 0)
    few = (number <= 4).astype(jnp.int32) + (number <= 2).astype(jnp.int32)
    stays = jnp.where(lane & (cells // 4) == 0, 2, 0)
    group = stays + jnp.where(lane < cells // 2, 1, 0)
    kind = jnp.where(number < 2, 12, few + 3 * group)
    square = (cells, cells)
    kind_col = as_column(kind)
    ahead = (kind_col < kind) | ((kind_col == kind) & (iota(square, 0) < iota(square, 1)))
    spot = count(ahead, 0)
    cell_block = jnp.where(number == 0, cells, jnp.where(number == 1, only, cells + 1 + spot))
    chosen = as_column(spot) == iota(square, 1)
    out_ref[:, CELL_BLOCK : CELL_BLOCK + cells] = cell_block
    firsts = picked(chosen, as_column(first), 0)
    out_ref[:, SUM : SUM + cells] = (firsts << COUNT_BITS) + picked(chosen, as_column(number), 0)
    small = iota((1, 128), 1)
    ends = jnp.zeros((1, 128), jnp.int32)
    for k in range(12):
        ends = jnp.where(small == k, count(kind <= k, 1), ends)
    out_ref[:, ENDS : ENDS + 128] = ends


def params(limit):
    return pltpu.CompilerParams(vmem_limit_bytes=limit * 1024 * 1024)


COST = pl.CostEstimate(flops=0, bytes_accessed=1 << 16, transcendentals=0)


def order_slots(nops, couplings, live):
    slots = couplings.shape[1]
    rows = jnp.concatenate([couplings, jnp.pad(live[None], ((0, 0), (0, slots - 1)))], axis=0)
    return pl.pallas_call(
        lambda *refs: order_kernel(nops, *refs),
        out_shape=jax.ShapeDtypeStruct((1, ORDER_SIZE), jnp.int32),
        in_specs=[VMEM],
        out_specs=VMEM,
        compiler_params=params(16),
        cost_estimate=COST,
        name="order",
    )(rows)


def hold_kernel(in_ref, out_ref):
    out_ref[...] = in_ref[...]


def hold(x):
    return pl.pallas_call(
        hold_kernel,
        out_shape=jax.ShapeDtypeStruct(x.shape, x.dtype),
        in_specs=[VMEM],
        out_specs=VMEM,
        compiler_params=params(4),
        cost_estimate=COST,
        name="hold",
    )(x)


def turn_kernel(right_ref, turned_ref):
    nops, m, _ = right_ref.shape
    for g in range(nops):
        turned_ref[g * m : (g + 1) * m] = right_ref[g].T


def turn(right_ops):
    nops, m, _ = right_ops.shape
    return pl.pallas_call(
        turn_kernel,
        out_shape=jax.ShapeDtypeStruct((nops * m, m), jnp.bfloat16),
        in_specs=[VMEM],
        out_specs=VMEM,
        compiler_params=params(4),
        cost_estimate=COST,
        name="turn",
    )(right_ops)


def add_up(order, block_ref, cells, begin, ends):
    many, some, two = ends
    m = block_ref.shape[1]

    def cell(k):
        packed = order(SUM + k)
        return packed >> COUNT_BITS, packed & ((1 << COUNT_BITS) - 1)

    @pl.loop(begin, many)
    def _(k):
        first, number = cell(k)

        def add(i, total):
            at = first + i * 4
            for j in range(4):
                block = jnp.where(i * 4 + j < number, order(BLOCKS + at + j), cells)
                total = total + block_ref[block].astype(jnp.float32)
            return total

        chunks = (number + 3) >> 2
        total = lax.fori_loop(0, chunks, add, jnp.zeros((m, m), jnp.float32))
        block_ref[cells + 1 + k] = total.astype(jnp.bfloat16)

    @pl.loop(many, some, step=2)
    def _(k):
        ks = (k, jnp.minimum(k + 1, some - 1))
        totals = []
        for k in ks:
            first, number = cell(k)
            fourth = jnp.where(number == 4, order(BLOCKS + first + 3), cells)
            total = block_ref[order(BLOCKS + first)].astype(jnp.float32)
            total += block_ref[order(BLOCKS + first + 1)].astype(jnp.float32)
            total += block_ref[order(BLOCKS + first + 2)].astype(jnp.float32)
            total += block_ref[fourth].astype(jnp.float32)
            totals.append(total.astype(jnp.bfloat16))
        for k, total in zip(ks, totals):
            block_ref[cells + 1 + k] = total

    @pl.loop(some, two, step=4)
    def _(k):
        ks = [jnp.minimum(k + i, two - 1) for i in range(4)]
        firsts = [cell(k)[0] for k in ks]
        totals = [
            block_ref[order(BLOCKS + first)] + block_ref[order(BLOCKS + first + 1)]
            for first in firsts
        ]
        for k, total in zip(ks, totals):
            block_ref[cells + 1 + k] = total


def multiply(order, block_ref, turned_ref, out_ref, offset, nops):
    half, m, _ = out_ref.shape
    step = 4
    for t in range(0, half, step):
        rows = [
            jnp.concatenate(
                [
                    block_ref[order(CELL_BLOCK + (offset + t + i) * nops + g)]
                    for g in range(nops)
                ],
                axis=1,
            )
            for i in range(step)
        ]
        out = jnp.dot(
            jnp.concatenate(rows, axis=0), turned_ref[...], preferred_element_type=jnp.float32
        )
        out_ref[t : t + step] = out.reshape(step, m, m)


def fill(psi_ref, left_ref, block_ref, offset):
    nops, m, _ = left_ref.shape
    step = 4
    for s in range(0, psi_ref.shape[0], 2):
        pair = jnp.concatenate([psi_ref[s], psi_ref[s + 1]], axis=1)
        for g in range(0, nops, step):
            rows = left_ref[g : g + step].reshape(step * m, m)
            both = jnp.dot(rows, pair, preferred_element_type=jnp.float32).astype(jnp.bfloat16)
            at = (offset + s) * nops + g
            block_ref[at : at + step] = both[:, :m].reshape(step, m, m)
            block_ref[at + nops : at + nops + step] = both[:, m:].reshape(step, m, m)


def early_kernel(psi_ref, left_ref, block_ref):
    nops, m, _ = left_ref.shape
    fill(psi_ref, left_ref, block_ref, 0)
    block_ref[OPS * nops] = jnp.zeros((m, m), jnp.bfloat16)


def early(psi, left, slots):
    nops, m, _ = left.shape
    cells = OPS * nops
    return pl.pallas_call(
        early_kernel,
        out_shape=jax.ShapeDtypeStruct((cells + 1 + slots // 2, m, m), jnp.bfloat16),
        in_specs=[VMEM] * 2,
        out_specs=VMEM,
        compiler_params=params(24),
        cost_estimate=COST,
        name="early",
    )(psi, left)


def more(psi, left, blocks, offset):
    nops, m, _ = left.shape

    def kernel(psi_ref, left_ref, _, block_ref):
        fill(psi_ref, left_ref, block_ref, offset)

    return pl.pallas_call(
        kernel,
        out_shape=jax.ShapeDtypeStruct(blocks.shape, blocks.dtype),
        in_specs=[VMEM] * 3,
        out_specs=VMEM,
        input_output_aliases={2: 0},
        compiler_params=params(24),
        cost_estimate=COST,
        name="more",
    )(psi, left, blocks)


def terms(order, turned, blocks, group, offset, psi=None, left=None):
    number = 4
    m = blocks.shape[1]
    nops = turned.shape[0] // m
    cells = OPS * nops
    extra = [] if psi is None else [psi, left]

    def kernel(order_in, turned_ref, *refs):
        block_ref, out_ref, order_ref, sem = refs[-4:]
        copy = pltpu.make_async_copy(order_in, order_ref, sem)
        copy.start()
        if extra:
            fill(refs[0], refs[1], block_ref, OPS - psi.shape[0])
        copy.wait()

        def order(i):
            return order_ref[0, i]

        begin = order(ENDS + 3 * group - 1) if group else 0
        ends = [order(ENDS + 3 * group + k) for k in range(3)]
        add_up(order, block_ref, cells, begin, ends)
        multiply(order, block_ref, turned_ref, out_ref, offset, nops)

    return pl.pallas_call(
        kernel,
        out_shape=[
            jax.ShapeDtypeStruct(blocks.shape, blocks.dtype),
            jax.ShapeDtypeStruct((number, m, m), jnp.float32),
        ],
        in_specs=[VMEM] * (3 + len(extra)),
        out_specs=[VMEM] * 2,
        scratch_shapes=[pltpu.SMEM(order.shape, jnp.int32), pltpu.SemaphoreType.DMA],
        input_output_aliases={2 + len(extra): 0},
        compiler_params=params(24),
        cost_estimate=COST,
        name=f"terms_{group}",
    )(order, turned, *extra, blocks)


def slot_kernel(live_ref, coup_ref, psi_ref, left_ref, right_ref, out_ref):
    out_ref[...] = jnp.zeros_like(out_ref)

    @pl.loop(0, live_ref[0])
    def _(c):
        g = coup_ref[0, c]
        half = jnp.dot(left_ref[g], psi_ref[coup_ref[1, c]], preferred_element_type=jnp.float32)
        out_ref[coup_ref[2, c]] += transposed_dot(half.astype(jnp.bfloat16), right_ref[g])


def by_slot(whole, left_ops, right_ops, couplings, live):
    return pl.pallas_call(
        slot_kernel,
        out_shape=jax.ShapeDtypeStruct(whole.shape, jnp.float32),
        in_specs=[SMEM] * 2 + [VMEM] * 3,
        out_specs=VMEM,
        compiler_params=pltpu.CompilerParams(vmem_limit_bytes=60 * 1024 * 1024),
        name="slots",
    )(live, couplings, whole, left_ops, right_ops)


def shards_small(psi, left_ops, right_ops, couplings, live):
    slots = couplings.shape[1]
    came = {apart: exchange(psi, apart) for apart in ALONG_Z}
    order = order_slots(left_ops.shape[0], couplings, live)
    four, order = lax.optimization_barrier(
        (jnp.concatenate([hold(psi), *came.values()], axis=0), order)
    )
    came = exchange(four, ALONG_X)
    left = hold(left_ops)
    four, blocks = lax.optimization_barrier((four, early(four, left, slots)))
    far_four = exchange(four, OTHER_CORE)
    turned = turn(right_ops)
    came, turned, blocks = lax.optimization_barrier((came, turned, blocks))
    far = exchange(came, OTHER_CORE)
    blocks = more(came, left, blocks, 4)
    blocks, far_four = lax.optimization_barrier((blocks, far_four))
    blocks = more(far_four, left, blocks, 8)
    blocks, send = terms(order, turned, blocks, 0, 12, far, left)
    came = exchange(send, OTHER_CORE)
    blocks, keep = terms(order, turned, blocks, 1, 4)
    leaving, blocks = lax.optimization_barrier(((keep + came).astype(jnp.bfloat16), blocks))
    arrived = exchange(leaving, ALONG_X)
    blocks, send = terms(order, turned, blocks, 2, 8)
    came = exchange(send, OTHER_CORE)
    _, keep = terms(order, turned, blocks, 3, 0)
    keep, came = lax.optimization_barrier((keep + arrived.astype(jnp.float32), came))
    total = keep + came
    parts = [
        exchange(total[k + 1].astype(jnp.bfloat16), apart) for k, apart in enumerate(ALONG_Z)
    ]
    return sum((part.astype(jnp.float32) for part in parts), total[0])[None]


def shards_large(psi, left_ops, right_ops, couplings, live):
    whole = lax.all_gather(psi, "ops", axis=0, tiled=True)
    total = by_slot(whole, left_ops, right_ops, couplings, live)
    return lax.psum_scatter(total, "ops", scatter_dimension=0, tiled=True)


def solution(mesh):
    ops = mesh.shape["ops"]
    placed = (
        P(("groups", "ops"), None, None),
        P(("groups", "ops"), None, None),
        P(("groups", "ops"), None, None),
        P(None, ("groups", "ops")),
        P(("groups", "ops")),
    )

    def shards(psi, *rest):
        if ops == OPS and psi.shape[0] == 1 and rest[0].shape[0] == 16 and rest[2].shape[1] == 384:
            return shards_small(psi, *rest)
        return shards_large(psi, *rest)

    return jax.shard_map(
        shards,
        mesh=mesh,
        in_specs=placed,
        out_specs=P(("groups", "ops"), None, None),
        check_vma=False,
    )
```
